32 devices in a mesh: group: 4 (over y, x), shard: 8 (over z, core).
Axes of the slice: x: 2, y: 2, z: 4, core: 2. Of those that a mesh axis runs over, the one named last changes fastest.
Arguments:
- samples: bfloat16 [4096, 1, 4096], P(('group', 'shard')), may hold values from -6 to 6
- fan_taps: float32 [33, 2048], replicated, may hold values from -1 to 1
- pair_blocks: int32 [128, 2], replicated, may hold values from 0 to 31
- pair_valid: int32 [128], P(('group', 'shard')), may hold values 0 or 1
- coil_offsets: int32 [32], replicated, may hold values from 0 to 63
Outputs:
- correlations: float32 [128, 128, 512], P(('group', 'shard'))
The draws below stay inside these ranges and needn't reach their ends.
Inputs may be any that keep to these rules, and one draw needn't show every extreme that they name: `pair_blocks`: block indices.
All inputs are finite; a program needn't handle non-finite values. No bound on the sum of `pair_valid` on one device may be relied on, other than what follows from the above.
Results may differ from the reference program's by a relative error of at most 0.0076.
Values may be sent and summed in bfloat16 or wider, within the bound.
No kernel may reach another device: no remote copies, remote signals or barrier semaphores. Data moves between devices by JAX's collectives and lax.ppermute only.
A program may use at most 192 MiB of HBM per device.

```python
import math
import jax
import jax.numpy as jnp
import numpy as np
from jax import lax

NB = 2048
NT = 4096
BLK = 128
HALF = 16
SMOOTH = 64
NLAG = 512
NSEG = 1
NBLK = 32
NCH = 4096
PAIRS = 128
N_GROUP = 4
N_SHARD = 8


def set_ends(entries, rng, least, largest):
    longest = entries.shape.index(max(entries.shape))
    spots = []
    for shift in (0, 1):
        where = [jax.random.randint(jax.random.fold_in(rng, axis), (), 0, length) for axis, length in enumerate(entries.shape)]
        where[longest] = (where[longest] + shift) % entries.shape[longest]
        spots.append(tuple(where))
    return entries.at[spots[0]].set(least).at[spots[1]].set(largest)


def block_levels(stream_key, dims, shards, smallest, high):
    level, own = 1.0, jax.random.fold_in(stream_key, 6)
    for axis_at, blocks in shards:
        steps = jnp.exp(jax.random.uniform(jax.random.fold_in(own, axis_at), (blocks,), jnp.float32, smallest / len(shards), high / len(shards)))
        level = level * jnp.repeat(steps, dims[axis_at] // blocks).reshape([-1 if axis == axis_at else 1 for axis in range(len(dims))])
    return level


def rank_bounds(count, slope):
    loads = [(1 << 20) // math.isqrt(grade ** slope) + 1 for grade in range(1, count + 1)]
    scale = 1 + sum(loads) // (1 << 30)
    return np.cumsum(np.array([max(1, weight // scale) for weight in loads]))


def ranked_ids(stream_key, extent, number_of, slope):
    listing = rank_bounds(number_of, slope)
    pick = jax.random.randint(jax.random.fold_in(stream_key, 1), extent, 0, int(listing[number_of - 1]))
    standing = jnp.searchsorted(jnp.asarray(listing, jnp.int32), pick, side="right")
    return jax.random.permutation(jax.random.fold_in(stream_key, 2), number_of)[standing].astype(jnp.int32)


def centred(key, dims, deviation, limit, cuts=(), kind=jnp.bfloat16):
    entries = jax.random.normal(key, dims, jnp.float32) * deviation
    if len(cuts) > 0:
        entries = block_levels(key, dims, cuts, -0.22, 0.18) * entries
    return jnp.clip(entries, min=-limit, max=limit).astype(kind)


def setup_inputs(seed: int = 0) -> dict:
    seeds = jax.random.split(jax.random.key(seed), 6)
    return {
        "samples": centred(seeds[0], (NCH, NSEG, NT), 1.0, 6.0, ((0, 32),)),
        "fan_taps": centred(seeds[1], (2 * HALF + 1, NB), (2 * HALF + 1) ** -0.5, 1.0, (), jnp.float32),
        "pair_blocks": set_ends(ranked_ids(seeds[2], (PAIRS, 2), NBLK, 2), jax.random.fold_in(seeds[2], 3), 0, NBLK - 1).astype(jnp.int32),
        "pair_valid": set_ends((jax.random.randint(seeds[3], (PAIRS,), 0, 4) < 3).astype(jnp.int32), jax.random.fold_in(seeds[3], 1), 0, 1),
        "coil_offsets": set_ends(jax.random.randint(seeds[4], (NBLK,), 0, 64), jax.random.fold_in(seeds[4], 1), 0, 63).astype(jnp.int32),
    }


EPSILON = 1e-05

def forward_tables(length, bin_count):
    split = 1 << length.bit_length() // 2
    coarse_n = (jnp.arange(length // split, dtype=jnp.int32) * split)[:, None]
    fine_n = jnp.arange(split, dtype=jnp.int32)[:, None]
    cols_k = jnp.arange(bin_count, dtype=jnp.int32)[None, :]
    coarse_ph = jnp.mod(coarse_n * cols_k, length).astype(jnp.float32) * (2.0 * jnp.pi / length)
    fine_ph = jnp.mod(fine_n * cols_k, length).astype(jnp.float32) * (2.0 * jnp.pi / length)
    cos_a = jnp.cos(coarse_ph)[:, None, :]
    sin_a = jnp.sin(coarse_ph)[:, None, :]
    cos_b = jnp.cos(fine_ph)[None, :, :]
    sin_b = jnp.sin(fine_ph)[None, :, :]
    cosine = (cos_a * cos_b - sin_a * sin_b).reshape(length, bin_count)
    sine_vals = (sin_a * cos_b + cos_a * sin_b).reshape(length, bin_count)
    scaled = 1.0 / jnp.sqrt(jnp.float32(length))
    return (jnp.concatenate([cosine, -sine_vals], axis=1) * scaled).astype(jnp.bfloat16)

def inverse_tables(length, bin_count, lag_count):
    freq_index = jnp.arange(bin_count, dtype=jnp.int32)[:, None]
    lagged = jnp.arange(lag_count, dtype=jnp.int32)[None, :] - lag_count // 2
    phases = jnp.mod(freq_index * lagged, length).astype(jnp.float32) * (2.0 * jnp.pi / length)
    return jnp.stack([jnp.cos(phases), -jnp.sin(phases)]).astype(jnp.bfloat16)

def box_mean(power_sum):
    bin_count = power_sum.shape[1]
    zero_row = jnp.zeros_like(power_sum[:, :1])
    prefix = jnp.concatenate([zero_row, jnp.cumsum(power_sum, axis=1)], axis=1)
    last_row = prefix[:, bin_count:bin_count + 1]
    first_row = prefix[:, 0:1]
    upper_vals = jnp.concatenate([prefix[:, SMOOTH + 1:], jnp.broadcast_to(last_row, (prefix.shape[0], SMOOTH) + prefix.shape[2:])], axis=1)
    lower_vals = jnp.concatenate([jnp.broadcast_to(first_row, (prefix.shape[0], SMOOTH + 1) + prefix.shape[2:]), prefix[:, 1:bin_count - SMOOTH]], axis=1)
    bins_k = jnp.arange(bin_count, dtype=jnp.int32)
    counts = (jnp.minimum(bins_k + SMOOTH, bin_count - 1) - jnp.maximum(bins_k - SMOOTH, 0) + 1).astype(jnp.float32)
    return (upper_vals - lower_vals) / counts[None, :, None]

def whiten(padded, fan_taps):
    width = padded.shape[3] - 2 * HALF
    filtered = jnp.zeros(padded.shape[:3] + (width,), jnp.float32)
    for offset in range(2 * HALF + 1):
        filtered = filtered + fan_taps[offset][None, None, :, None] * padded[:, :, :, offset:offset + width].astype(jnp.float32)
    power_sum = filtered[:, 0] * filtered[:, 0] + filtered[:, 1] * filtered[:, 1]
    mean_power = box_mean(power_sum)
    return (filtered * lax.rsqrt(mean_power + EPSILON)[:, None]).astype(jnp.bfloat16)

def reference(samples, fan_taps, pair_blocks, pair_valid, coil_offsets):
    nblocks = N_GROUP * N_SHARD
    forward = forward_tables(NT, NB).astype(jnp.float32)

    def block_spectra(channel_rows):
        spectra = jnp.einsum('cst,tk->skc', channel_rows.astype(jnp.float32), forward)
        return spectra.astype(jnp.bfloat16).reshape(NSEG, 2, NB, BLK)
    per_block = lax.map(block_spectra, samples.reshape(nblocks, BLK, NSEG, NT))
    whole_line = jnp.moveaxis(per_block, 0, 3).reshape(NSEG, 2, NB, nblocks * BLK)
    padded = jnp.pad(whole_line, ((0, 0), (0, 0), (0, 0), (HALF, HALF)))

    def block_white(index_block):
        window = lax.dynamic_slice_in_dim(padded, index_block * BLK, BLK + 2 * HALF, axis=3)
        return whiten(window, fan_taps)
    whitened = lax.map(block_white, jnp.arange(nblocks, dtype=jnp.int32))
    inverse = inverse_tables(NT, NB, NLAG).astype(jnp.float32)
    bin_index = jnp.arange(NB, dtype=jnp.int32)

    def one_pair(pair_slot):
        first_block = pair_blocks[pair_slot, 0]
        second_block = pair_blocks[pair_slot, 1]
        left_side = whitened[first_block].astype(jnp.float32)
        right_side = jnp.roll(whitened[second_block], -(BLK // 2), axis=3).astype(jnp.float32)
        real_part = lax.optimization_barrier(jnp.sum(left_side[:, 0] * right_side[:, 0] + left_side[:, 1] * right_side[:, 1], axis=0))
        imag_part = lax.optimization_barrier(jnp.sum(left_side[:, 1] * right_side[:, 0] - left_side[:, 0] * right_side[:, 1], axis=0))
        shift_samples = coil_offsets[first_block] - coil_offsets[second_block]
        phases = jnp.mod(bin_index * shift_samples, NT).astype(jnp.float32) * (2.0 * jnp.pi / NT)
        cosine = jnp.cos(phases)[:, None]
        sine_values = jnp.sin(phases)[:, None]
        cross_spec = jnp.stack([real_part * cosine + imag_part * sine_values, imag_part * cosine - real_part * sine_values]).astype(jnp.bfloat16)
        correlation = jnp.einsum('rkc,rkl->cl', cross_spec.astype(jnp.float32), inverse)
        return correlation * (pair_valid[pair_slot].astype(jnp.float32) / jnp.sqrt(jnp.float32(NB * NSEG)))
    return lax.map(one_pair, jnp.arange(PAIRS, dtype=jnp.int32))
```

```python
import functools

import jax
import jax.numpy as jnp
import ml_dtypes
import numpy as np
from jax import lax
from jax.experimental import pallas as pl
from jax.experimental.pallas import tpu as pltpu
from jax.sharding import PartitionSpec as P

AXES = ("group", "shard")
HALF = 16
SMOOTH = 64
NLAG = 512
EPSILON = 1e-05
RADIX = 16
VMEM_BYTES = 56 * 1024 * 1024
F32 = jnp.float32
BF16 = jnp.bfloat16


def as_bf16(table):
    return table.astype(ml_dtypes.bfloat16)


def forward_constants(length):
    inner = length // RADIX
    n1 = np.arange(inner)
    turns = (np.arange(RADIX)[:, None] * n1[None, :]) * (2.0 * np.pi / length)
    twiddle = np.concatenate([np.cos(turns), np.sin(turns)]).astype(np.float32)
    angle = np.mod(n1[:, None] * np.arange(inner // 2)[None, :], inner) * (2.0 * np.pi / inner)
    cosine, sine = np.cos(angle), np.sin(angle)
    table = np.concatenate(
        [np.concatenate([cosine, -sine], axis=1), np.concatenate([sine, cosine], axis=1)]
    ) / np.sqrt(length)
    high = as_bf16(table)
    low = as_bf16(table - high.astype(np.float64))
    return twiddle, np.concatenate([high, high, low])


def band_constants(bands, width, length):
    place = np.arange(width)
    diagonal = ((width - 1 - 2 * place) / 2.0) ** 2 * np.cos(np.pi * NLAG / length)
    beside = place[1:] * (width - place[1:]) / 2.0
    matrix = np.diag(diagonal) + np.diag(beside, 1) + np.diag(beside, -1)
    vectors = np.linalg.eigh(matrix)[1][:, ::-1]
    upper = vectors[(width + 1) // 2 :]
    vectors = vectors * np.sign(upper[np.argmax(np.abs(upper), axis=0), np.arange(width)])[None, :]
    lags = np.arange(NLAG) - NLAG // 2
    waves = np.exp(2j * np.pi * np.outer(place - (width - 1) / 2.0, lags) / length)
    rank = width
    for fewer in range(4, width, 4):
        basis = vectors[:, :fewer]
        if np.abs(waves - basis @ (basis.T @ waves)).max() < 1e-7:
            rank = fewer
            break
    basis = vectors[:, :rank]
    partner = basis.T @ waves
    centres = width * np.arange(bands) + (width - 1) / 2.0
    carrier = np.exp(2j * np.pi * np.outer(centres, lags) / length)
    whole = carrier[:, None, :] * partner[None, :, :]
    table = np.concatenate([whole.real, -whole.imag], axis=1).reshape(bands * 2 * rank, NLAG)
    return basis, as_bf16(np.ascontiguousarray(table.T))


def projection_constants(basis, bins_device):
    width, rank = basis.shape
    rows = np.zeros((2, rank, width // RADIX, 2, RADIX))
    split = basis.T.reshape(rank, width // RADIX, RADIX)
    rows[0, :, :, 0, :] = split
    rows[1, :, :, 1, :] = split
    return as_bf16(rows.reshape(2 * rank, 2 * width))


def real_dft(values):
    count = len(values)
    if count == 1:
        return [(values[0], None)]
    even, odd = real_dft(values[0::2]), real_dft(values[1::2])
    out = [None] * (count // 2 + 1)
    out[0] = (even[0][0] + odd[0][0], None)
    out[count // 2] = (even[0][0] - odd[0][0], None)
    for k in range(1, count // 4 + 1):
        er, ei = even[k]
        orr, oi = odd[k]
        if 4 * k == count:
            out[k] = (er, -orr)
            continue
        c, s = float(np.cos(2 * np.pi * k / count)), float(np.sin(2 * np.pi * k / count))
        tr = orr * c + oi * s
        ti = oi * c - orr * s
        out[k] = (er + tr, ei + ti)
        out[count // 2 - k] = (er - tr, ti - ei)
    return out


def transform_rows(x_ref, twiddle_ref, z_ref, rows):
    inner = x_ref.shape[1] // RADIX

    def step(i, carry):
        at = pl.multiple_of(i * 16, 16)
        for half in range(inner // 128):
            lane = 128 * half
            values = [
                x_ref[pl.ds(at, 16), inner * j + lane : inner * j + lane + 128].astype(F32)
                for j in range(RADIX)
            ]
            bins = real_dft(values)
            for q in range(RADIX):
                yr, yi = bins[q] if q <= RADIX // 2 else bins[RADIX - q]
                if q > RADIX // 2:
                    yi = -yi
                if q == 0:
                    zr, zi = yr, jnp.zeros_like(yr)
                else:
                    c = twiddle_ref[q : q + 1, lane : lane + 128]
                    s = twiddle_ref[RADIX + q : RADIX + q + 1, lane : lane + 128]
                    if yi is None:
                        zr, zi = yr * c, -yr * s
                    else:
                        zr, zi = yr * c + yi * s, yi * c - yr * s
                where = pl.ds(pl.multiple_of(q * rows + at, 16), 16)
                for part, z in ((0, zr), (1, zi)):
                    high = z.astype(BF16)
                    z_ref[where, part * inner + lane : part * inner + lane + 128] = high
                    low = (z - high.astype(F32)).astype(BF16)
                    start = (2 + part) * inner + lane
                    z_ref[where, start : start + 128] = low
        return carry

    lax.fori_loop(0, rows // 16, step, 0)


def transform_inner(z, table_ref):
    depth = z.shape[1]
    out = jnp.dot(z, table_ref[0:depth, :], preferred_element_type=F32)
    return out + jnp.dot(
        z[:, : depth // 2], table_ref[depth:, :], preferred_element_type=F32
    )


def own_kernel(x_ref, twiddle_ref, table_ref, out_ref, z_ref):
    rows = x_ref.shape[0]
    transform_rows(x_ref, twiddle_ref, z_ref, rows)
    for q in range(RADIX):
        values = transform_inner(z_ref[q * rows : (q + 1) * rows, :], table_ref)
        out_ref[q, 0] = values[:, :128]
        out_ref[q, 1] = values[:, 128:]


def shifted(values, by):
    count = values.shape[1]
    lane = lax.broadcasted_iota(jnp.int32, values.shape, 1)
    inside = (lane + by >= 0) & (lane + by < count)
    return jnp.where(inside, pltpu.roll(values, (-by) % count, 1), 0.0)


def whiten_kernel(
    length, offset_ref, own_ref, left_ref, right_ref, twiddle_ref, table_ref, taps_ref, count_ref, out_ref,
    x_ref, z_ref, halo_ref, line_ref, filtered_ref, power_ref, base_ref, rows_ref,
):
    width = own_ref.shape[2]
    x_ref[0:HALF, :] = left_ref[...]
    x_ref[HALF:, :] = right_ref[...]
    transform_rows(x_ref, twiddle_ref, z_ref, 2 * HALF)
    halo_ref[...] = transform_inner(z_ref[...], table_ref)

    power_ref[0] = jnp.zeros(power_ref.shape[1:], F32)

    def filter_step(q, carry):
        at = pl.multiple_of(q * 2 * HALF, 2 * HALF)
        total = None
        for r in range(2):
            halo = halo_ref[pl.ds(at, 2 * HALF), 128 * r : 128 * r + 128]
            line_ref[r, 0:HALF, :] = halo[:HALF]
            line_ref[r, HALF : HALF + width, :] = own_ref[q, r]
            line_ref[r, HALF + width :, :] = halo[HALF:]
            result = jnp.zeros((width, 128), F32)
            for t in range(2 * HALF + 1):
                result = result + taps_ref[q, t : t + 1, :] * line_ref[r, t : t + width, :]
            filtered_ref[q, r] = result
            total = result * result if total is None else total + result * result
        power_ref[q + 1] = power_ref[q] + total
        return carry

    lax.fori_loop(0, RADIX, filter_step, 0)

    reach = SMOOTH // RADIX
    whole = power_ref[RADIX]
    base = whole
    for by in range(1, reach):
        base = base + (shifted(whole, by) + shifted(whole, -by))
    base_ref[...] = base

    bins = lax.broadcasted_iota(jnp.int32, (RADIX, 128), 1) * RADIX + lax.broadcasted_iota(
        jnp.int32, (RADIX, 128), 0
    )
    phases = lax.rem(bins * offset_ref[0], length).astype(F32) * (2.0 * np.pi / length)
    cosine, sine = jnp.cos(phases), jnp.sin(phases)
    for q in range(RADIX):
        window = (
            base_ref[...]
            + shifted(power_ref[RADIX] - power_ref[q], -reach)
            + shifted(power_ref[q + 1], reach)
        )
        scale = lax.rsqrt(window * count_ref[q : q + 1, :] + EPSILON)
        fr, fi = filtered_ref[q, 0], filtered_ref[q, 1]
        c, s = cosine[q : q + 1, :], sine[q : q + 1, :]
        wr = (fr * c + fi * s) * scale
        wi = (fi * c - fr * s) * scale
        rows_ref[pl.ds(q, 128, stride=2 * RADIX), :] = wr.T
        rows_ref[pl.ds(RADIX + q, 128, stride=2 * RADIX), :] = wi.T
    out_ref[...] = rows_ref[...].astype(BF16)


def pair_kernel(slots, pairs_ref, band_ref, basis_ref, out_ref, left_ref, right_ref, cross_ref):
    blocks = band_ref.shape[0]
    groups = band_ref.shape[1] // (2 * RADIX)
    deep = basis_ref.shape[0]

    def spread(i, carry):
        values = band_ref[i].astype(F32)
        left_ref[i] = values
        right_ref[i] = pltpu.roll(values, 64, 1)
        return carry

    lax.fori_loop(0, blocks, spread, 0)

    def owner(d, carry):
        for j in range(slots):
            a = pairs_ref[d * slots + j, 0]
            b = pairs_ref[d * slots + j, 1]
            for m in range(groups):
                lo, mid, hi = 2 * RADIX * m, 2 * RADIX * m + RADIX, 2 * RADIX * (m + 1)
                lr, li = left_ref[a, lo:mid, :], left_ref[a, mid:hi, :]
                rr, ri = right_ref[b, lo:mid, :], right_ref[b, mid:hi, :]
                cross_ref[lo:mid, 128 * j : 128 * j + 128] = (lr * rr + li * ri).astype(BF16)
                cross_ref[mid:hi, 128 * j : 128 * j + 128] = (li * rr - lr * ri).astype(BF16)
        result = jnp.dot(basis_ref[...], cross_ref[...], preferred_element_type=F32)
        stacked = jnp.concatenate([result[:, 128 * j : 128 * j + 128] for j in range(slots)], axis=0)
        out_ref[d] = stacked.astype(BF16)
        return carry

    lax.fori_loop(0, blocks, owner, 0)


def lag_kernel(slots, scale, valid_ref, parts_ref, table_ref, out_ref, wide_ref):
    bands = parts_ref.shape[0]
    deep = parts_ref.shape[1] // slots

    def gather(b, carry):
        values = parts_ref[b].astype(F32)
        for j in range(slots):
            at = pl.multiple_of(b * deep, 8)
            wide_ref[pl.ds(at, deep), 128 * j : 128 * j + 128] = values[deep * j : deep * (j + 1)]
        return carry

    lax.fori_loop(0, bands, gather, 0)
    result = jnp.dot(table_ref[...], wide_ref[...].astype(BF16), preferred_element_type=F32)
    for j in range(slots):
        weight = valid_ref[j].astype(F32) * scale
        out_ref[j] = result[:, 128 * j : 128 * j + 128].T * weight


def vmem():
    return pl.BlockSpec(memory_space=pltpu.VMEM)


def smem():
    return pl.BlockSpec(memory_space=pltpu.SMEM)


def params():
    return pltpu.CompilerParams(vmem_limit_bytes=VMEM_BYTES)


def body(samples, fan_taps, pair_blocks, pair_valid, coil_offsets):
    width = samples.shape[0]
    length = samples.shape[2]
    bin_count = length // 2
    devices = lax.axis_size("group") * lax.axis_size("shard")
    bins_device = bin_count // devices
    slots = pair_valid.shape[0]
    inner = length // RADIX
    lanes = bin_count // RADIX

    twiddle, table = forward_constants(length)
    basis, lag_table = band_constants(devices, bins_device, length)
    project = projection_constants(basis, bins_device)
    deep = project.shape[0]
    bins_k = np.arange(bin_count)
    counts = np.minimum(bins_k + SMOOTH, bin_count - 1) - np.maximum(bins_k - SMOOTH, 0) + 1
    inverse_count = (1.0 / counts).reshape(lanes, RADIX).T.astype(np.float32)

    x = samples.reshape(width, length)
    ends = devices - 1
    left = lax.ppermute(x[width - HALF :], AXES, [(i, i + 1) for i in range(ends)])
    right = lax.ppermute(x[:HALF], AXES, [(i + 1, i) for i in range(ends)])
    taps = jnp.transpose(fan_taps.reshape(2 * HALF + 1, lanes, RADIX), (2, 0, 1))
    offset = lax.dynamic_slice(coil_offsets, (lax.axis_index(AXES),), (1,))

    own = pl.pallas_call(
        own_kernel,
        out_shape=jax.ShapeDtypeStruct((RADIX, 2, width, lanes), F32),
        in_specs=[vmem()] * 3,
        out_specs=vmem(),
        scratch_shapes=[pltpu.VMEM((RADIX * width, 4 * inner), BF16)],
        compiler_params=params(),
        name="own_spectra",
    )(x, twiddle, table)

    rows = pl.pallas_call(
        functools.partial(whiten_kernel, length),
        out_shape=jax.ShapeDtypeStruct((2 * bin_count, width), BF16),
        in_specs=[smem()] + [vmem()] * 7,
        out_specs=vmem(),
        scratch_shapes=[
            pltpu.VMEM((2 * HALF, length), BF16),
            pltpu.VMEM((RADIX * 2 * HALF, 4 * inner), BF16),
            pltpu.VMEM((RADIX * 2 * HALF, 2 * lanes), F32),
            pltpu.VMEM((2, width + 2 * HALF, lanes), F32),
            pltpu.VMEM((RADIX, 2, width, lanes), F32),
            pltpu.VMEM((RADIX + 1, width, lanes), F32),
            pltpu.VMEM((width, lanes), F32),
            pltpu.VMEM((2 * bin_count, width), F32),
        ],
        compiler_params=params(),
        name="whiten",
    )(offset, own, left, right, twiddle, table, taps, inverse_count)

    band = lax.all_to_all(
        rows.reshape(devices, 2 * bins_device, width), AXES, split_axis=0, concat_axis=0, tiled=True
    )

    parts = pl.pallas_call(
        functools.partial(pair_kernel, slots),
        out_shape=jax.ShapeDtypeStruct((devices, slots * deep, width), BF16),
        in_specs=[smem(), vmem(), vmem()],
        out_specs=vmem(),
        scratch_shapes=[
            pltpu.VMEM((devices, 2 * bins_device, width), F32),
            pltpu.VMEM((devices, 2 * bins_device, width), F32),
            pltpu.VMEM((2 * bins_device, slots * width), BF16),
        ],
        compiler_params=params(),
        name="pair_products",
    )(pair_blocks, band, project)

    owned = lax.all_to_all(parts, AXES, split_axis=0, concat_axis=0, tiled=True)

    return pl.pallas_call(
        functools.partial(lag_kernel, slots, float(1.0 / np.sqrt(bin_count * samples.shape[1]))),
        out_shape=jax.ShapeDtypeStruct((slots, width, NLAG), F32),
        in_specs=[smem(), vmem(), vmem()],
        out_specs=vmem(),
        scratch_shapes=[pltpu.VMEM((devices * deep, slots * width), F32)],
        compiler_params=params(),
        name="lags",
    )(pair_valid, owned, lag_table)


def solution(mesh):
    return jax.shard_map(
        body,
        mesh=mesh,
        in_specs=(P(AXES, None, None), P(), P(), P(AXES), P()),
        out_specs=P(AXES, None, None),
        check_vma=False,
    )
```

```python
import functools

import jax
import jax.numpy as jnp
import ml_dtypes
import numpy as np
from jax import lax
from jax.experimental import pallas as pl
from jax.experimental.pallas import tpu as pltpu
from jax.sharding import PartitionSpec as P

AXES = ("group", "shard")
HALF = 16
SMOOTH = 64
NLAG = 512
EPSILON = 1e-05
RADIX = 16
VMEM_BYTES = 32 * 1024 * 1024
F32 = jnp.float32
BF16 = jnp.bfloat16


def as_bf16(table):
    return table.astype(ml_dtypes.bfloat16)


def forward_constants(length):
    inner = length // RADIX
    n1 = np.arange(inner)
    turns = (np.arange(RADIX)[:, None] * n1[None, :]) * (2.0 * np.pi / length)
    twiddle = np.concatenate([np.cos(turns), np.sin(turns)]).astype(np.float32)
    angle = np.mod(n1[:, None] * np.arange(inner // 2)[None, :], inner) * (2.0 * np.pi / inner)
    cosine, sine = np.cos(angle), np.sin(angle)
    table = np.concatenate(
        [np.concatenate([cosine, -sine], axis=1), np.concatenate([sine, cosine], axis=1)]
    ) / np.sqrt(length)
    high = as_bf16(table)
    low = as_bf16(table - high.astype(np.float64))
    return twiddle, np.concatenate([high, high, low])


def band_constants(bands, width, length):
    place = np.arange(width)
    diagonal = ((width - 1 - 2 * place) / 2.0) ** 2 * np.cos(np.pi * NLAG / length)
    beside = place[1:] * (width - place[1:]) / 2.0
    matrix = np.diag(diagonal) + np.diag(beside, 1) + np.diag(beside, -1)
    vectors = np.linalg.eigh(matrix)[1][:, ::-1]
    upper = vectors[(width + 1) // 2 :]
    vectors = vectors * np.sign(upper[np.argmax(np.abs(upper), axis=0), np.arange(width)])[None, :]
    lags = np.arange(NLAG) - NLAG // 2
    waves = np.exp(2j * np.pi * np.outer(place - (width - 1) / 2.0, lags) / length)
    rank = width
    for fewer in range(4, width, 4):
        basis = vectors[:, :fewer]
        if np.abs(waves - basis @ (basis.T @ waves)).max() < 1e-7:
            rank = fewer
            break
    basis = vectors[:, :rank]
    partner = basis.T @ waves
    centres = width * np.arange(bands) + (width - 1) / 2.0
    carrier = np.exp(2j * np.pi * np.outer(centres, lags) / length)
    whole = carrier[:, None, :] * partner[None, :, :]
    table = np.concatenate([whole.real, -whole.imag], axis=1).reshape(bands * 2 * rank, NLAG)
    return basis, as_bf16(np.ascontiguousarray(table.T))


def projection_constants(basis, bins_device):
    width, rank = basis.shape
    rows = np.zeros((2, rank, width // RADIX, 2, RADIX))
    split = basis.T.reshape(rank, width // RADIX, RADIX)
    rows[0, :, :, 0, :] = split
    rows[1, :, :, 1, :] = split
    return as_bf16(rows.reshape(2 * rank, 2 * width))


def real_dft(values):
    count = len(values)
    if count == 1:
        return [(values[0], None)]
    even, odd = real_dft(values[0::2]), real_dft(values[1::2])
    out = [None] * (count // 2 + 1)
    out[0] = (even[0][0] + odd[0][0], None)
    out[count // 2] = (even[0][0] - odd[0][0], None)
    for k in range(1, count // 4 + 1):
        er, ei = even[k]
        orr, oi = odd[k]
        if 4 * k == count:
            out[k] = (er, -orr)
            continue
        c, s = float(np.cos(2 * np.pi * k / count)), float(np.sin(2 * np.pi * k / count))
        tr = orr * c + oi * s
        ti = oi * c - orr * s
        out[k] = (er + tr, ei + ti)
        out[count // 2 - k] = (er - tr, ti - ei)
    return out


def transform_rows(x_ref, first, rows, twiddle_ref, z_ref):
    inner = x_ref.shape[1] // RADIX
    for at in range(0, rows, 16):
        for lane in range(0, inner, 128):
            values = [
                x_ref[first + at : first + at + 16, inner * j + lane : inner * j + lane + 128].astype(F32)
                for j in range(RADIX)
            ]
            bins = real_dft(values)
            for q in range(RADIX):
                yr, yi = bins[q] if q <= RADIX // 2 else bins[RADIX - q]
                if q > RADIX // 2:
                    yi = -yi
                if q == 0:
                    zr, zi = yr, jnp.zeros_like(yr)
                else:
                    c = twiddle_ref[q : q + 1, lane : lane + 128]
                    s = twiddle_ref[RADIX + q : RADIX + q + 1, lane : lane + 128]
                    if yi is None:
                        zr, zi = yr * c, -yr * s
                    else:
                        zr, zi = yr * c + yi * s, yi * c - yr * s
                where = slice(q * rows + at, q * rows + at + 16)
                for part, z in ((0, zr), (1, zi)):
                    high = z.astype(BF16)
                    z_ref[where, part * inner + lane : part * inner + lane + 128] = high
                    low = (z - high.astype(F32)).astype(BF16)
                    start = (2 + part) * inner + lane
                    z_ref[where, start : start + 128] = low


def transform_inner(z, table_ref):
    depth = z.shape[1]
    out = jnp.dot(z, table_ref[0:depth, :], preferred_element_type=F32)
    return out + jnp.dot(
        z[:, : depth // 2], table_ref[depth:, :], preferred_element_type=F32
    )


def own_kernel(x_ref, taps_ref, twiddle_ref, table_ref, out_ref, split_ref, z0_ref, z1_ref, turned_ref):
    chunk = z0_ref.shape[0] // RADIX
    steps = x_ref.shape[0] // chunk
    slots = (z0_ref, z1_ref)
    transform_rows(x_ref, 0, chunk, twiddle_ref, z0_ref)
    for i in range(steps):
        if i + 1 < steps:
            transform_rows(x_ref, (i + 1) * chunk, chunk, twiddle_ref, slots[(i + 1) % 2])
        values = transform_inner(slots[i % 2][...], table_ref)
        for q in range(RADIX):
            out_ref[q, 0, i * chunk : (i + 1) * chunk, :] = values[q * chunk : (q + 1) * chunk, :128]
            out_ref[q, 1, i * chunk : (i + 1) * chunk, :] = values[q * chunk : (q + 1) * chunk, 128:]
    count = taps_ref.shape[0]
    for at in range(0, taps_ref.shape[1], 128):
        turned_ref[at : at + 128, 0:count] = taps_ref[:, at : at + 128].T
    for q in range(RADIX):
        split_ref[q] = turned_ref[pl.ds(q, 128, stride=RADIX), 0:count].T


def shifted(values, by):
    count = values.shape[1]
    lane = lax.broadcasted_iota(jnp.int32, values.shape, 1)
    inside = (lane + by >= 0) & (lane + by < count)
    return jnp.where(inside, pltpu.roll(values, (-by) % count, 1), 0.0)


def whiten_kernel(
    length, offset_ref, own_ref, left_ref, right_ref, twiddle_ref, table_ref, taps_ref, count_ref, out_ref,
    x_ref, z_ref, halo_ref, line_ref, filtered_ref, power_ref, base_ref, rows_ref,
):
    width = own_ref.shape[2]
    x_ref[0:HALF, :] = left_ref[...]
    x_ref[HALF:, :] = right_ref[...]
    transform_rows(x_ref, 0, 2 * HALF, twiddle_ref, z_ref)
    halo_ref[...] = transform_inner(z_ref[...], table_ref)

    power_ref[0] = jnp.zeros(power_ref.shape[1:], F32)

    def filter_step(q, carry):
        at = pl.multiple_of(q * 2 * HALF, 2 * HALF)
        total = None
        for r in range(2):
            halo = halo_ref[pl.ds(at, 2 * HALF), 128 * r : 128 * r + 128]
            line_ref[r, 0:HALF, :] = halo[:HALF]
            line_ref[r, HALF : HALF + width, :] = own_ref[q, r]
            line_ref[r, HALF + width :, :] = halo[HALF:]
            result = jnp.zeros((width, 128), F32)
            for t in range(2 * HALF + 1):
                result = result + taps_ref[q, t : t + 1, :] * line_ref[r, t : t + width, :]
            filtered_ref[q, r] = result
            total = result * result if total is None else total + result * result
        power_ref[q + 1] = power_ref[q] + total
        return carry

    lax.fori_loop(0, RADIX, filter_step, 0)

    reach = SMOOTH // RADIX
    whole = power_ref[RADIX]
    base = whole
    for by in range(1, reach):
        base = base + (shifted(whole, by) + shifted(whole, -by))
    base_ref[...] = base

    bins = lax.broadcasted_iota(jnp.int32, (RADIX, 128), 1) * RADIX + lax.broadcasted_iota(
        jnp.int32, (RADIX, 128), 0
    )
    phases = lax.rem(bins * offset_ref[lax.axis_index(AXES)], length).astype(F32) * (2.0 * np.pi / length)
    cosine, sine = jnp.cos(phases), jnp.sin(phases)
    for q in range(RADIX):
        window = (
            base_ref[...]
            + shifted(power_ref[RADIX] - power_ref[q], -reach)
            + shifted(power_ref[q + 1], reach)
        )
        scale = lax.rsqrt(window * count_ref[q : q + 1, :] + EPSILON)
        fr, fi = filtered_ref[q, 0], filtered_ref[q, 1]
        c, s = cosine[q : q + 1, :], sine[q : q + 1, :]
        wr = (fr * c + fi * s) * scale
        wi = (fi * c - fr * s) * scale
        rows_ref[pl.ds(q, 128, stride=2 * RADIX), :] = wr.T
        rows_ref[pl.ds(RADIX + q, 128, stride=2 * RADIX), :] = wi.T
    out_ref[...] = rows_ref[...].astype(BF16)


def pair_kernel(slots, pairs_ref, band_ref, basis_ref, out_ref, left_ref, right_ref, cross0_ref, cross1_ref):
    blocks = band_ref.shape[0]
    groups = band_ref.shape[1] // (2 * RADIX)

    def spread(i, carry):
        for n in range(4):
            values = band_ref[4 * i + n].astype(F32)
            left_ref[4 * i + n] = values
            right_ref[4 * i + n] = pltpu.roll(values, 64, 1)
        return carry

    lax.fori_loop(0, blocks // 4, spread, 0)

    def products(d, cross_ref):
        for j in range(slots):
            a = pairs_ref[0, d * slots + j]
            b = pairs_ref[1, d * slots + j]
            for m in range(groups):
                lo, mid, hi = 2 * RADIX * m, 2 * RADIX * m + RADIX, 2 * RADIX * (m + 1)
                lr, li = left_ref[a, lo:mid, :], left_ref[a, mid:hi, :]
                rr, ri = right_ref[b, lo:mid, :], right_ref[b, mid:hi, :]
                cross_ref[lo:mid, 128 * j : 128 * j + 128] = (lr * rr + li * ri).astype(BF16)
                cross_ref[mid:hi, 128 * j : 128 * j + 128] = (li * rr - lr * ri).astype(BF16)

    def project(d, cross_ref):
        result = jnp.dot(basis_ref[...], cross_ref[...], preferred_element_type=F32)
        stacked = jnp.concatenate([result[:, 128 * j : 128 * j + 128] for j in range(slots)], axis=0)
        out_ref[d] = stacked.astype(BF16)

    products(0, cross0_ref)

    def owners(i, carry):
        products(2 * i + 1, cross1_ref)
        project(2 * i, cross0_ref)
        products(jnp.minimum(2 * i + 2, blocks - 1), cross0_ref)
        project(2 * i + 1, cross1_ref)
        return carry

    lax.fori_loop(0, blocks // 2, owners, 0)


def lag_kernel(slots, scale, valid_ref, parts_ref, table_ref, out_ref, wide_ref, stage_ref, sem_ref):
    bands = parts_ref.shape[0]
    deep = parts_ref.shape[1] // slots

    def gather(i, carry):
        for n in range(4):
            b = 4 * i + n
            values = parts_ref[b].astype(F32)
            for j in range(slots):
                at = pl.multiple_of(b * deep, 8)
                wide_ref[pl.ds(at, deep), 128 * j : 128 * j + 128] = values[deep * j : deep * (j + 1)]
        return carry

    lax.fori_loop(0, bands // 4, gather, 0)
    copies = []
    for first in range(0, slots, 2):
        columns = wide_ref[:, 128 * first : 128 * first + 256].astype(BF16)
        result = jnp.dot(table_ref[...], columns, preferred_element_type=F32)
        for j in range(2):
            weight = valid_ref[first + j].astype(F32) * scale
            stage_ref[first + j] = result[:, 128 * j : 128 * j + 128].T * weight
            copy = pltpu.make_async_copy(stage_ref.at[first + j], out_ref.at[first + j], sem_ref.at[first + j])
            copy.start()
            copies.append(copy)
    for copy in copies:
        copy.wait()


def vmem():
    return pl.BlockSpec(memory_space=pltpu.VMEM)


def smem():
    return pl.BlockSpec(memory_space=pltpu.SMEM)


def params():
    return pltpu.CompilerParams(vmem_limit_bytes=VMEM_BYTES)


def near(array):
    return pltpu.with_memory_space_constraint(array, pltpu.VMEM)


def body(samples, fan_taps, pair_blocks, pair_valid, coil_offsets):
    width = samples.shape[0]
    length = samples.shape[2]
    bin_count = length // 2
    devices = lax.axis_size("group") * lax.axis_size("shard")
    bins_device = bin_count // devices
    slots = pair_valid.shape[0]
    inner = length // RADIX
    lanes = bin_count // RADIX
    chunk = 32

    twiddle, table = forward_constants(length)
    basis, lag_table = band_constants(devices, bins_device, length)
    project = projection_constants(basis, bins_device)
    deep = project.shape[0]
    bins_k = np.arange(bin_count)
    counts = np.minimum(bins_k + SMOOTH, bin_count - 1) - np.maximum(bins_k - SMOOTH, 0) + 1
    inverse_count = (1.0 / counts).reshape(lanes, RADIX).T.astype(np.float32)
    twiddle, table = near(jnp.asarray(twiddle)), near(jnp.asarray(table))

    x = samples.reshape(width, length)
    ends = devices - 1
    left = lax.ppermute(x[width - HALF :], AXES, [(i, i + 1) for i in range(ends)])
    right = lax.ppermute(x[:HALF], AXES, [(i + 1, i) for i in range(ends)])

    own, taps = pl.pallas_call(
        own_kernel,
        out_shape=(
            pltpu.VMEM((RADIX, 2, width, lanes), F32),
            pltpu.VMEM((RADIX, 2 * HALF + 1, lanes), F32),
        ),
        in_specs=[vmem()] * 4,
        out_specs=(vmem(), vmem()),
        scratch_shapes=[
            pltpu.VMEM((RADIX * chunk, 4 * inner), BF16),
            pltpu.VMEM((RADIX * chunk, 4 * inner), BF16),
            pltpu.VMEM((bin_count, 128), F32),
        ],
        compiler_params=params(),
        name="own_spectra",
    )(near(x), near(fan_taps), twiddle, table)

    rows = pl.pallas_call(
        functools.partial(whiten_kernel, length),
        out_shape=pltpu.VMEM((2 * bin_count, width), BF16),
        in_specs=[smem()] + [vmem()] * 7,
        out_specs=vmem(),
        scratch_shapes=[
            pltpu.VMEM((2 * HALF, length), BF16),
            pltpu.VMEM((RADIX * 2 * HALF, 4 * inner), BF16),
            pltpu.VMEM((RADIX * 2 * HALF, 2 * lanes), F32),
            pltpu.VMEM((2, width + 2 * HALF, lanes), F32),
            pltpu.VMEM((RADIX, 2, width, lanes), F32),
            pltpu.VMEM((RADIX + 1, width, lanes), F32),
            pltpu.VMEM((width, lanes), F32),
            pltpu.VMEM((2 * bin_count, width), F32),
        ],
        compiler_params=params(),
        name="whiten",
    )(
        coil_offsets, near(own), near(left), near(right), twiddle, table, near(taps),
        near(jnp.asarray(inverse_count)),
    )

    band = lax.all_to_all(
        rows.reshape(devices, 2 * bins_device, width), AXES, split_axis=0, concat_axis=0, tiled=True
    )

    parts = pl.pallas_call(
        functools.partial(pair_kernel, slots),
        out_shape=pltpu.VMEM((devices, slots * deep, width), BF16),
        in_specs=[smem(), vmem(), vmem()],
        out_specs=vmem(),
        scratch_shapes=[
            pltpu.VMEM((devices, 2 * bins_device, width), F32),
            pltpu.VMEM((devices, 2 * bins_device, width), F32),
            pltpu.VMEM((2 * bins_device, slots * width), BF16),
            pltpu.VMEM((2 * bins_device, slots * width), BF16),
        ],
        compiler_params=params(),
        name="pair_products",
    )(pair_blocks.T, near(band), near(jnp.asarray(project)))

    owned = lax.all_to_all(parts, AXES, split_axis=0, concat_axis=0, tiled=True)

    return pl.pallas_call(
        functools.partial(lag_kernel, slots, float(1.0 / np.sqrt(bin_count * samples.shape[1]))),
        out_shape=jax.ShapeDtypeStruct((slots, width, NLAG), F32),
        in_specs=[smem(), vmem(), vmem()],
        out_specs=pl.BlockSpec(memory_space=pl.ANY),
        scratch_shapes=[
            pltpu.VMEM((devices * deep, slots * width), F32),
            pltpu.VMEM((slots, width, NLAG), F32),
            pltpu.SemaphoreType.DMA((slots,)),
        ],
        compiler_params=params(),
        name="lags",
    )(pair_valid, near(owned), near(jnp.asarray(lag_table)))


def solution(mesh):
    return jax.shard_map(
        body,
        mesh=mesh,
        in_specs=(P(AXES, None, None), P(), P(), P(AXES), P()),
        out_specs=P(AXES, None, None),
        check_vma=False,
    )
```

```python
import functools

import jax
import jax.numpy as jnp
import ml_dtypes
import numpy as np
from jax import lax
from jax.experimental import pallas as pl
from jax.experimental.pallas import tpu as pltpu
from jax.sharding import PartitionSpec as P

AXES = ("group", "shard")
HALF = 16
SMOOTH = 64
NLAG = 512
EPSILON = 1e-05
RADIX = 16
VMEM_BYTES = 32 * 1024 * 1024
F32 = jnp.float32
BF16 = jnp.bfloat16


def as_bf16(table):
    return table.astype(ml_dtypes.bfloat16)


def forward_constants(length):
    inner = length // RADIX
    n1 = np.arange(inner)
    turns = (np.arange(RADIX)[:, None] * n1[None, :]) * (2.0 * np.pi / length)
    twiddle = np.concatenate([np.cos(turns), np.sin(turns)]).astype(np.float32)
    angle = np.mod(n1[:, None] * np.arange(inner // 2)[None, :], inner) * (2.0 * np.pi / inner)
    cosine, sine = np.cos(angle), np.sin(angle)
    table = np.concatenate(
        [np.concatenate([cosine, -sine], axis=1), np.concatenate([sine, cosine], axis=1)]
    ) / np.sqrt(length)
    high = as_bf16(table)
    low = as_bf16(table - high.astype(np.float64))
    return twiddle, np.concatenate([high, high, low])


def band_constants(bands, width, length):
    place = np.arange(width)
    diagonal = ((width - 1 - 2 * place) / 2.0) ** 2 * np.cos(np.pi * NLAG / length)
    beside = place[1:] * (width - place[1:]) / 2.0
    matrix = np.diag(diagonal) + np.diag(beside, 1) + np.diag(beside, -1)
    vectors = np.linalg.eigh(matrix)[1][:, ::-1]
    upper = vectors[(width + 1) // 2 :]
    vectors = vectors * np.sign(upper[np.argmax(np.abs(upper), axis=0), np.arange(width)])[None, :]
    lags = np.arange(NLAG) - NLAG // 2
    waves = np.exp(2j * np.pi * np.outer(place - (width - 1) / 2.0, lags) / length)
    rank = width
    for fewer in range(4, width, 4):
        basis = vectors[:, :fewer]
        error = waves - basis @ (basis.T @ waves)
        if np.sqrt(np.mean(np.abs(error) ** 2)) < 1e-7:
            rank = fewer
            break
    basis = vectors[:, :rank]
    partner = basis.T @ waves
    centres = width * np.arange(bands) + (width - 1) / 2.0
    carrier = np.exp(2j * np.pi * np.outer(centres, lags) / length)
    whole = carrier[:, None, :] * partner[None, :, :]
    table = np.concatenate([whole.real, -whole.imag], axis=1).reshape(bands * 2 * rank, NLAG)
    return basis, as_bf16(np.ascontiguousarray(table.T))


def projection_constants(basis, halves):
    width, rank = basis.shape
    groups = width // halves // RADIX
    rows = np.zeros((halves, 2, rank, groups, 2, RADIX))
    split = basis.T.reshape(rank, halves, groups, RADIX).transpose(1, 0, 2, 3)
    rows[:, 0, :, :, 0, :] = split
    rows[:, 1, :, :, 1, :] = split
    return as_bf16(rows.reshape(halves, 2 * rank, 2 * groups * RADIX))


def real_dft(values):
    count = len(values)
    if count == 1:
        return [(values[0], None)]
    even, odd = real_dft(values[0::2]), real_dft(values[1::2])
    out = [None] * (count // 2 + 1)
    out[0] = (even[0][0] + odd[0][0], None)
    out[count // 2] = (even[0][0] - odd[0][0], None)
    for k in range(1, count // 4 + 1):
        er, ei = even[k]
        orr, oi = odd[k]
        if 4 * k == count:
            out[k] = (er, -orr)
            continue
        c, s = float(np.cos(2 * np.pi * k / count)), float(np.sin(2 * np.pi * k / count))
        tr = orr * c + oi * s
        ti = oi * c - orr * s
        out[k] = (er + tr, ei + ti)
        out[count // 2 - k] = (er - tr, ti - ei)
    return out


def transform_rows(x_ref, first, rows, twiddle_ref, z_ref):
    inner = x_ref.shape[1] // RADIX
    for at in range(0, rows, 16):
        for lane in range(0, inner, 128):
            values = [
                x_ref[first + at : first + at + 16, inner * j + lane : inner * j + lane + 128].astype(F32)
                for j in range(RADIX)
            ]
            bins = real_dft(values)
            for q in range(RADIX):
                yr, yi = bins[q] if q <= RADIX // 2 else bins[RADIX - q]
                if q > RADIX // 2:
                    yi = -yi
                if q == 0:
                    zr, zi = yr, jnp.zeros_like(yr)
                else:
                    c = twiddle_ref[q : q + 1, lane : lane + 128]
                    s = twiddle_ref[RADIX + q : RADIX + q + 1, lane : lane + 128]
                    if yi is None:
                        zr, zi = yr * c, -yr * s
                    else:
                        zr, zi = yr * c + yi * s, yi * c - yr * s
                where = slice(q * rows + at, q * rows + at + 16)
                for part, z in ((0, zr), (1, zi)):
                    high = z.astype(BF16)
                    z_ref[where, part * inner + lane : part * inner + lane + 128] = high
                    low = (z - high.astype(F32)).astype(BF16)
                    start = (2 + part) * inner + lane
                    z_ref[where, start : start + 128] = low


def transform_inner(z, table_ref):
    depth = z.shape[1]
    out = jnp.dot(z, table_ref[0:depth, :], preferred_element_type=F32)
    return out + jnp.dot(
        z[:, : depth // 2], table_ref[depth:, :], preferred_element_type=F32
    )


def own_kernel(
    x_hbm, taps_hbm, small_hbm, table_hbm, out_ref, split_ref, small_ref, table_ref,
    x_ref, taps_ref, z0_ref, z1_ref, turned_ref, sem_ref,
):
    chunk = z0_ref.shape[0] // RADIX
    steps = x_ref.shape[0] // chunk
    slots = (z0_ref, z1_ref)
    copies = [pltpu.make_async_copy(small_hbm, small_ref, sem_ref.at[0])]
    for i in range(steps):
        part = pl.ds(i * chunk, chunk)
        copies.append(pltpu.make_async_copy(x_hbm.at[part], x_ref.at[part], sem_ref.at[1 + i]))
    copies.append(pltpu.make_async_copy(table_hbm, table_ref, sem_ref.at[1 + steps]))
    copies.append(pltpu.make_async_copy(taps_hbm, taps_ref, sem_ref.at[2 + steps]))
    for copy in copies:
        copy.start()
    copies[0].wait()
    copies[1].wait()
    transform_rows(x_ref, 0, chunk, small_ref, z0_ref)
    for i in range(steps):
        if i + 1 < steps:
            copies[2 + i].wait()
        if i == 0:
            copies[1 + steps].wait()
        if i + 1 < steps:
            transform_rows(x_ref, (i + 1) * chunk, chunk, small_ref, slots[(i + 1) % 2])
        values = transform_inner(slots[i % 2][...], table_ref)
        for q in range(RADIX):
            out_ref[q, 0, i * chunk : (i + 1) * chunk, :] = values[q * chunk : (q + 1) * chunk, :128]
            out_ref[q, 1, i * chunk : (i + 1) * chunk, :] = values[q * chunk : (q + 1) * chunk, 128:]
    copies[2 + steps].wait()
    count = taps_ref.shape[0]
    for at in range(0, taps_ref.shape[1], 128):
        turned_ref[at : at + 128, 0:count] = taps_ref[:, at : at + 128].T
    for q in range(RADIX):
        split_ref[q] = turned_ref[pl.ds(q, 128, stride=RADIX), 0:count].T


def shifted(values, by):
    count = values.shape[1]
    lane = lax.broadcasted_iota(jnp.int32, values.shape, 1)
    inside = (lane + by >= 0) & (lane + by < count)
    return jnp.where(inside, pltpu.roll(values, (-by) % count, 1), 0.0)


def whiten_kernel(
    length, offset_ref, own_ref, left_ref, right_ref, small_ref, table_ref, taps_ref, out_ref,
    x_ref, z_ref, halo_ref, line_ref, filtered_ref, power_ref, base_ref, rows_ref,
):
    width = own_ref.shape[2]
    x_ref[0:HALF, :] = left_ref[...]
    x_ref[HALF:, :] = right_ref[...]
    transform_rows(x_ref, 0, 2 * HALF, small_ref, z_ref)
    halo_ref[...] = transform_inner(z_ref[...], table_ref)

    power_ref[0] = jnp.zeros(power_ref.shape[1:], F32)

    def filter_step(q, carry):
        at = pl.multiple_of(q * 2 * HALF, 2 * HALF)
        total = None
        for r in range(2):
            halo = halo_ref[pl.ds(at, 2 * HALF), 128 * r : 128 * r + 128]
            line_ref[r, 0:HALF, :] = halo[:HALF]
            line_ref[r, HALF : HALF + width, :] = own_ref[q, r]
            line_ref[r, HALF + width :, :] = halo[HALF:]
            result = jnp.zeros((width, 128), F32)
            for t in range(2 * HALF + 1):
                result = result + taps_ref[q, t : t + 1, :] * line_ref[r, t : t + width, :]
            filtered_ref[q, r] = result
            total = result * result if total is None else total + result * result
        power_ref[q + 1] = power_ref[q] + total
        return carry

    lax.fori_loop(0, RADIX, filter_step, 0)

    reach = SMOOTH // RADIX
    whole = power_ref[RADIX]
    base = whole
    for by in range(1, reach):
        base = base + (shifted(whole, by) + shifted(whole, -by))
    base_ref[...] = base

    bins = lax.broadcasted_iota(jnp.int32, (RADIX, 128), 1) * RADIX + lax.broadcasted_iota(
        jnp.int32, (RADIX, 128), 0
    )
    phases = lax.rem(bins * offset_ref[lax.axis_index(AXES)], length).astype(F32) * (2.0 * np.pi / length)
    cosine, sine = jnp.cos(phases), jnp.sin(phases)
    for q in range(RADIX):
        window = (
            base_ref[...]
            + shifted(power_ref[RADIX] - power_ref[q], -reach)
            + shifted(power_ref[q + 1], reach)
        )
        scale = lax.rsqrt(window * small_ref[2 * RADIX + q : 2 * RADIX + q + 1, 0:128] + EPSILON)
        fr, fi = filtered_ref[q, 0], filtered_ref[q, 1]
        c, s = cosine[q : q + 1, :], sine[q : q + 1, :]
        wr = (fr * c + fi * s) * scale
        wi = (fi * c - fr * s) * scale
        rows_ref[pl.ds(q, 128, stride=2 * RADIX), :] = wr.T
        rows_ref[pl.ds(RADIX + q, 128, stride=2 * RADIX), :] = wi.T
    out_ref[...] = rows_ref[...].astype(BF16)


def pair_kernel(slots, mine, pairs_ref, band_ref, basis_ref, *refs):
    if mine:
        before_ref, (out_ref, left_ref, right_ref, cross0_ref, cross1_ref) = None, refs
    else:
        before_ref, out_ref, left_ref, right_ref, cross0_ref, cross1_ref = refs
    blocks = band_ref.shape[0]
    groups = band_ref.shape[1] // (2 * RADIX)
    deep = basis_ref.shape[1]
    half = lax.rem(lax.axis_index("shard"), 2)
    part = half if mine else 1 - half
    kept = slots // 2

    def spread(i, carry):
        for n in range(4):
            values = band_ref[4 * i + n].astype(F32)
            left_ref[4 * i + n] = values
            right_ref[4 * i + n] = pltpu.roll(values, 64, 1)
        return carry

    lax.fori_loop(0, blocks // 4, spread, 0)

    def products(i, cross_ref):
        for n in range(2 * kept):
            slot = (2 * i + n // kept) * slots + half * kept + n % kept
            a, b = pairs_ref[0, slot], pairs_ref[1, slot]
            for m in range(groups):
                lo, mid, hi = 2 * RADIX * m, 2 * RADIX * m + RADIX, 2 * RADIX * (m + 1)
                lr, li = left_ref[a, lo:mid, :], left_ref[a, mid:hi, :]
                rr, ri = right_ref[b, lo:mid, :], right_ref[b, mid:hi, :]
                cross_ref[lo:mid, 128 * n : 128 * n + 128] = (lr * rr + li * ri).astype(BF16)
                cross_ref[mid:hi, 128 * n : 128 * n + 128] = (li * rr - lr * ri).astype(BF16)

    def project(i, cross_ref):
        result = jnp.dot(basis_ref[part], cross_ref[...], preferred_element_type=F32)
        for u in range(2):
            lanes = [128 * (kept * u + j) for j in range(kept)]
            stacked = jnp.concatenate([result[:, at : at + 128] for at in lanes], axis=0)
            if mine:
                out_ref[2 * i + u] = stacked
            else:
                out_ref[2 * i + u] = (stacked + before_ref[2 * i + u]).astype(BF16)

    last = blocks // 2 - 1
    products(0, cross0_ref)

    def owners(i, carry):
        products(2 * i + 1, cross1_ref)
        project(2 * i, cross0_ref)
        products(jnp.minimum(2 * i + 2, last), cross0_ref)
        project(2 * i + 1, cross1_ref)
        return carry

    lax.fori_loop(0, blocks // 4, owners, 0)


def lag_kernel(slots, scale, valid_ref, parts_ref, table_ref, out_ref, wide_ref, stage_ref, sem_ref):
    bands = parts_ref.shape[0] // 2
    kept = slots // 2
    deep = parts_ref.shape[1] // kept

    def gather(i, carry):
        for n in range(4):
            b = 4 * i + n
            at = pl.multiple_of(b * deep, 8)
            for half in range(2):
                values = parts_ref[2 * b + half].astype(F32)
                for j in range(kept):
                    lane = 128 * (half * kept + j)
                    wide_ref[pl.ds(at, deep), lane : lane + 128] = values[deep * j : deep * (j + 1)]
        return carry

    lax.fori_loop(0, bands // 4, gather, 0)
    copies = []
    for first in range(0, slots, 2):
        columns = wide_ref[:, 128 * first : 128 * first + 256].astype(BF16)
        result = jnp.dot(table_ref[...], columns, preferred_element_type=F32)
        for j in range(2):
            weight = valid_ref[first + j].astype(F32) * scale
            stage_ref[first + j] = result[:, 128 * j : 128 * j + 128].T * weight
            copy = pltpu.make_async_copy(stage_ref.at[first + j], out_ref.at[first + j], sem_ref.at[first + j])
            copy.start()
            copies.append(copy)
    for copy in copies:
        copy.wait()


def vmem():
    return pl.BlockSpec(memory_space=pltpu.VMEM)


def smem():
    return pl.BlockSpec(memory_space=pltpu.SMEM)


def params():
    return pltpu.CompilerParams(vmem_limit_bytes=VMEM_BYTES)


def near(array):
    return pltpu.with_memory_space_constraint(array, pltpu.VMEM)


def distant(array):
    return pltpu.with_memory_space_constraint(array, pltpu.HBM)


def far():
    return pl.BlockSpec(memory_space=pltpu.HBM)


def body(samples, fan_taps, pair_blocks, pair_valid, coil_offsets):
    width = samples.shape[0]
    length = samples.shape[2]
    bin_count = length // 2
    devices = lax.axis_size("group") * lax.axis_size("shard")
    shards = lax.axis_size("shard")
    bins_device = bin_count // devices
    slots = pair_valid.shape[0]
    inner = length // RADIX
    lanes = bin_count // RADIX
    chunk = 32

    twiddle, table = forward_constants(length)
    basis, lag_table = band_constants(devices // 2, 2 * bins_device, length)
    project = projection_constants(basis, 2)
    deep = project.shape[1]
    bins_k = np.arange(bin_count)
    counts = np.minimum(bins_k + SMOOTH, bin_count - 1) - np.maximum(bins_k - SMOOTH, 0) + 1
    small = np.zeros((3 * RADIX, inner), np.float32)
    small[: 2 * RADIX] = twiddle
    small[2 * RADIX :, :lanes] = (1.0 / counts).reshape(lanes, RADIX).T

    x = samples.reshape(width, length)
    ends = devices - 1
    left = lax.ppermute(x[width - HALF :], AXES, [(i, i + 1) for i in range(ends)])
    right = lax.ppermute(x[:HALF], AXES, [(i + 1, i) for i in range(ends)])

    own, taps, small, table = pl.pallas_call(
        own_kernel,
        out_shape=(
            pltpu.VMEM((RADIX, 2, width, lanes), F32),
            pltpu.VMEM((RADIX, 2 * HALF + 1, lanes), F32),
            pltpu.VMEM(small.shape, F32),
            pltpu.VMEM(table.shape, BF16),
        ),
        in_specs=[far()] * 4,
        out_specs=(vmem(), vmem(), vmem(), vmem()),
        scratch_shapes=[
            pltpu.VMEM((width, length), BF16),
            pltpu.VMEM(fan_taps.shape, F32),
            pltpu.VMEM((RADIX * chunk, 4 * inner), BF16),
            pltpu.VMEM((RADIX * chunk, 4 * inner), BF16),
            pltpu.VMEM((bin_count, 128), F32),
            pltpu.SemaphoreType.DMA((width // chunk + 3,)),
        ],
        compiler_params=params(),
        name="own_spectra",
    )(distant(x), distant(fan_taps), distant(jnp.asarray(small)), distant(jnp.asarray(table)))

    rows = pl.pallas_call(
        functools.partial(whiten_kernel, length),
        out_shape=pltpu.VMEM((2 * bin_count, width), BF16),
        in_specs=[smem()] + [vmem()] * 6,
        out_specs=vmem(),
        scratch_shapes=[
            pltpu.VMEM((2 * HALF, length), BF16),
            pltpu.VMEM((RADIX * 2 * HALF, 4 * inner), BF16),
            pltpu.VMEM((RADIX * 2 * HALF, 2 * lanes), F32),
            pltpu.VMEM((2, width + 2 * HALF, lanes), F32),
            pltpu.VMEM((RADIX, 2, width, lanes), F32),
            pltpu.VMEM((RADIX + 1, width, lanes), F32),
            pltpu.VMEM((width, lanes), F32),
            pltpu.VMEM((2 * bin_count, width), F32),
        ],
        compiler_params=params(),
        name="whiten",
    )(coil_offsets, near(own), near(left), near(right), near(small), near(table), near(taps))

    band = lax.all_to_all(
        rows.reshape(devices, 2 * bins_device, width), AXES, split_axis=0, concat_axis=0, tiled=True
    )
    other = lax.ppermute(band, "shard", [(i, i ^ 1) for i in range(shards)])

    pairs = pair_blocks.T
    project = near(jnp.asarray(project))
    sums = (devices, slots // 2 * deep, width)

    def products(mine, part, before):
        return pl.pallas_call(
            functools.partial(pair_kernel, slots, mine),
            out_shape=pltpu.VMEM(sums, F32 if mine else BF16),
            in_specs=[smem()] + [vmem()] * (2 + len(before)),
            out_specs=vmem(),
            scratch_shapes=[
                pltpu.VMEM((devices, 2 * bins_device, width), F32),
                pltpu.VMEM((devices, 2 * bins_device, width), F32),
                pltpu.VMEM((2 * bins_device, slots * width), BF16),
                pltpu.VMEM((2 * bins_device, slots * width), BF16),
            ],
            compiler_params=params(),
            name="pairs_own_part" if mine else "pairs_other_part",
        )(pairs, near(part), project, *before)

    first = products(True, band, ())
    parts = products(False, other, (near(first),))

    owned = lax.all_to_all(parts, AXES, split_axis=0, concat_axis=0, tiled=True)

    return pl.pallas_call(
        functools.partial(lag_kernel, slots, float(1.0 / np.sqrt(bin_count * samples.shape[1]))),
        out_shape=jax.ShapeDtypeStruct((slots, width, NLAG), F32),
        in_specs=[smem(), vmem(), vmem()],
        out_specs=pl.BlockSpec(memory_space=pl.ANY),
        scratch_shapes=[
            pltpu.VMEM((devices // 2 * deep, slots * width), F32),
            pltpu.VMEM((slots, width, NLAG), F32),
            pltpu.SemaphoreType.DMA((slots,)),
        ],
        compiler_params=params(),
        name="lags",
    )(pair_valid, near(owned), near(jnp.asarray(lag_table)))


def solution(mesh):
    return jax.shard_map(
        body,
        mesh=mesh,
        in_specs=(P(AXES, None, None), P(), P(), P(AXES), P()),
        out_specs=P(AXES, None, None),
        check_vma=False,
    )
```

```python
import functools

import jax
import jax.numpy as jnp
import ml_dtypes
import numpy as np
from jax import lax
from jax.experimental import pallas as pl
from jax.experimental.pallas import tpu as pltpu
from jax.sharding import PartitionSpec as P

AXES = ("group", "shard")
HALF = 16
SMOOTH = 64
NLAG = 512
EPSILON = 1e-05
RADIX = 16
VMEM_BYTES = 32 * 1024 * 1024
F32 = jnp.float32
BF16 = jnp.bfloat16


def as_bf16(table):
    return table.astype(ml_dtypes.bfloat16)


def forward_constants(length):
    inner = length // RADIX
    n1 = np.arange(inner)
    turns = (np.arange(RADIX)[:, None] * n1[None, :]) * (2.0 * np.pi / length)
    twiddle = np.concatenate([np.cos(turns), np.sin(turns)]).astype(np.float32)
    angle = np.mod(n1[:, None] * np.arange(inner // 2)[None, :], inner) * (2.0 * np.pi / inner)
    cosine, sine = np.cos(angle), np.sin(angle)
    table = np.concatenate(
        [np.concatenate([cosine, -sine], axis=1), np.concatenate([sine, cosine], axis=1)]
    ) / np.sqrt(length)
    high = as_bf16(table)
    low = as_bf16(table - high.astype(np.float64))
    return twiddle, np.concatenate([high, low])


def band_constants(bands, width, length):
    place = np.arange(width)
    diagonal = ((width - 1 - 2 * place) / 2.0) ** 2 * np.cos(np.pi * NLAG / length)
    beside = place[1:] * (width - place[1:]) / 2.0
    matrix = np.diag(diagonal) + np.diag(beside, 1) + np.diag(beside, -1)
    vectors = np.linalg.eigh(matrix)[1][:, ::-1]
    upper = vectors[(width + 1) // 2 :]
    vectors = vectors * np.sign(upper[np.argmax(np.abs(upper), axis=0), np.arange(width)])[None, :]
    lags = np.arange(NLAG) - NLAG // 2
    waves = np.exp(2j * np.pi * np.outer(place - (width - 1) / 2.0, lags) / length)
    rank = width
    for fewer in range(4, width, 4):
        basis = vectors[:, :fewer]
        error = waves - basis @ (basis.T @ waves)
        if np.sqrt(np.mean(np.abs(error) ** 2)) < 1e-7:
            rank = fewer
            break
    basis = vectors[:, :rank]
    partner = basis.T @ waves
    centres = width * np.arange(bands) + (width - 1) / 2.0
    carrier = np.exp(2j * np.pi * np.outer(centres, lags) / length)
    whole = carrier[:, None, :] * partner[None, :, :]
    table = np.concatenate([whole.real, -whole.imag], axis=1).reshape(bands * 2 * rank, NLAG)
    return basis, as_bf16(np.ascontiguousarray(table.T))


def projection_constants(basis, halves):
    width, rank = basis.shape
    groups = width // halves // RADIX
    rows = np.zeros((halves, 2, rank, groups, 2, RADIX))
    split = basis.T.reshape(rank, halves, groups, RADIX).transpose(1, 0, 2, 3)
    rows[:, 0, :, :, 0, :] = split
    rows[:, 1, :, :, 1, :] = split
    return as_bf16(rows.reshape(halves, 2 * rank, 2 * groups * RADIX))


def real_dft(values):
    count = len(values)
    if count == 1:
        return [(values[0], None)]
    even, odd = real_dft(values[0::2]), real_dft(values[1::2])
    out = [None] * (count // 2 + 1)
    out[0] = (even[0][0] + odd[0][0], None)
    out[count // 2] = (even[0][0] - odd[0][0], None)
    for k in range(1, count // 4 + 1):
        er, ei = even[k]
        orr, oi = odd[k]
        if 4 * k == count:
            out[k] = (er, -orr)
            continue
        c, s = float(np.cos(2 * np.pi * k / count)), float(np.sin(2 * np.pi * k / count))
        tr = orr * c + oi * s
        ti = oi * c - orr * s
        out[k] = (er + tr, ei + ti)
        out[count // 2 - k] = (er - tr, ti - ei)
    return out


def transform_rows(x_ref, first, rows, twiddle_ref, z_ref):
    inner = x_ref.shape[1] // RADIX
    for at in range(0, rows, 16):
        for lane in range(0, inner, 128):
            values = [
                x_ref[first + at : first + at + 16, inner * j + lane : inner * j + lane + 128].astype(F32)
                for j in range(RADIX)
            ]
            bins = real_dft(values)
            for q in range(RADIX):
                yr, yi = bins[q] if q <= RADIX // 2 else bins[RADIX - q]
                if q > RADIX // 2:
                    yi = -yi
                if q == 0:
                    zr, zi = yr, jnp.zeros_like(yr)
                else:
                    c = twiddle_ref[q : q + 1, lane : lane + 128]
                    s = twiddle_ref[RADIX + q : RADIX + q + 1, lane : lane + 128]
                    if yi is None:
                        zr, zi = yr * c, -yr * s
                    else:
                        zr, zi = yr * c + yi * s, yi * c - yr * s
                where = slice(q * rows + at, q * rows + at + 16)
                for part, z in ((0, zr), (1, zi)):
                    high = z.astype(BF16)
                    z_ref[where, part * inner + lane : part * inner + lane + 128] = high
                    low = (z - high.astype(F32)).astype(BF16)
                    start = (2 + part) * inner + lane
                    z_ref[where, start : start + 128] = low


def transform_inner(z, table_ref):
    depth = z.shape[1] // 2
    high, low = table_ref[0:depth, :], table_ref[depth:, :]
    out = jnp.dot(z[:, :depth], high, preferred_element_type=F32)
    out = out + jnp.dot(z[:, depth:], high, preferred_element_type=F32)
    return out + jnp.dot(z[:, :depth], low, preferred_element_type=F32)


def own_kernel(
    x_hbm, taps_hbm, small_hbm, table_hbm, out_ref, split_ref, both_ref, small_ref, table_ref,
    x_ref, taps_ref, z0_ref, z1_ref, turned_ref, sem_ref,
):
    chunk = z0_ref.shape[0] // RADIX
    steps = x_ref.shape[0] // chunk
    slots = (z0_ref, z1_ref)
    copies = [pltpu.make_async_copy(taps_hbm, taps_ref, sem_ref.at[0])]
    copies.append(pltpu.make_async_copy(small_hbm, small_ref, sem_ref.at[1]))
    copies.append(pltpu.make_async_copy(table_hbm, table_ref, sem_ref.at[2]))
    for i in range(steps):
        part = pl.ds(i * chunk, chunk)
        copies.append(pltpu.make_async_copy(x_hbm.at[part], x_ref.at[part], sem_ref.at[3 + i]))
    for copy in copies:
        copy.start()

    copies[0].wait()
    count = taps_ref.shape[0]
    pitch = RADIX + 1
    for at in range(0, taps_ref.shape[1], 128):
        turned = taps_ref[:, at : at + 128].T
        for n in range(128 // RADIX):
            row = (at // RADIX + n) * pitch
            turned_ref[row : row + RADIX, 0:count] = turned[RADIX * n : RADIX * (n + 1)]
    for q in range(RADIX):
        taps = turned_ref[pl.ds(q, 128, stride=pitch), 0:count].T
        split_ref[q, 0:count, :] = taps
        even = split_ref[q, pl.ds(0, HALF, stride=2), :]
        odd = split_ref[q, pl.ds(1, HALF, stride=2), :]
        both_ref[q, 0:HALF, :] = even + odd
        both_ref[q, HALF : HALF + 1, :] = taps[count - 1 :]

    copies[1].wait()
    copies[3].wait()
    transform_rows(x_ref, 0, chunk, small_ref, z0_ref)
    copies[2].wait()
    for i in range(steps):
        if i + 1 < steps:
            copies[4 + i].wait()
            transform_rows(x_ref, (i + 1) * chunk, chunk, small_ref, slots[(i + 1) % 2])
        values = transform_inner(slots[i % 2][...], table_ref)
        for q in range(RADIX):
            out_ref[q, 0, i * chunk : (i + 1) * chunk, :] = values[q * chunk : (q + 1) * chunk, :128]
            out_ref[q, 1, i * chunk : (i + 1) * chunk, :] = values[q * chunk : (q + 1) * chunk, 128:]


def whiten_kernel(
    length, offset_ref, own_ref, left_ref, right_ref, small_ref, table_ref, taps_ref, both_ref, out_ref,
    x_ref, z_ref, halo_ref, even_ref, odd_ref, pair_ref, part_ref, filtered_ref, power_ref, base_ref, rows_ref,
):
    width = own_ref.shape[2]
    x_ref[0:HALF, :] = left_ref[...]
    x_ref[HALF:, :] = right_ref[...]
    transform_rows(x_ref, 0, 2 * HALF, small_ref, z_ref)
    values = transform_inner(z_ref[...], table_ref)
    halo_ref[0] = values[:, :128]
    halo_ref[1] = values[:, 128:]

    power_ref[0] = jnp.zeros(power_ref.shape[1:], F32)

    half = width // 2
    count = half + HALF
    edge = HALF // 2
    even_ref[:, count:, :] = jnp.zeros((2, even_ref.shape[1] - count, 128), F32)

    def placed(values, parity):
        quarter = half // 2
        for high in range(2):
            first = half * high + quarter * parity
            yield slice(first, first + quarter), values[quarter * high : quarter * (high + 1)]

    def filter_step(q, carry):
        at = pl.multiple_of(q * 2 * HALF, 2 * HALF)
        total = [None, None]
        for r in range(2):
            for first, ref in ((0, even_ref), (1, odd_ref)):
                ref[r, 0:edge, :] = halo_ref[r, pl.ds(at + first, edge, stride=2), :]
                ref[r, edge : edge + half, :] = own_ref[q, r, pl.ds(first, half, stride=2), :]
                ref[r, edge + half : count, :] = halo_ref[r, pl.ds(at + HALF + first, edge, stride=2), :]
            pair_ref[r] = odd_ref[r] + even_ref[r, 1 : count + 1, :]
            evens = jnp.zeros((half + 8, 128), F32)
            odds = jnp.zeros((half, 128), F32)
            pairs = jnp.zeros((half, 128), F32)
            for u in range(HALF + 1):
                evens = evens + taps_ref[q, 2 * u : 2 * u + 1, :] * even_ref[r, u : u + half + 8, :]
            part_ref[r] = evens
            for u in range(HALF):
                odds = odds + taps_ref[q, 2 * u + 1 : 2 * u + 2, :] * odd_ref[r, u : u + half, :]
            for u in range(HALF + 1):
                pairs = pairs + both_ref[q, u : u + 1, :] * pair_ref[r, u : u + half, :]
            result = (evens[:half] + odds, pairs - (part_ref[r, 1 : half + 1, :] + odds))
            for n in range(2):
                for rows, values in placed(result[n], n):
                    filtered_ref[q, r, rows, :] = values
                square = result[n] * result[n]
                total[n] = square if r == 0 else total[n] + square
        for n in range(2):
            for rows, values in placed(total[n], n):
                power_ref[q + 1, rows, :] = power_ref[q, rows, :] + values
        return carry

    lax.fori_loop(0, RADIX, filter_step, 0)

    reach = SMOOTH // RADIX
    lane = lax.broadcasted_iota(jnp.int32, (1, 128), 1)

    def shifted(values, by):
        inside = jnp.where((lane + by >= 0) & (lane + by < 128), 1.0, 0.0)
        return pltpu.roll(values, (-by) % 128, 1) * inside

    whole = power_ref[RADIX]
    base = whole
    for by in range(1, reach):
        base = base + (shifted(whole, by) + shifted(whole, -by))
    base_ref[...] = base

    bins = lax.broadcasted_iota(jnp.int32, (RADIX, 128), 1) * RADIX + lax.broadcasted_iota(
        jnp.int32, (RADIX, 128), 0
    )
    phases = lax.rem(bins * offset_ref[lax.axis_index(AXES)], length).astype(F32) * (2.0 * np.pi / length)
    cosine, sine = jnp.cos(phases), jnp.sin(phases)
    pitch = 2 * RADIX + 1
    for q in range(RADIX):
        window = (
            base_ref[...]
            + shifted(power_ref[RADIX] - power_ref[q], -reach)
            + shifted(power_ref[q + 1], reach)
        )
        scale = lax.rsqrt(window * small_ref[2 * RADIX + q : 2 * RADIX + q + 1, 0:128] + EPSILON)
        fr, fi = filtered_ref[q, 0], filtered_ref[q, 1]
        c, s = cosine[q : q + 1, :], sine[q : q + 1, :]
        wr = (fr * c + fi * s) * scale
        wi = (fi * c - fr * s) * scale
        rows_ref[pl.ds(q, 128, stride=pitch), :] = wr.T
        rows_ref[pl.ds(RADIX + q, 128, stride=pitch), :] = wi.T
    for m in range(128):
        rows = rows_ref[m * pitch : m * pitch + 2 * RADIX, :]
        out_ref[2 * RADIX * m : 2 * RADIX * (m + 1), :] = rows.astype(BF16)


def pair_kernel(slots, mine, pairs_ref, band_ref, basis_ref, *refs):
    if mine:
        before_ref, (out_ref, left_ref, right_ref, cross0_ref, cross1_ref) = None, refs
    else:
        before_ref, out_ref, left_ref, right_ref, cross0_ref, cross1_ref = refs
    blocks = band_ref.shape[0]
    groups = band_ref.shape[1] // (2 * RADIX)
    deep = basis_ref.shape[1]
    half = lax.rem(lax.axis_index("shard"), 2)
    part = half if mine else 1 - half
    kept = slots // 2
    step = cross0_ref.shape[1] // (128 * kept)

    def spread(i, carry):
        for n in range(8):
            values = band_ref[8 * i + n].astype(F32)
            left_ref[8 * i + n] = values
            right_ref[8 * i + n] = pltpu.roll(values, 64, 1)
        return carry

    lax.fori_loop(0, blocks // 8, spread, 0)

    def products(i, cross_ref):
        for n in range(step * kept):
            slot = (step * i + n // kept) * slots + half * kept + n % kept
            a, b = pairs_ref[0, slot], pairs_ref[1, slot]
            for m in range(groups):
                lo, mid, hi = 2 * RADIX * m, 2 * RADIX * m + RADIX, 2 * RADIX * (m + 1)
                lr, li = left_ref[a, lo:mid, :], left_ref[a, mid:hi, :]
                rr, ri = right_ref[b, lo:mid, :], right_ref[b, mid:hi, :]
                cross_ref[lo:mid, 128 * n : 128 * n + 128] = (lr * rr + li * ri).astype(BF16)
                cross_ref[mid:hi, 128 * n : 128 * n + 128] = (li * rr - lr * ri).astype(BF16)

    def project(i, cross_ref):
        result = jnp.dot(basis_ref[part], cross_ref[...], preferred_element_type=F32)
        for u in range(step):
            lanes = [128 * (kept * u + j) for j in range(kept)]
            stacked = jnp.concatenate([result[:, at : at + 128] for at in lanes], axis=0)
            if mine:
                out_ref[step * i + u] = stacked
            else:
                out_ref[step * i + u] = (stacked + before_ref[step * i + u]).astype(BF16)

    last = blocks // step - 1
    products(0, cross0_ref)

    def owners(i, carry):
        products(2 * i + 1, cross1_ref)
        project(2 * i, cross0_ref)
        products(jnp.minimum(2 * i + 2, last), cross0_ref)
        project(2 * i + 1, cross1_ref)
        return carry

    lax.fori_loop(0, blocks // (2 * step), owners, 0)


def lag_kernel(slots, scale, valid_ref, parts_ref, table_ref, out_ref, wide_ref, stage_ref, sem_ref):
    bands = parts_ref.shape[0] // 2
    kept = slots // 2
    deep = parts_ref.shape[1] // kept

    def gather(i, carry):
        for n in range(4):
            b = 4 * i + n
            at = pl.multiple_of(b * deep, 8)
            for half in range(2):
                values = parts_ref[2 * b + half].astype(F32)
                for j in range(kept):
                    lane = 128 * (half * kept + j)
                    wide_ref[pl.ds(at, deep), lane : lane + 128] = values[deep * j : deep * (j + 1)]
        return carry

    lax.fori_loop(0, bands // 4, gather, 0)
    copies = []
    for first in range(0, slots, 2):
        columns = wide_ref[:, 128 * first : 128 * first + 256].astype(BF16)
        for n in range(NLAG // 128):
            result = jnp.dot(table_ref[128 * n : 128 * n + 128, :], columns, preferred_element_type=F32)
            for j in range(2):
                turned = result[:, 128 * j : 128 * j + 128].T * (valid_ref[first + j].astype(F32) * scale)
                half = turned.shape[0] // 2
                at = (first + j) * (NLAG // 128) + n
                for high in range(2):
                    for parity in range(2):
                        row = half * high + half // 2 * parity
                        rows = turned[row : row + half // 2]
                        stage_ref[at, pl.ds(half * high + parity, half // 2, stride=2), :] = rows
                lanes = pl.ds(128 * n, 128)
                copy = pltpu.make_async_copy(stage_ref.at[at], out_ref.at[first + j, :, lanes], sem_ref.at[at])
                copy.start()
                copies.append(copy)
    for copy in copies:
        copy.wait()


def vmem():
    return pl.BlockSpec(memory_space=pltpu.VMEM)


def smem():
    return pl.BlockSpec(memory_space=pltpu.SMEM)


def params():
    return pltpu.CompilerParams(vmem_limit_bytes=VMEM_BYTES)


def near(array):
    return pltpu.with_memory_space_constraint(array, pltpu.VMEM)


def distant(array):
    return pltpu.with_memory_space_constraint(array, pltpu.HBM)


def far():
    return pl.BlockSpec(memory_space=pltpu.HBM)


def body(samples, fan_taps, pair_blocks, pair_valid, coil_offsets):
    width = samples.shape[0]
    length = samples.shape[2]
    bin_count = length // 2
    devices = lax.axis_size("group") * lax.axis_size("shard")
    shards = lax.axis_size("shard")
    bins_device = bin_count // devices
    slots = pair_valid.shape[0]
    inner = length // RADIX
    lanes = bin_count // RADIX
    chunk = 64

    twiddle, table = forward_constants(length)
    basis, lag_table = band_constants(devices // 2, 2 * bins_device, length)
    project = projection_constants(basis, 2)
    deep = project.shape[1]
    bins_k = np.arange(bin_count)
    counts = np.minimum(bins_k + SMOOTH, bin_count - 1) - np.maximum(bins_k - SMOOTH, 0) + 1
    small = np.zeros((3 * RADIX, inner), np.float32)
    small[: 2 * RADIX] = twiddle
    small[2 * RADIX :, :lanes] = (1.0 / counts).reshape(lanes, RADIX).T

    x = samples.reshape(width, length)
    ends = devices - 1
    left = lax.ppermute(x[width - HALF :], AXES, [(i, i + 1) for i in range(ends)])
    right = lax.ppermute(x[:HALF], AXES, [(i + 1, i) for i in range(ends)])

    own, taps, both, small, table = pl.pallas_call(
        own_kernel,
        out_shape=(
            pltpu.VMEM((RADIX, 2, width, lanes), F32),
            pltpu.VMEM((RADIX, 2 * HALF + 1, lanes), F32),
            pltpu.VMEM((RADIX, HALF + 1, lanes), F32),
            pltpu.VMEM(small.shape, F32),
            pltpu.VMEM(table.shape, BF16),
        ),
        in_specs=[far()] * 4,
        out_specs=(vmem(),) * 5,
        scratch_shapes=[
            pltpu.VMEM((width, length), BF16),
            pltpu.VMEM(fan_taps.shape, F32),
            pltpu.VMEM((RADIX * chunk, 4 * inner), BF16),
            pltpu.VMEM((RADIX * chunk, 4 * inner), BF16),
            pltpu.VMEM((bin_count + lanes, 128), F32),
            pltpu.SemaphoreType.DMA((width // chunk + 3,)),
        ],
        compiler_params=params(),
        name="own_spectra",
    )(distant(x), distant(fan_taps), distant(jnp.asarray(small)), distant(jnp.asarray(table)))

    rows = pl.pallas_call(
        functools.partial(whiten_kernel, length),
        out_shape=pltpu.VMEM((2 * bin_count, width), BF16),
        in_specs=[smem()] + [vmem()] * 7,
        out_specs=vmem(),
        scratch_shapes=[
            pltpu.VMEM((2 * HALF, length), BF16),
            pltpu.VMEM((RADIX * 2 * HALF, 4 * inner), BF16),
            pltpu.VMEM((2, RADIX * 2 * HALF, lanes), F32),
            pltpu.VMEM((2, width // 2 + HALF + 8, lanes), F32),
            pltpu.VMEM((2, width // 2 + HALF, lanes), F32),
            pltpu.VMEM((2, width // 2 + HALF, lanes), F32),
            pltpu.VMEM((2, width // 2 + 8, lanes), F32),
            pltpu.VMEM((RADIX, 2, width, lanes), F32),
            pltpu.VMEM((RADIX + 1, width, lanes), F32),
            pltpu.VMEM((width, lanes), F32),
            pltpu.VMEM((2 * bin_count + lanes, width), F32),
        ],
        compiler_params=params(),
        name="whiten",
    )(coil_offsets, near(own), near(left), near(right), near(small), near(table), near(taps), near(both))

    band = lax.all_to_all(
        rows.reshape(devices, 2 * bins_device, width), AXES, split_axis=0, concat_axis=0, tiled=True
    )
    other = lax.ppermute(band, "shard", [(i, i ^ 1) for i in range(shards)])

    pairs = pair_blocks.T
    project = near(jnp.asarray(project))
    sums = (devices, slots // 2 * deep, width)

    def products(mine, part, before):
        return pl.pallas_call(
            functools.partial(pair_kernel, slots, mine),
            out_shape=pltpu.VMEM(sums, F32 if mine else BF16),
            in_specs=[smem()] + [vmem()] * (2 + len(before)),
            out_specs=vmem(),
            scratch_shapes=[
                pltpu.VMEM((devices, 2 * bins_device, width), F32),
                pltpu.VMEM((devices, 2 * bins_device, width), F32),
                pltpu.VMEM((2 * bins_device, 4 * slots * width), BF16),
                pltpu.VMEM((2 * bins_device, 4 * slots * width), BF16),
            ],
            compiler_params=params(),
            name="pairs_own_part" if mine else "pairs_other_part",
        )(pairs, near(part), project, *before)

    first = products(True, band, ())
    parts = products(False, other, (near(first),))

    owned = lax.all_to_all(parts, AXES, split_axis=0, concat_axis=0, tiled=True)

    return pl.pallas_call(
        functools.partial(lag_kernel, slots, float(1.0 / np.sqrt(bin_count * samples.shape[1]))),
        out_shape=jax.ShapeDtypeStruct((slots, width, NLAG), F32),
        in_specs=[smem(), vmem(), vmem()],
        out_specs=pl.BlockSpec(memory_space=pl.ANY),
        scratch_shapes=[
            pltpu.VMEM((devices // 2 * deep, slots * width), F32),
            pltpu.VMEM((slots * NLAG // 128, width, 128), F32),
            pltpu.SemaphoreType.DMA((slots * NLAG // 128,)),
        ],
        compiler_params=params(),
        name="lags",
    )(pair_valid, near(owned), near(jnp.asarray(lag_table)))


def solution(mesh):
    return jax.shard_map(
        body,
        mesh=mesh,
        in_specs=(P(AXES, None, None), P(), P(), P(AXES), P()),
        out_specs=P(AXES, None, None),
        check_vma=False,
    )
```

```python
import functools

import jax
import jax.numpy as jnp
import ml_dtypes
import numpy as np
from jax import lax
from jax.experimental import pallas as pl
from jax.experimental.pallas import tpu as pltpu
from jax.sharding import PartitionSpec as P

AXES = ("group", "shard")
HALF = 16
SMOOTH = 64
NLAG = 512
EPSILON = 1e-05
RADIX = 16
VMEM_BYTES = 32 * 1024 * 1024
F32 = jnp.float32
BF16 = jnp.bfloat16


def as_bf16(table):
    return table.astype(ml_dtypes.bfloat16)


def forward_constants(length):
    inner = length // RADIX
    n1 = np.arange(inner)
    turns = (np.arange(RADIX)[:, None] * n1[None, :]) * (2.0 * np.pi / length)
    twiddle = np.concatenate([np.cos(turns), np.sin(turns)]).astype(np.float32)
    angle = np.mod(n1[:, None] * np.arange(inner // 2)[None, :], inner) * (2.0 * np.pi / inner)
    cosine, sine = np.cos(angle), np.sin(angle)
    table = np.concatenate(
        [np.concatenate([cosine, -sine], axis=1), np.concatenate([sine, cosine], axis=1)]
    ) / np.sqrt(length)
    high = as_bf16(table)
    low = as_bf16(table - high.astype(np.float64))
    return twiddle, np.concatenate([high, low])


def band_constants(bands, width, length):
    place = np.arange(width)
    diagonal = ((width - 1 - 2 * place) / 2.0) ** 2 * np.cos(np.pi * NLAG / length)
    beside = place[1:] * (width - place[1:]) / 2.0
    matrix = np.diag(diagonal) + np.diag(beside, 1) + np.diag(beside, -1)
    vectors = np.linalg.eigh(matrix)[1][:, ::-1]
    upper = vectors[(width + 1) // 2 :]
    vectors = vectors * np.sign(upper[np.argmax(np.abs(upper), axis=0), np.arange(width)])[None, :]
    lags = np.arange(NLAG) - NLAG // 2
    waves = np.exp(2j * np.pi * np.outer(place - (width - 1) / 2.0, lags) / length)
    rank = width
    for fewer in range(4, width, 4):
        basis = vectors[:, :fewer]
        error = waves - basis @ (basis.T @ waves)
        if np.sqrt(np.mean(np.abs(error) ** 2)) < 1e-7:
            rank = fewer
            break
    basis = vectors[:, :rank]
    partner = basis.T @ waves
    centres = width * np.arange(bands) + (width - 1) / 2.0
    carrier = np.exp(2j * np.pi * np.outer(centres, lags) / length)
    whole = carrier[:, None, :] * partner[None, :, :]
    table = np.concatenate([whole.real, -whole.imag], axis=1).reshape(bands * 2 * rank, NLAG)
    return basis, as_bf16(np.ascontiguousarray(table.T))


def projection_constants(basis, halves):
    width, rank = basis.shape
    groups = width // halves // RADIX
    rows = np.zeros((halves, 2, rank, groups, 2, RADIX))
    split = basis.T.reshape(rank, halves, groups, RADIX).transpose(1, 0, 2, 3)
    rows[:, 0, :, :, 0, :] = split
    rows[:, 1, :, :, 1, :] = split
    return as_bf16(rows.reshape(halves, 2 * rank, 2 * groups * RADIX))


def real_dft(values):
    count = len(values)
    if count == 1:
        return [(values[0], None)]
    even, odd = real_dft(values[0::2]), real_dft(values[1::2])
    out = [None] * (count // 2 + 1)
    out[0] = (even[0][0] + odd[0][0], None)
    out[count // 2] = (even[0][0] - odd[0][0], None)
    for k in range(1, count // 4 + 1):
        er, ei = even[k]
        orr, oi = odd[k]
        if 4 * k == count:
            out[k] = (er, -orr)
            continue
        c, s = float(np.cos(2 * np.pi * k / count)), float(np.sin(2 * np.pi * k / count))
        tr = orr * c + oi * s
        ti = oi * c - orr * s
        out[k] = (er + tr, ei + ti)
        out[count // 2 - k] = (er - tr, ti - ei)
    return out


def transform_rows(x_ref, first, rows, twiddle_ref, z_ref):
    inner = x_ref.shape[1] // RADIX
    for at in range(0, rows, 16):
        for lane in range(0, inner, 128):
            values = [
                x_ref[first + at : first + at + 16, inner * j + lane : inner * j + lane + 128].astype(F32)
                for j in range(RADIX)
            ]
            bins = real_dft(values)
            for q in range(RADIX):
                yr, yi = bins[q] if q <= RADIX // 2 else bins[RADIX - q]
                if q > RADIX // 2:
                    yi = -yi
                if q == 0:
                    zr, zi = yr, jnp.zeros_like(yr)
                else:
                    c = twiddle_ref[q : q + 1, lane : lane + 128]
                    s = twiddle_ref[RADIX + q : RADIX + q + 1, lane : lane + 128]
                    if yi is None:
                        zr, zi = yr * c, -yr * s
                    else:
                        zr, zi = yr * c + yi * s, yi * c - yr * s
                where = slice(q * rows + at, q * rows + at + 16)
                for part, z in ((0, zr), (1, zi)):
                    high = z.astype(BF16)
                    z_ref[where, part * inner + lane : part * inner + lane + 128] = high
                    low = (z - high.astype(F32)).astype(BF16)
                    start = (2 + part) * inner + lane
                    z_ref[where, start : start + 128] = low


def transform_inner(z, table_ref):
    depth = z.shape[1] // 2
    high, low = table_ref[0:depth, :], table_ref[depth:, :]
    out = jnp.dot(z[:, :depth], high, preferred_element_type=F32)
    out = out + jnp.dot(z[:, depth:], high, preferred_element_type=F32)
    return out + jnp.dot(z[:, :depth], low, preferred_element_type=F32)


def own_kernel(
    x_hbm, taps_hbm, small_hbm, table_hbm, out_ref, split_ref, both_ref, small_ref, table_ref,
    x_ref, taps_ref, z0_ref, z1_ref, turned_ref, sem_ref,
):
    chunk = z0_ref.shape[0] // RADIX
    steps = x_ref.shape[0] // chunk
    slots = (z0_ref, z1_ref)
    copies = [pltpu.make_async_copy(taps_hbm, taps_ref, sem_ref.at[0])]
    copies.append(pltpu.make_async_copy(small_hbm, small_ref, sem_ref.at[1]))
    for i in range(steps):
        rows = pl.ds(i * chunk, chunk)
        copies.append(pltpu.make_async_copy(x_hbm.at[rows], x_ref.at[rows], sem_ref.at[3 + i]))
    table_copy = pltpu.make_async_copy(table_hbm, table_ref, sem_ref.at[2])
    for i, copy in enumerate(copies):
        copy.start()
        if i == 2:
            table_copy.start()

    copies[0].wait()
    count = taps_ref.shape[0]
    pitch = RADIX + 1
    for at in range(0, taps_ref.shape[1], 128):
        turned = taps_ref[:, at : at + 128].T
        for n in range(128 // RADIX):
            row = (at // RADIX + n) * pitch
            turned_ref[row : row + RADIX, 0:count] = turned[RADIX * n : RADIX * (n + 1)]
    for q in range(RADIX):
        taps = turned_ref[pl.ds(q, 128, stride=pitch), 0:count].T
        split_ref[q, 0:count, :] = taps
        even = split_ref[q, pl.ds(0, HALF, stride=2), :]
        odd = split_ref[q, pl.ds(1, HALF, stride=2), :]
        both_ref[q, 0:HALF, :] = even + odd
        both_ref[q, HALF : HALF + 1, :] = taps[count - 1 :]

    copies[1].wait()

    copies[2].wait()
    transform_rows(x_ref, 0, chunk, small_ref, z0_ref)
    table_copy.wait()
    for i in range(steps):
        if i + 1 < steps:
            copies[3 + i].wait()
            transform_rows(x_ref, (i + 1) * chunk, chunk, small_ref, slots[(i + 1) % 2])
        values = transform_inner(slots[i % 2][...], table_ref)
        for q in range(RADIX):
            out_ref[q, 0, i * chunk : (i + 1) * chunk, :] = values[q * chunk : (q + 1) * chunk, :128]
            out_ref[q, 1, i * chunk : (i + 1) * chunk, :] = values[q * chunk : (q + 1) * chunk, 128:]


def whiten_kernel(
    length, offset_ref, own_ref, left_ref, right_ref, small_ref, table_ref, taps_ref, both_ref, out_ref,
    x_ref, z_ref, halo_ref, even_ref, odd_ref, pair_ref, part_ref, filtered_ref, power_ref, base_ref, rows_ref,
):
    width = own_ref.shape[2]
    x_ref[0:HALF, :] = left_ref[...]
    x_ref[HALF:, :] = right_ref[...]
    transform_rows(x_ref, 0, 2 * HALF, small_ref, z_ref)
    values = transform_inner(z_ref[...], table_ref)
    halo_ref[0] = values[:, :128]
    halo_ref[1] = values[:, 128:]

    power_ref[0] = jnp.zeros(power_ref.shape[1:], F32)

    half = width // 2
    count = half + HALF
    edge = HALF // 2
    even_ref[:, count:, :] = jnp.zeros((2, even_ref.shape[1] - count, 128), F32)

    def placed(values, parity):
        quarter = half // 2
        for high in range(2):
            first = half * high + quarter * parity
            yield slice(first, first + quarter), values[quarter * high : quarter * (high + 1)]

    def filter_step(q, carry):
        at = pl.multiple_of(q * 2 * HALF, 2 * HALF)
        total = [None, None]
        for r in range(2):
            for first, ref in ((0, even_ref), (1, odd_ref)):
                ref[r, 0:edge, :] = halo_ref[r, pl.ds(at + first, edge, stride=2), :]
                ref[r, edge : edge + half, :] = own_ref[q, r, pl.ds(first, half, stride=2), :]
                ref[r, edge + half : count, :] = halo_ref[r, pl.ds(at + HALF + first, edge, stride=2), :]
            pair_ref[r] = odd_ref[r] + even_ref[r, 1 : count + 1, :]
            evens = jnp.zeros((half + 8, 128), F32)
            odds = jnp.zeros((half, 128), F32)
            pairs = jnp.zeros((half, 128), F32)
            for u in range(HALF + 1):
                evens = evens + taps_ref[q, 2 * u : 2 * u + 1, :] * even_ref[r, u : u + half + 8, :]
            part_ref[r] = evens
            for u in range(HALF):
                odds = odds + taps_ref[q, 2 * u + 1 : 2 * u + 2, :] * odd_ref[r, u : u + half, :]
            for u in range(HALF + 1):
                pairs = pairs + both_ref[q, u : u + 1, :] * pair_ref[r, u : u + half, :]
            result = (evens[:half] + odds, pairs - (part_ref[r, 1 : half + 1, :] + odds))
            for n in range(2):
                for rows, values in placed(result[n], n):
                    filtered_ref[q, r, rows, :] = values
                square = result[n] * result[n]
                total[n] = square if r == 0 else total[n] + square
        for n in range(2):
            for rows, values in placed(total[n], n):
                power_ref[q + 1, rows, :] = power_ref[q, rows, :] + values
        return carry

    lax.fori_loop(0, RADIX, filter_step, 0)

    reach = SMOOTH // RADIX
    lane = lax.broadcasted_iota(jnp.int32, (1, 128), 1)

    def shifted(values, by):
        inside = jnp.where((lane + by >= 0) & (lane + by < 128), 1.0, 0.0)
        return pltpu.roll(values, (-by) % 128, 1) * inside

    whole = power_ref[RADIX]
    base = whole
    for by in range(1, reach):
        base = base + (shifted(whole, by) + shifted(whole, -by))
    base_ref[...] = base

    bins = lax.broadcasted_iota(jnp.int32, (RADIX, 128), 1) * RADIX + lax.broadcasted_iota(
        jnp.int32, (RADIX, 128), 0
    )
    place = lax.broadcasted_iota(jnp.int32, offset_ref.shape, 1)
    offset = jnp.sum(jnp.where(place == lax.axis_index(AXES), offset_ref[...], 0), axis=1, keepdims=True)
    phases = lax.rem(bins * offset, length).astype(F32) * (2.0 * np.pi / length)
    cosine, sine = jnp.cos(phases), jnp.sin(phases)
    pitch = 2 * RADIX + 1
    for q in range(RADIX):
        window = (
            base_ref[...]
            + shifted(power_ref[RADIX] - power_ref[q], -reach)
            + shifted(power_ref[q + 1], reach)
        )
        scale = lax.rsqrt(window * small_ref[2 * RADIX + q : 2 * RADIX + q + 1, 0:128] + EPSILON)
        fr, fi = filtered_ref[q, 0], filtered_ref[q, 1]
        c, s = cosine[q : q + 1, :], sine[q : q + 1, :]
        wr = (fr * c + fi * s) * scale
        wi = (fi * c - fr * s) * scale
        rows_ref[pl.ds(q, 128, stride=pitch), :] = wr.T
        rows_ref[pl.ds(RADIX + q, 128, stride=pitch), :] = wi.T
    for m in range(128):
        rows = rows_ref[m * pitch : m * pitch + 2 * RADIX, :]
        out_ref[2 * RADIX * m : 2 * RADIX * (m + 1), :] = rows.astype(BF16)


def pair_kernel(slots, mine, pairs_hbm, band_ref, basis_ref, *refs):
    if mine:
        before_ref = None
    else:
        before_ref, refs = refs[0], refs[1:]
    out_ref, left_ref, right_ref, cross0_ref, cross1_ref, pairs_ref, sem_ref = refs
    copy = pltpu.make_async_copy(pairs_hbm, pairs_ref, sem_ref.at[0])
    copy.start()
    blocks = band_ref.shape[0]
    groups = band_ref.shape[1] // (2 * RADIX)
    deep = basis_ref.shape[1]
    half = lax.rem(lax.axis_index("shard"), 2)
    part = half if mine else 1 - half
    kept = slots // 2
    step = cross0_ref.shape[1] // (128 * kept)

    def spread(i, carry):
        for n in range(8):
            values = band_ref[8 * i + n].astype(F32)
            left_ref[8 * i + n] = values
            right_ref[8 * i + n] = pltpu.roll(values, 64, 1)
        return carry

    lax.fori_loop(0, blocks // 8, spread, 0)
    copy.wait()

    def products(i, cross_ref):
        for n in range(step * kept):
            slot = (step * i + n // kept) * slots + half * kept + n % kept
            a, b = pairs_ref[0, slot], pairs_ref[1, slot]
            for m in range(groups):
                lo, mid, hi = 2 * RADIX * m, 2 * RADIX * m + RADIX, 2 * RADIX * (m + 1)
                lr, li = left_ref[a, lo:mid, :], left_ref[a, mid:hi, :]
                rr, ri = right_ref[b, lo:mid, :], right_ref[b, mid:hi, :]
                cross_ref[lo:mid, 128 * n : 128 * n + 128] = (lr * rr + li * ri).astype(BF16)
                cross_ref[mid:hi, 128 * n : 128 * n + 128] = (li * rr - lr * ri).astype(BF16)

    def project(i, cross_ref):
        result = jnp.dot(basis_ref[part], cross_ref[...], preferred_element_type=F32)
        for u in range(step):
            lanes = [128 * (kept * u + j) for j in range(kept)]
            stacked = jnp.concatenate([result[:, at : at + 128] for at in lanes], axis=0)
            if mine:
                out_ref[step * i + u] = stacked
            else:
                out_ref[step * i + u] = (stacked + before_ref[step * i + u]).astype(BF16)

    last = blocks // step - 1
    products(0, cross0_ref)

    def owners(i, carry):
        products(2 * i + 1, cross1_ref)
        project(2 * i, cross0_ref)
        products(jnp.minimum(2 * i + 2, last), cross0_ref)
        project(2 * i + 1, cross1_ref)
        return carry

    lax.fori_loop(0, blocks // (2 * step), owners, 0)


def lag_kernel(slots, scale, valid_ref, parts_ref, table_ref, out_ref, wide_ref, stage_ref, sem_ref):
    bands = parts_ref.shape[0] // 2
    kept = slots // 2
    deep = parts_ref.shape[1] // kept

    def gather(i, carry):
        for n in range(4):
            b = 4 * i + n
            at = pl.multiple_of(b * deep, 8)
            for half in range(2):
                values = parts_ref[2 * b + half].astype(F32)
                for j in range(kept):
                    lane = 128 * (half * kept + j)
                    wide_ref[pl.ds(at, deep), lane : lane + 128] = values[deep * j : deep * (j + 1)]
        return carry

    lax.fori_loop(0, bands // 4, gather, 0)
    copies = []
    for first in range(0, slots, 2):
        columns = wide_ref[:, 128 * first : 128 * first + 256].astype(BF16)
        for n in range(NLAG // 128):
            result = jnp.dot(table_ref[128 * n : 128 * n + 128, :], columns, preferred_element_type=F32)
            for j in range(2):
                weight = valid_ref[:, first + j : first + j + 1].astype(F32) * scale
                turned = result[:, 128 * j : 128 * j + 128].T * weight
                half = turned.shape[0] // 2
                at = (first + j) * (NLAG // 128) + n
                for high in range(2):
                    for parity in range(2):
                        row = half * high + half // 2 * parity
                        rows = turned[row : row + half // 2]
                        stage_ref[at, pl.ds(half * high + parity, half // 2, stride=2), :] = rows
                lanes = pl.ds(128 * n, 128)
                copy = pltpu.make_async_copy(stage_ref.at[at], out_ref.at[first + j, :, lanes], sem_ref.at[at])
                copy.start()
                copies.append(copy)
    for copy in copies:
        copy.wait()


def vmem():
    return pl.BlockSpec(memory_space=pltpu.VMEM)


def params():
    return pltpu.CompilerParams(vmem_limit_bytes=VMEM_BYTES)


def near(array):
    return pltpu.with_memory_space_constraint(array, pltpu.VMEM)


def distant(array):
    return pltpu.with_memory_space_constraint(array, pltpu.HBM)


def far():
    return pl.BlockSpec(memory_space=pltpu.HBM)


def body(samples, fan_taps, pair_blocks, pair_valid, coil_offsets):
    width = samples.shape[0]
    length = samples.shape[2]
    bin_count = length // 2
    devices = lax.axis_size("group") * lax.axis_size("shard")
    shards = lax.axis_size("shard")
    bins_device = bin_count // devices
    slots = pair_valid.shape[0]
    inner = length // RADIX
    lanes = bin_count // RADIX
    chunk = 64

    twiddle, table = forward_constants(length)
    basis, lag_table = band_constants(devices // 2, 2 * bins_device, length)
    project = projection_constants(basis, 2)
    deep = project.shape[1]
    bins_k = np.arange(bin_count)
    counts = np.minimum(bins_k + SMOOTH, bin_count - 1) - np.maximum(bins_k - SMOOTH, 0) + 1
    small = np.zeros((3 * RADIX, inner), np.float32)
    small[: 2 * RADIX] = twiddle
    small[2 * RADIX :, :lanes] = (1.0 / counts).reshape(lanes, RADIX).T

    x = samples.reshape(width, length)
    ends = devices - 1
    left = lax.ppermute(x[width - HALF :], AXES, [(i, i + 1) for i in range(ends)])
    right = lax.ppermute(x[:HALF], AXES, [(i + 1, i) for i in range(ends)])

    own, taps, both, small, table = pl.pallas_call(
        own_kernel,
        out_shape=(
            pltpu.VMEM((RADIX, 2, width, lanes), F32),
            pltpu.VMEM((RADIX, 2 * HALF + 1, lanes), F32),
            pltpu.VMEM((RADIX, HALF + 1, lanes), F32),
            pltpu.VMEM(small.shape, F32),
            pltpu.VMEM(table.shape, BF16),
        ),
        in_specs=[far()] * 4,
        out_specs=(vmem(),) * 5,
        scratch_shapes=[
            pltpu.VMEM((width, length), BF16),
            pltpu.VMEM(fan_taps.shape, F32),
            pltpu.VMEM((RADIX * chunk, 4 * inner), BF16),
            pltpu.VMEM((RADIX * chunk, 4 * inner), BF16),
            pltpu.VMEM((bin_count + lanes, 128), F32),
            pltpu.SemaphoreType.DMA((width // chunk + 3,)),
        ],
        compiler_params=params(),
        name="own_spectra",
    )(distant(x), distant(fan_taps), distant(jnp.asarray(small)), distant(jnp.asarray(table)))

    rows = pl.pallas_call(
        functools.partial(whiten_kernel, length),
        out_shape=pltpu.VMEM((2 * bin_count, width), BF16),
        in_specs=[vmem()] * 8,
        out_specs=vmem(),
        scratch_shapes=[
            pltpu.VMEM((2 * HALF, length), BF16),
            pltpu.VMEM((RADIX * 2 * HALF, 4 * inner), BF16),
            pltpu.VMEM((2, RADIX * 2 * HALF, lanes), F32),
            pltpu.VMEM((2, width // 2 + HALF + 8, lanes), F32),
            pltpu.VMEM((2, width // 2 + HALF, lanes), F32),
            pltpu.VMEM((2, width // 2 + HALF, lanes), F32),
            pltpu.VMEM((2, width // 2 + 8, lanes), F32),
            pltpu.VMEM((RADIX, 2, width, lanes), F32),
            pltpu.VMEM((RADIX + 1, width, lanes), F32),
            pltpu.VMEM((width, lanes), F32),
            pltpu.VMEM((2 * bin_count + lanes, width), F32),
        ],
        compiler_params=params(),
        name="whiten",
    )(near(coil_offsets.reshape(1, -1)), near(own), near(left), near(right), near(small), near(table), near(taps), near(both))

    band = lax.all_to_all(
        rows.reshape(devices, 2 * bins_device, width), AXES, split_axis=0, concat_axis=0, tiled=True
    )
    other = lax.ppermute(band, "shard", [(i, i ^ 1) for i in range(shards)])

    pairs = distant(pair_blocks.T)
    project = near(jnp.asarray(project))
    sums = (devices, slots // 2 * deep, width)

    def products(mine, part, before):
        return pl.pallas_call(
            functools.partial(pair_kernel, slots, mine),
            out_shape=pltpu.VMEM(sums, F32 if mine else BF16),
            in_specs=[far()] + [vmem()] * (2 + len(before)),
            out_specs=vmem(),
            scratch_shapes=[
                pltpu.VMEM((devices, 2 * bins_device, width), F32),
                pltpu.VMEM((devices, 2 * bins_device, width), F32),
                pltpu.VMEM((2 * bins_device, 4 * slots * width), BF16),
                pltpu.VMEM((2 * bins_device, 4 * slots * width), BF16),
                pltpu.SMEM(pairs.shape, jnp.int32),
                pltpu.SemaphoreType.DMA((1,)),
            ],
            compiler_params=params(),
            name="pairs_own_part" if mine else "pairs_other_part",
        )(pairs, near(part), project, *before)

    first = products(True, band, ())
    parts = products(False, other, (near(first),))

    owned = lax.all_to_all(parts, AXES, split_axis=0, concat_axis=0, tiled=True)

    return pl.pallas_call(
        functools.partial(lag_kernel, slots, float(1.0 / np.sqrt(bin_count * samples.shape[1]))),
        out_shape=jax.ShapeDtypeStruct((slots, width, NLAG), F32),
        in_specs=[vmem()] * 3,
        out_specs=pl.BlockSpec(memory_space=pl.ANY),
        scratch_shapes=[
            pltpu.VMEM((devices // 2 * deep, slots * width), F32),
            pltpu.VMEM((slots * NLAG // 128, width, 128), F32),
            pltpu.SemaphoreType.DMA((slots * NLAG // 128,)),
        ],
        compiler_params=params(),
        name="lags",
    )(near(pair_valid.reshape(1, -1)), near(owned), near(jnp.asarray(lag_table)))


def solution(mesh):
    return jax.shard_map(
        body,
        mesh=mesh,
        in_specs=(P(AXES, None, None), P(), P(), P(AXES), P()),
        out_specs=P(AXES, None, None),
        check_vma=False,
    )
```

```python
import functools

import jax
import jax.numpy as jnp
import ml_dtypes
import numpy as np
from jax import lax
from jax.experimental import pallas as pl
from jax.experimental.pallas import tpu as pltpu
from jax.sharding import PartitionSpec as P

AXES = ("group", "shard")
HALF = 16
SMOOTH = 64
NLAG = 512
EPSILON = 1e-05
RADIX = 16
VMEM_BYTES = 32 * 1024 * 1024
F32 = jnp.float32
BF16 = jnp.bfloat16


def as_bf16(table):
    return table.astype(ml_dtypes.bfloat16)


def forward_constants(length):
    inner = length // RADIX
    n1 = np.arange(inner)
    turns = (np.arange(RADIX)[:, None] * n1[None, :]) * (2.0 * np.pi / length)
    twiddle = np.concatenate([np.cos(turns), np.sin(turns)]).astype(np.float32)
    angle = np.mod(n1[:, None] * np.arange(inner // 2)[None, :], inner) * (2.0 * np.pi / inner)
    cosine, sine = np.cos(angle), np.sin(angle)
    table = np.concatenate(
        [np.concatenate([cosine, -sine], axis=1), np.concatenate([sine, cosine], axis=1)]
    ) / np.sqrt(length)
    high = as_bf16(table)
    low = as_bf16(table - high.astype(np.float64))
    return twiddle, np.concatenate([high, low])


def band_constants(bands, width, length):
    place = np.arange(width)
    diagonal = ((width - 1 - 2 * place) / 2.0) ** 2 * np.cos(np.pi * NLAG / length)
    beside = place[1:] * (width - place[1:]) / 2.0
    matrix = np.diag(diagonal) + np.diag(beside, 1) + np.diag(beside, -1)
    vectors = np.linalg.eigh(matrix)[1][:, ::-1]
    upper = vectors[(width + 1) // 2 :]
    vectors = vectors * np.sign(upper[np.argmax(np.abs(upper), axis=0), np.arange(width)])[None, :]
    lags = np.arange(NLAG) - NLAG // 2
    waves = np.exp(2j * np.pi * np.outer(place - (width - 1) / 2.0, lags) / length)
    rank = width
    for fewer in range(4, width, 4):
        basis = vectors[:, :fewer]
        error = waves - basis @ (basis.T @ waves)
        if np.sqrt(np.mean(np.abs(error) ** 2)) < 1e-7:
            rank = fewer
            break
    basis = vectors[:, :rank]
    partner = basis.T @ waves
    centres = width * np.arange(bands) + (width - 1) / 2.0
    carrier = np.exp(2j * np.pi * np.outer(centres, lags) / length)
    whole = carrier[:, None, :] * partner[None, :, :]
    table = np.concatenate([whole.real, -whole.imag], axis=1).reshape(bands * 2 * rank, NLAG)
    return basis, as_bf16(np.ascontiguousarray(table.T))


def projection_constants(basis, halves):
    width, rank = basis.shape
    groups = width // halves // RADIX
    rows = np.zeros((halves, 2, rank, groups, 2, RADIX))
    split = basis.T.reshape(rank, halves, groups, RADIX).transpose(1, 0, 2, 3)
    rows[:, 0, :, :, 0, :] = split
    rows[:, 1, :, :, 1, :] = split
    return as_bf16(rows.reshape(halves, 2 * rank, 2 * groups * RADIX))


def real_dft(values):
    count = len(values)
    if count == 1:
        return [(values[0], None)]
    even, odd = real_dft(values[0::2]), real_dft(values[1::2])
    out = [None] * (count // 2 + 1)
    out[0] = (even[0][0] + odd[0][0], None)
    out[count // 2] = (even[0][0] - odd[0][0], None)
    for k in range(1, count // 4 + 1):
        er, ei = even[k]
        orr, oi = odd[k]
        if 4 * k == count:
            out[k] = (er, -orr)
            continue
        c, s = float(np.cos(2 * np.pi * k / count)), float(np.sin(2 * np.pi * k / count))
        tr = orr * c + oi * s
        ti = oi * c - orr * s
        out[k] = (er + tr, ei + ti)
        out[count // 2 - k] = (er - tr, ti - ei)
    return out


def transform_rows(x_ref, first, rows, twiddle_ref, z_ref):
    inner = x_ref.shape[1] // RADIX
    for at in range(0, rows, 16):
        for lane in range(0, inner, 128):
            values = [
                x_ref[first + at : first + at + 16, inner * j + lane : inner * j + lane + 128].astype(F32)
                for j in range(RADIX)
            ]
            bins = real_dft(values)
            for q in range(RADIX):
                yr, yi = bins[q] if q <= RADIX // 2 else bins[RADIX - q]
                if q > RADIX // 2:
                    yi = -yi
                if q == 0:
                    zr, zi = yr, jnp.zeros_like(yr)
                else:
                    c = twiddle_ref[q : q + 1, lane : lane + 128]
                    s = twiddle_ref[RADIX + q : RADIX + q + 1, lane : lane + 128]
                    if yi is None:
                        zr, zi = yr * c, -yr * s
                    else:
                        zr, zi = yr * c + yi * s, yi * c - yr * s
                where = slice(q * rows + at, q * rows + at + 16)
                for part, z in ((0, zr), (1, zi)):
                    high = z.astype(BF16)
                    z_ref[where, part * inner + lane : part * inner + lane + 128] = high
                    low = (z - high.astype(F32)).astype(BF16)
                    start = (2 + part) * inner + lane
                    z_ref[where, start : start + 128] = low


def transform_inner(z, table_ref):
    depth = z.shape[1] // 2
    high, low = table_ref[0:depth, :], table_ref[depth:, :]
    out = jnp.dot(z[:, :depth], high, preferred_element_type=F32)
    out = out + jnp.dot(z[:, depth:], high, preferred_element_type=F32)
    return out + jnp.dot(z[:, :depth], low, preferred_element_type=F32)


def own_kernel(
    x_hbm, taps_hbm, small_hbm, table_hbm, out_ref, split_ref, both_ref, small_ref, table_ref,
    x_ref, taps_ref, z0_ref, z1_ref, turned_ref, sem_ref,
):
    chunk = z0_ref.shape[0] // RADIX
    steps = x_ref.shape[0] // chunk
    slots = (z0_ref, z1_ref)
    copies = [pltpu.make_async_copy(taps_hbm, taps_ref, sem_ref.at[0])]
    copies.append(pltpu.make_async_copy(small_hbm, small_ref, sem_ref.at[1]))
    for i in range(steps):
        rows = pl.ds(i * chunk, chunk)
        copies.append(pltpu.make_async_copy(x_hbm.at[rows], x_ref.at[rows], sem_ref.at[3 + i]))
    table_copy = pltpu.make_async_copy(table_hbm, table_ref, sem_ref.at[2])
    for i, copy in enumerate(copies):
        copy.start()
        if i == 2:
            table_copy.start()

    copies[0].wait()
    count = taps_ref.shape[0]
    pitch = RADIX + 1
    for at in range(0, taps_ref.shape[1], 128):
        turned = taps_ref[:, at : at + 128].T
        for n in range(128 // RADIX):
            row = (at // RADIX + n) * pitch
            turned_ref[row : row + RADIX, 0:count] = turned[RADIX * n : RADIX * (n + 1)]
    for q in range(RADIX):
        taps = turned_ref[pl.ds(q, 128, stride=pitch), 0:count].T
        split_ref[q, 0:count, :] = taps
        even = split_ref[q, pl.ds(0, HALF, stride=2), :]
        odd = split_ref[q, pl.ds(1, HALF, stride=2), :]
        both_ref[q, 0:HALF, :] = even + odd
        both_ref[q, HALF : HALF + 1, :] = taps[count - 1 :]

    copies[1].wait()

    copies[2].wait()
    transform_rows(x_ref, 0, chunk, small_ref, z0_ref)
    table_copy.wait()
    for i in range(steps):
        if i + 1 < steps:
            copies[3 + i].wait()
            transform_rows(x_ref, (i + 1) * chunk, chunk, small_ref, slots[(i + 1) % 2])
        values = transform_inner(slots[i % 2][...], table_ref)
        for q in range(RADIX):
            out_ref[q, 0, i * chunk : (i + 1) * chunk, :] = values[q * chunk : (q + 1) * chunk, :128]
            out_ref[q, 1, i * chunk : (i + 1) * chunk, :] = values[q * chunk : (q + 1) * chunk, 128:]


def whiten_kernel(
    length, offset_ref, own_ref, next_ref, small_ref, table_ref, taps_ref, both_ref, out_ref,
    z_ref, halo_ref, even_ref, odd_ref, pair_ref, part_ref, filtered_ref, power_ref, base_ref, rows_ref,
):
    width = own_ref.shape[2]
    device = lax.axis_index(AXES)
    devices = offset_ref.shape[1]
    inside = jnp.where(device == devices - 1, 0.0, 1.0)
    transform_rows(next_ref, 0, 2 * HALF, small_ref, z_ref)
    values = transform_inner(z_ref[...], table_ref)
    halo_ref[0] = values[:, :128]
    halo_ref[1] = values[:, 128:]

    power_ref[0] = jnp.zeros(power_ref.shape[1:], F32)

    half = width // 2
    edge = HALF // 2
    main = half - edge
    even_tail, odd_tail = main + 3 * edge, main + 2 * edge
    zeros = jnp.zeros((edge, 128), F32)

    def placed(values, parity):
        quarter = half // 2
        for high in range(2):
            first = half * high + quarter * parity
            yield slice(first, first + quarter), values[quarter * high : quarter * (high + 1)]

    def filter_step(q, carry):
        at = pl.multiple_of(q * 2 * HALF, 2 * HALF)
        total = [None, None]
        for r in range(2):
            for first, ref, tail in ((0, even_ref, even_tail), (1, odd_ref, odd_tail)):
                last = own_ref[q, r, pl.ds(2 * main + first, edge, stride=2), :]
                after = halo_ref[r, pl.ds(at + first, 2 * edge, stride=2), :]
                ref[r, 0:main, :] = own_ref[q, r, pl.ds(first, main, stride=2), :]
                ref[r, main : main + edge, :] = last
                ref[r, main + edge : main + 2 * edge, :] = after[:edge] * inside
                ref[r, tail : tail + edge, :] = last * inside
                ref[r, tail + edge : tail + 3 * edge, :] = after
            even_ref[r, main + 2 * edge : even_tail, :] = zeros
            even_ref[r, even_tail + 3 * edge :, :] = zeros
            pair_ref[r, 0:odd_tail, :] = odd_ref[r, 0:odd_tail, :] + even_ref[r, 1 : odd_tail + 1, :]
            pair_ref[r, odd_tail:, :] = odd_ref[r, odd_tail:, :] + even_ref[r, even_tail + 1 : even_tail + 3 * edge + 1, :]
            result = ([], [])
            for rows, even, odd in ((main, 0, 0), (edge, even_tail, odd_tail)):
                evens = jnp.zeros((rows + 8, 128), F32)
                odds = jnp.zeros((rows, 128), F32)
                pairs = jnp.zeros((rows, 128), F32)
                for u in range(HALF + 1):
                    evens = evens + taps_ref[q, 2 * u : 2 * u + 1, :] * even_ref[r, even + u : even + u + rows + 8, :]
                part_ref[r, 0 : rows + 8, :] = evens
                for u in range(HALF):
                    odds = odds + taps_ref[q, 2 * u + 1 : 2 * u + 2, :] * odd_ref[r, odd + u : odd + u + rows, :]
                for u in range(HALF + 1):
                    pairs = pairs + both_ref[q, u : u + 1, :] * pair_ref[r, odd + u : odd + u + rows, :]
                result[0].append(evens[:rows] + odds)
                result[1].append(pairs - (part_ref[r, 1 : rows + 1, :] + odds))
            result = [jnp.concatenate(parts, axis=0) for parts in result]
            for n in range(2):
                for rows, values in placed(result[n], n):
                    filtered_ref[q, r, rows, :] = values
                square = result[n] * result[n]
                total[n] = square if r == 0 else total[n] + square
        for n in range(2):
            for rows, values in placed(total[n], n):
                power_ref[q + 1, rows, :] = power_ref[q, rows, :] + values
        return carry

    lax.fori_loop(0, RADIX, filter_step, 0)

    reach = SMOOTH // RADIX
    lane = lax.broadcasted_iota(jnp.int32, (1, 128), 1)

    def shifted(values, by):
        inside = jnp.where((lane + by >= 0) & (lane + by < 128), 1.0, 0.0)
        return pltpu.roll(values, (-by) % 128, 1) * inside

    whole = power_ref[RADIX]
    base = whole
    for by in range(1, reach):
        base = base + (shifted(whole, by) + shifted(whole, -by))
    base_ref[...] = base

    bins = lax.broadcasted_iota(jnp.int32, (RADIX, 128), 1) * RADIX + lax.broadcasted_iota(
        jnp.int32, (RADIX, 128), 0
    )
    place = lax.broadcasted_iota(jnp.int32, offset_ref.shape, 1)
    turns = []
    for block in (device, lax.rem(device + 1, devices)):
        offset = jnp.sum(jnp.where(place == block, offset_ref[...], 0), axis=1, keepdims=True)
        phases = lax.rem(bins * offset, length).astype(F32) * (2.0 * np.pi / length)
        turns.append((jnp.cos(phases), jnp.sin(phases)))

    def by_row(part, q):
        mine, its = turns[0][part][q : q + 1, :], turns[1][part][q : q + 1, :]
        sizes = (half + half // 2 - edge, edge, half // 2 - edge, edge)
        return jnp.concatenate(
            [jnp.broadcast_to(its if n % 2 else mine, (size, 128)) for n, size in enumerate(sizes)], axis=0
        )

    pitch = 2 * RADIX + 1
    for q in range(RADIX):
        window = (
            base_ref[...]
            + shifted(power_ref[RADIX] - power_ref[q], -reach)
            + shifted(power_ref[q + 1], reach)
        )
        scale = lax.rsqrt(window * small_ref[2 * RADIX + q : 2 * RADIX + q + 1, 0:128] + EPSILON)
        fr, fi = filtered_ref[q, 0], filtered_ref[q, 1]
        c, s = by_row(0, q), by_row(1, q)
        wr = (fr * c + fi * s) * scale
        wi = (fi * c - fr * s) * scale
        rows_ref[pl.ds(q, 128, stride=pitch), :] = wr.T
        rows_ref[pl.ds(RADIX + q, 128, stride=pitch), :] = wi.T
    for m in range(128):
        rows = rows_ref[m * pitch : m * pitch + 2 * RADIX, :]
        out_ref[2 * RADIX * m : 2 * RADIX * (m + 1), :] = rows.astype(BF16)


def pair_kernel(slots, mine, pairs_hbm, band_ref, basis_ref, *refs):
    if mine:
        before_ref = None
    else:
        before_ref, refs = refs[0], refs[1:]
    out_ref, left_ref, right_ref, cross0_ref, cross1_ref, pairs_ref, sem_ref = refs
    copy = pltpu.make_async_copy(pairs_hbm, pairs_ref, sem_ref.at[0])
    copy.start()
    blocks = band_ref.shape[0]
    groups = band_ref.shape[1] // (2 * RADIX)
    deep = basis_ref.shape[1]
    half = lax.rem(lax.axis_index("shard"), 2)
    part = half if mine else 1 - half
    kept = slots // 2
    step = cross0_ref.shape[1] // (128 * kept)

    lane = lax.broadcasted_iota(jnp.int32, band_ref.shape[1:], 1)
    from_before = (lane >= 64) & (lax.rem(lane, 32) >= 32 - HALF // 2)

    def spread(i, carry):
        before = band_ref[lax.rem(8 * i + blocks - 1, blocks)].astype(F32)
        for n in range(8):
            values = band_ref[8 * i + n].astype(F32)
            whole = jnp.where(from_before, before, values)
            left_ref[8 * i + n] = whole
            right_ref[8 * i + n] = pltpu.roll(whole, 64, 1)
            before = values
        return carry

    lax.fori_loop(0, blocks // 8, spread, 0)
    copy.wait()

    def products(i, cross_ref):
        for n in range(step * kept):
            slot = (step * i + n // kept) * slots + half * kept + n % kept
            a, b = pairs_ref[0, slot], pairs_ref[1, slot]
            for m in range(groups):
                lo, mid, hi = 2 * RADIX * m, 2 * RADIX * m + RADIX, 2 * RADIX * (m + 1)
                lr, li = left_ref[a, lo:mid, :], left_ref[a, mid:hi, :]
                rr, ri = right_ref[b, lo:mid, :], right_ref[b, mid:hi, :]
                cross_ref[lo:mid, 128 * n : 128 * n + 128] = (lr * rr + li * ri).astype(BF16)
                cross_ref[mid:hi, 128 * n : 128 * n + 128] = (li * rr - lr * ri).astype(BF16)

    def project(i, cross_ref):
        result = jnp.dot(basis_ref[part], cross_ref[...], preferred_element_type=F32)
        for u in range(step):
            lanes = [128 * (kept * u + j) for j in range(kept)]
            stacked = jnp.concatenate([result[:, at : at + 128] for at in lanes], axis=0)
            if mine:
                out_ref[step * i + u] = stacked
            else:
                out_ref[step * i + u] = (stacked + before_ref[step * i + u]).astype(BF16)

    last = blocks // step - 1
    products(0, cross0_ref)

    def owners(i, carry):
        products(2 * i + 1, cross1_ref)
        project(2 * i, cross0_ref)
        products(jnp.minimum(2 * i + 2, last), cross0_ref)
        project(2 * i + 1, cross1_ref)
        return carry

    lax.fori_loop(0, blocks // (2 * step), owners, 0)


def lag_kernel(slots, scale, valid_ref, parts_ref, table_ref, out_ref, wide_ref, stage_ref, sem_ref):
    bands = parts_ref.shape[0] // 2
    kept = slots // 2
    deep = parts_ref.shape[1] // kept

    def gather(i, carry):
        for n in range(4):
            b = 4 * i + n
            at = pl.multiple_of(b * deep, 8)
            for half in range(2):
                values = parts_ref[2 * b + half].astype(F32)
                for j in range(kept):
                    lane = 128 * (half * kept + j)
                    wide_ref[pl.ds(at, deep), lane : lane + 128] = values[deep * j : deep * (j + 1)]
        return carry

    lax.fori_loop(0, bands // 4, gather, 0)
    copies = []
    for first in range(0, slots, 2):
        columns = wide_ref[:, 128 * first : 128 * first + 256].astype(BF16)
        for n in range(NLAG // 128):
            result = jnp.dot(table_ref[128 * n : 128 * n + 128, :], columns, preferred_element_type=F32)
            for j in range(2):
                weight = valid_ref[:, first + j : first + j + 1].astype(F32) * scale
                turned = result[:, 128 * j : 128 * j + 128].T * weight
                half = turned.shape[0] // 2
                at = (first + j) * (NLAG // 128) + n
                quarter = half // 2
                for parity in range(2):
                    pieces = (
                        (quarter * parity, HALF, quarter),
                        (half + quarter * parity, half + HALF, quarter - HALF // 2),
                        (half + quarter * (parity + 1) - HALF // 2, 0, HALF // 2),
                    )
                    for row, channel, count in pieces:
                        stage_ref[at, pl.ds(channel + parity, count, stride=2), :] = turned[row : row + count]
                lanes = pl.ds(128 * n, 128)
                copy = pltpu.make_async_copy(stage_ref.at[at], out_ref.at[first + j, :, lanes], sem_ref.at[at])
                copy.start()
                copies.append(copy)
    for copy in copies:
        copy.wait()


def vmem():
    return pl.BlockSpec(memory_space=pltpu.VMEM)


def params():
    return pltpu.CompilerParams(vmem_limit_bytes=VMEM_BYTES)


def near(array):
    return pltpu.with_memory_space_constraint(array, pltpu.VMEM)


def distant(array):
    return pltpu.with_memory_space_constraint(array, pltpu.HBM)


def far():
    return pl.BlockSpec(memory_space=pltpu.HBM)


def body(samples, fan_taps, pair_blocks, pair_valid, coil_offsets):
    width = samples.shape[0]
    length = samples.shape[2]
    bin_count = length // 2
    devices = lax.axis_size("group") * lax.axis_size("shard")
    shards = lax.axis_size("shard")
    bins_device = bin_count // devices
    slots = pair_valid.shape[0]
    inner = length // RADIX
    lanes = bin_count // RADIX
    chunk = 64

    twiddle, table = forward_constants(length)
    basis, lag_table = band_constants(devices // 2, 2 * bins_device, length)
    project = projection_constants(basis, 2)
    deep = project.shape[1]
    bins_k = np.arange(bin_count)
    counts = np.minimum(bins_k + SMOOTH, bin_count - 1) - np.maximum(bins_k - SMOOTH, 0) + 1
    small = np.zeros((3 * RADIX, inner), np.float32)
    small[: 2 * RADIX] = twiddle
    small[2 * RADIX :, :lanes] = (1.0 / counts).reshape(lanes, RADIX).T

    x = samples.reshape(width, length)
    after = lax.ppermute(x[: 2 * HALF], AXES, [((i + 1) % devices, i) for i in range(devices)])

    own, taps, both, small, table = pl.pallas_call(
        own_kernel,
        out_shape=(
            pltpu.VMEM((RADIX, 2, width, lanes), F32),
            pltpu.VMEM((RADIX, 2 * HALF + 1, lanes), F32),
            pltpu.VMEM((RADIX, HALF + 1, lanes), F32),
            pltpu.VMEM(small.shape, F32),
            pltpu.VMEM(table.shape, BF16),
        ),
        in_specs=[far()] * 4,
        out_specs=(vmem(),) * 5,
        scratch_shapes=[
            pltpu.VMEM((width, length), BF16),
            pltpu.VMEM(fan_taps.shape, F32),
            pltpu.VMEM((RADIX * chunk, 4 * inner), BF16),
            pltpu.VMEM((RADIX * chunk, 4 * inner), BF16),
            pltpu.VMEM((bin_count + lanes, 128), F32),
            pltpu.SemaphoreType.DMA((width // chunk + 3,)),
        ],
        compiler_params=params(),
        name="own_spectra",
    )(distant(x), distant(fan_taps), distant(jnp.asarray(small)), distant(jnp.asarray(table)))

    rows = pl.pallas_call(
        functools.partial(whiten_kernel, length),
        out_shape=pltpu.VMEM((2 * bin_count, width), BF16),
        in_specs=[vmem()] * 7,
        out_specs=vmem(),
        scratch_shapes=[
            pltpu.VMEM((RADIX * 2 * HALF, 4 * inner), BF16),
            pltpu.VMEM((2, RADIX * 2 * HALF, lanes), F32),
            pltpu.VMEM((2, width // 2 + 3 * HALF, lanes), F32),
            pltpu.VMEM((2, width // 2 + 2 * HALF, lanes), F32),
            pltpu.VMEM((2, width // 2 + 2 * HALF, lanes), F32),
            pltpu.VMEM((2, width // 2 + 8, lanes), F32),
            pltpu.VMEM((RADIX, 2, width, lanes), F32),
            pltpu.VMEM((RADIX + 1, width, lanes), F32),
            pltpu.VMEM((width, lanes), F32),
            pltpu.VMEM((2 * bin_count + lanes, width), F32),
        ],
        compiler_params=params(),
        name="whiten",
    )(near(coil_offsets.reshape(1, -1)), near(own), near(after), near(small), near(table), near(taps), near(both))

    band = lax.all_to_all(
        rows.reshape(devices, 2 * bins_device, width), AXES, split_axis=0, concat_axis=0, tiled=True
    )
    other = lax.ppermute(band, "shard", [(i, i ^ 1) for i in range(shards)])

    pairs = distant(pair_blocks.T)
    project = near(jnp.asarray(project))
    sums = (devices, slots // 2 * deep, width)

    def products(mine, part, before):
        return pl.pallas_call(
            functools.partial(pair_kernel, slots, mine),
            out_shape=pltpu.VMEM(sums, F32 if mine else BF16),
            in_specs=[far()] + [vmem()] * (2 + len(before)),
            out_specs=vmem(),
            scratch_shapes=[
                pltpu.VMEM((devices, 2 * bins_device, width), F32),
                pltpu.VMEM((devices, 2 * bins_device, width), F32),
                pltpu.VMEM((2 * bins_device, 4 * slots * width), BF16),
                pltpu.VMEM((2 * bins_device, 4 * slots * width), BF16),
                pltpu.SMEM(pairs.shape, jnp.int32),
                pltpu.SemaphoreType.DMA((1,)),
            ],
            compiler_params=params(),
            name="pairs_own_part" if mine else "pairs_other_part",
        )(pairs, near(part), project, *before)

    first = products(True, band, ())
    parts = products(False, other, (near(first),))

    owned = lax.all_to_all(parts, AXES, split_axis=0, concat_axis=0, tiled=True)

    return pl.pallas_call(
        functools.partial(lag_kernel, slots, float(1.0 / np.sqrt(bin_count * samples.shape[1]))),
        out_shape=jax.ShapeDtypeStruct((slots, width, NLAG), F32),
        in_specs=[vmem()] * 3,
        out_specs=pl.BlockSpec(memory_space=pl.ANY),
        scratch_shapes=[
            pltpu.VMEM((devices // 2 * deep, slots * width), F32),
            pltpu.VMEM((slots * NLAG // 128, width, 128), F32),
            pltpu.SemaphoreType.DMA((slots * NLAG // 128,)),
        ],
        compiler_params=params(),
        name="lags",
    )(near(pair_valid.reshape(1, -1)), near(owned), near(jnp.asarray(lag_table)))


def solution(mesh):
    return jax.shard_map(
        body,
        mesh=mesh,
        in_specs=(P(AXES, None, None), P(), P(), P(AXES), P()),
        out_specs=P(AXES, None, None),
        check_vma=False,
    )
```

```python
import functools

import jax
import jax.numpy as jnp
import ml_dtypes
import numpy as np
from jax import lax
from jax.experimental import pallas as pl
from jax.experimental.pallas import tpu as pltpu
from jax.sharding import PartitionSpec as P

AXES = ("group", "shard")
HALF = 16
SMOOTH = 64
NLAG = 512
EPSILON = 1e-05
RADIX = 16
VMEM_BYTES = 32 * 1024 * 1024
F32 = jnp.float32
BF16 = jnp.bfloat16


def as_bf16(table):
    return table.astype(ml_dtypes.bfloat16)


def forward_constants(length):
    inner = length // RADIX
    n1 = np.arange(inner)
    turns = (np.arange(RADIX)[:, None] * n1[None, :]) * (2.0 * np.pi / length)
    twiddle = np.concatenate([np.cos(turns), np.sin(turns)]).astype(np.float32)
    angle = np.mod(n1[:, None] * np.arange(inner // 2)[None, :], inner) * (2.0 * np.pi / inner)
    cosine, sine = np.cos(angle), np.sin(angle)
    table = np.concatenate(
        [np.concatenate([cosine, -sine], axis=1), np.concatenate([sine, cosine], axis=1)]
    ) / np.sqrt(length)
    high = as_bf16(table)
    low = as_bf16(table - high.astype(np.float64))
    return twiddle, np.concatenate([high, low])


def band_constants(bands, width, length):
    place = np.arange(width)
    diagonal = ((width - 1 - 2 * place) / 2.0) ** 2 * np.cos(np.pi * NLAG / length)
    beside = place[1:] * (width - place[1:]) / 2.0
    matrix = np.diag(diagonal) + np.diag(beside, 1) + np.diag(beside, -1)
    vectors = np.linalg.eigh(matrix)[1][:, ::-1]
    upper = vectors[(width + 1) // 2 :]
    vectors = vectors * np.sign(upper[np.argmax(np.abs(upper), axis=0), np.arange(width)])[None, :]
    lags = np.arange(NLAG) - NLAG // 2
    waves = np.exp(2j * np.pi * np.outer(place - (width - 1) / 2.0, lags) / length)
    rank = width
    for fewer in range(4, width, 4):
        basis = vectors[:, :fewer]
        error = waves - basis @ (basis.T @ waves)
        if np.sqrt(np.mean(np.abs(error) ** 2)) < 1e-7:
            rank = fewer
            break
    basis = vectors[:, :rank]
    partner = basis.T @ waves
    centres = width * np.arange(bands) + (width - 1) / 2.0
    carrier = np.exp(2j * np.pi * np.outer(centres, lags) / length)
    whole = carrier[:, None, :] * partner[None, :, :]
    table = np.concatenate([whole.real, -whole.imag], axis=1).reshape(bands * 2 * rank, NLAG)
    return basis, as_bf16(np.ascontiguousarray(table.T))


def projection_constants(basis, halves):
    width, rank = basis.shape
    groups = width // halves // RADIX
    rows = np.zeros((halves, 2, rank, groups, 2, RADIX))
    split = basis.T.reshape(rank, halves, groups, RADIX).transpose(1, 0, 2, 3)
    rows[:, 0, :, :, 0, :] = split
    rows[:, 1, :, :, 1, :] = split
    return as_bf16(rows.reshape(halves, 2 * rank, 2 * groups * RADIX))


def real_dft(values):
    count = len(values)
    if count == 1:
        return [(values[0], None)]
    even, odd = real_dft(values[0::2]), real_dft(values[1::2])
    out = [None] * (count // 2 + 1)
    out[0] = (even[0][0] + odd[0][0], None)
    out[count // 2] = (even[0][0] - odd[0][0], None)
    for k in range(1, count // 4 + 1):
        er, ei = even[k]
        orr, oi = odd[k]
        if 4 * k == count:
            out[k] = (er, -orr)
            continue
        c, s = float(np.cos(2 * np.pi * k / count)), float(np.sin(2 * np.pi * k / count))
        tr = orr * c + oi * s
        ti = oi * c - orr * s
        out[k] = (er + tr, ei + ti)
        out[count // 2 - k] = (er - tr, ti - ei)
    return out


def transform_rows(x_ref, first, rows, twiddle_ref, z_ref):
    inner = x_ref.shape[1] // RADIX
    for at in range(0, rows, 16):
        for lane in range(0, inner, 128):
            values = [
                x_ref[first + at : first + at + 16, inner * j + lane : inner * j + lane + 128].astype(F32)
                for j in range(RADIX)
            ]
            bins = real_dft(values)
            for q in range(RADIX):
                yr, yi = bins[q] if q <= RADIX // 2 else bins[RADIX - q]
                if q > RADIX // 2:
                    yi = -yi
                if q == 0:
                    zr, zi = yr, jnp.zeros_like(yr)
                else:
                    c = twiddle_ref[q : q + 1, lane : lane + 128]
                    s = twiddle_ref[RADIX + q : RADIX + q + 1, lane : lane + 128]
                    if yi is None:
                        zr, zi = yr * c, -yr * s
                    else:
                        zr, zi = yr * c + yi * s, yi * c - yr * s
                where = slice(q * rows + at, q * rows + at + 16)
                for part, z in ((0, zr), (1, zi)):
                    high = z.astype(BF16)
                    z_ref[where, part * inner + lane : part * inner + lane + 128] = high
                    low = (z - high.astype(F32)).astype(BF16)
                    start = (2 + part) * inner + lane
                    z_ref[where, start : start + 128] = low


def transform_inner(z, table_ref):
    depth = z.shape[1] // 2
    high, low = table_ref[0:depth, :], table_ref[depth:, :]
    out = jnp.dot(z[:, :depth], high, preferred_element_type=F32)
    out = out + jnp.dot(z[:, depth:], high, preferred_element_type=F32)
    return out + jnp.dot(z[:, :depth], low, preferred_element_type=F32)


def short_filters(taps_ref, both_ref, q, even_ref, odd_ref, pair_ref, part_ref, r, even, odd, rows):
    evens = jnp.zeros((rows + 8, 128), F32)
    odds = jnp.zeros((rows, 128), F32)
    pairs = jnp.zeros((rows, 128), F32)
    for u in range(HALF + 1):
        evens = evens + taps_ref[q, 2 * u : 2 * u + 1, :] * even_ref[r, even + u : even + u + rows + 8, :]
    part_ref[r, 0 : rows + 8, :] = evens
    for u in range(HALF):
        odds = odds + taps_ref[q, 2 * u + 1 : 2 * u + 2, :] * odd_ref[r, odd + u : odd + u + rows, :]
    for u in range(HALF + 1):
        pairs = pairs + both_ref[q, u : u + 1, :] * pair_ref[r, odd + u : odd + u + rows, :]
    return evens[:rows] + odds, pairs - (part_ref[r, 1 : rows + 1, :] + odds)


def own_kernel(
    x_hbm, taps_hbm, small_hbm, table_hbm, out_ref, first_ref, split_ref, both_ref, small_ref, table_ref,
    x_ref, taps_ref, z0_ref, z1_ref, turned_ref, even_ref, odd_ref, pair_ref, part_ref, sem_ref,
):
    chunk = z0_ref.shape[0] // RADIX
    steps = x_ref.shape[0] // chunk
    slots = (z0_ref, z1_ref)
    copies = [pltpu.make_async_copy(taps_hbm, taps_ref, sem_ref.at[0])]
    copies.append(pltpu.make_async_copy(small_hbm, small_ref, sem_ref.at[1]))
    for i in range(steps):
        rows = pl.ds(i * chunk, chunk)
        copies.append(pltpu.make_async_copy(x_hbm.at[rows], x_ref.at[rows], sem_ref.at[3 + i]))
    table_copy = pltpu.make_async_copy(table_hbm, table_ref, sem_ref.at[2])
    for i, copy in enumerate(copies):
        copy.start()
        if i == 2:
            table_copy.start()

    copies[0].wait()
    count = taps_ref.shape[0]
    pitch = RADIX + 1
    for at in range(0, taps_ref.shape[1], 128):
        turned = taps_ref[:, at : at + 128].T
        for n in range(128 // RADIX):
            row = (at // RADIX + n) * pitch
            turned_ref[row : row + RADIX, 0:count] = turned[RADIX * n : RADIX * (n + 1)]
    for q in range(RADIX):
        taps = turned_ref[pl.ds(q, 128, stride=pitch), 0:count].T
        split_ref[q, 0:count, :] = taps
        even = split_ref[q, pl.ds(0, HALF, stride=2), :]
        odd = split_ref[q, pl.ds(1, HALF, stride=2), :]
        both_ref[q, 0:HALF, :] = even + odd
        both_ref[q, HALF : HALF + 1, :] = taps[count - 1 :]

    copies[1].wait()

    copies[2].wait()
    transform_rows(x_ref, 0, chunk, small_ref, z0_ref)
    table_copy.wait()
    for i in range(steps):
        if i + 1 < steps:
            copies[3 + i].wait()
            transform_rows(x_ref, (i + 1) * chunk, chunk, small_ref, slots[(i + 1) % 2])
        values = transform_inner(slots[i % 2][...], table_ref)
        for q in range(RADIX):
            out_ref[q, 0, i * chunk : (i + 1) * chunk, :] = values[q * chunk : (q + 1) * chunk, :128]
            out_ref[q, 1, i * chunk : (i + 1) * chunk, :] = values[q * chunk : (q + 1) * chunk, 128:]

    half = x_ref.shape[0] // 2
    rows = half - HALF
    quarter = half // 2
    even_ref[:, half:, :] = jnp.zeros((2, 8, 128), F32)

    def filter_step(q, carry):
        for r in range(2):
            even_ref[r, 0:half, :] = out_ref[q, r, pl.ds(0, half, stride=2), :]
            odd_ref[r] = out_ref[q, r, pl.ds(1, half, stride=2), :]
            pair_ref[r] = odd_ref[r] + even_ref[r, 1 : half + 1, :]
            result = short_filters(split_ref, both_ref, q, even_ref, odd_ref, pair_ref, part_ref, r, 0, 0, rows)
            for parity in range(2):
                first_ref[q, r, quarter * parity : quarter * (parity + 1), :] = result[parity][:quarter]
                at = half + quarter * parity
                first_ref[q, r, at : at + rows - quarter, :] = result[parity][quarter:]
        return carry

    lax.fori_loop(0, RADIX, filter_step, 0)


def whiten_kernel(
    length, offset_ref, own_ref, first_ref, next_ref, small_ref, table_ref, taps_ref, both_ref, out_ref,
    z_ref, halo_ref, even_ref, odd_ref, pair_ref, part_ref, late_ref, power_ref, base_ref, rows_ref,
):
    width = own_ref.shape[2]
    device = lax.axis_index(AXES)
    devices = offset_ref.shape[1]
    inside = jnp.where(device == devices - 1, 0.0, 1.0)
    transform_rows(next_ref, 0, 2 * HALF, small_ref, z_ref)
    values = transform_inner(z_ref[...], table_ref)
    halo_ref[0] = values[:, :128]
    halo_ref[1] = values[:, 128:]

    power_ref[0] = jnp.zeros(power_ref.shape[1:], F32)

    half = width // 2
    edge = HALF // 2
    main = half - HALF
    zeros = jnp.zeros((edge, 128), F32)

    def joined(q, r):
        count = half // 2 - HALF
        parts = [first_ref[q, r, 0 : half + count, :], late_ref[q, r, 0:HALF, :]]
        parts += [first_ref[q, r, half + half // 2 : half + half // 2 + count, :], late_ref[q, r, HALF:, :]]
        return jnp.concatenate(parts, axis=0)

    def filter_step(q, carry):
        at = pl.multiple_of(q * 2 * HALF, 2 * HALF)
        for r in range(2):
            for parity, ref, pitch in ((0, even_ref, 4 * edge), (1, odd_ref, 3 * edge)):
                last = own_ref[q, r, pl.ds(2 * main + parity, 2 * edge, stride=2), :]
                after = halo_ref[r, pl.ds(at + parity, 2 * edge, stride=2), :]
                ref[r, 0 : 2 * edge, :] = last
                ref[r, 2 * edge : 3 * edge, :] = after[:edge] * inside
                ref[r, pitch : pitch + edge, :] = last[edge:] * inside
                ref[r, pitch + edge : pitch + 3 * edge, :] = after
            for line in range(2):
                even, odd = 4 * edge * line, 3 * edge * line
                even_ref[r, even + 3 * edge : even + 4 * edge, :] = zeros
                pair_ref[r, odd : odd + 3 * edge, :] = (
                    odd_ref[r, odd : odd + 3 * edge, :] + even_ref[r, even + 1 : even + 3 * edge + 1, :]
                )
            for line in range(2):
                result = short_filters(
                    taps_ref, both_ref, q, even_ref, odd_ref, pair_ref, part_ref, r, 4 * edge * line, 3 * edge * line, edge
                )
                for parity in range(2):
                    row = HALF * parity + edge * line
                    late_ref[q, r, row : row + edge, :] = result[parity]
        real, imaginary = joined(q, 0), joined(q, 1)
        power_ref[q + 1] = power_ref[q] + (real * real + imaginary * imaginary)
        return carry

    lax.fori_loop(0, RADIX, filter_step, 0)

    reach = SMOOTH // RADIX
    lane = lax.broadcasted_iota(jnp.int32, (1, 128), 1)

    def shifted(values, by):
        inside = jnp.where((lane + by >= 0) & (lane + by < 128), 1.0, 0.0)
        return pltpu.roll(values, (-by) % 128, 1) * inside

    whole = power_ref[RADIX]
    base = whole
    for by in range(1, reach):
        base = base + (shifted(whole, by) + shifted(whole, -by))
    base_ref[...] = base

    bins = lax.broadcasted_iota(jnp.int32, (RADIX, 128), 1) * RADIX + lax.broadcasted_iota(
        jnp.int32, (RADIX, 128), 0
    )
    place = lax.broadcasted_iota(jnp.int32, offset_ref.shape, 1)
    turns = []
    for block in (device, lax.rem(device + 1, devices)):
        offset = jnp.sum(jnp.where(place == block, offset_ref[...], 0), axis=1, keepdims=True)
        phases = lax.rem(bins * offset, length).astype(F32) * (2.0 * np.pi / length)
        turns.append((jnp.cos(phases), jnp.sin(phases)))

    def by_row(part, q):
        mine, its = turns[0][part][q : q + 1, :], turns[1][part][q : q + 1, :]
        sizes = (half + half // 2 - edge, edge, half // 2 - edge, edge)
        return jnp.concatenate(
            [jnp.broadcast_to(its if n % 2 else mine, (size, 128)) for n, size in enumerate(sizes)], axis=0
        )

    pitch = 2 * RADIX + 1
    for q in range(RADIX):
        window = (
            base_ref[...]
            + shifted(power_ref[RADIX] - power_ref[q], -reach)
            + shifted(power_ref[q + 1], reach)
        )
        scale = lax.rsqrt(window * small_ref[2 * RADIX + q : 2 * RADIX + q + 1, 0:128] + EPSILON)
        fr, fi = joined(q, 0), joined(q, 1)
        c, s = by_row(0, q), by_row(1, q)
        wr = (fr * c + fi * s) * scale
        wi = (fi * c - fr * s) * scale
        rows_ref[pl.ds(q, 128, stride=pitch), :] = wr.T
        rows_ref[pl.ds(RADIX + q, 128, stride=pitch), :] = wi.T
    for m in range(128):
        rows = rows_ref[m * pitch : m * pitch + 2 * RADIX, :]
        out_ref[2 * RADIX * m : 2 * RADIX * (m + 1), :] = rows.astype(BF16)


def pair_kernel(slots, mine, pairs_hbm, band_ref, basis_ref, *refs):
    if mine:
        before_ref = None
    else:
        before_ref, refs = refs[0], refs[1:]
    out_ref, left_ref, right_ref, cross0_ref, cross1_ref, pairs_ref, sem_ref = refs
    copy = pltpu.make_async_copy(pairs_hbm, pairs_ref, sem_ref.at[0])
    copy.start()
    blocks = band_ref.shape[0]
    groups = band_ref.shape[1] // (2 * RADIX)
    deep = basis_ref.shape[1]
    half = lax.rem(lax.axis_index("shard"), 2)
    part = half if mine else 1 - half
    kept = slots // 2
    step = cross0_ref.shape[1] // (128 * kept)

    lane = lax.broadcasted_iota(jnp.int32, band_ref.shape[1:], 1)
    from_before = (lane >= 64) & (lax.rem(lane, 32) >= 32 - HALF // 2)

    def spread(i, carry):
        before = band_ref[lax.rem(8 * i + blocks - 1, blocks)].astype(F32)
        for n in range(8):
            values = band_ref[8 * i + n].astype(F32)
            whole = jnp.where(from_before, before, values)
            left_ref[8 * i + n] = whole
            right_ref[8 * i + n] = pltpu.roll(whole, 64, 1)
            before = values
        return carry

    lax.fori_loop(0, blocks // 8, spread, 0)
    copy.wait()

    def products(i, cross_ref):
        for n in range(step * kept):
            slot = (step * i + n // kept) * slots + half * kept + n % kept
            a, b = pairs_ref[0, slot], pairs_ref[1, slot]
            for m in range(groups):
                lo, mid, hi = 2 * RADIX * m, 2 * RADIX * m + RADIX, 2 * RADIX * (m + 1)
                lr, li = left_ref[a, lo:mid, :], left_ref[a, mid:hi, :]
                rr, ri = right_ref[b, lo:mid, :], right_ref[b, mid:hi, :]
                cross_ref[lo:mid, 128 * n : 128 * n + 128] = (lr * rr + li * ri).astype(BF16)
                cross_ref[mid:hi, 128 * n : 128 * n + 128] = (li * rr - lr * ri).astype(BF16)

    def project(i, cross_ref):
        result = jnp.dot(basis_ref[part], cross_ref[...], preferred_element_type=F32)
        for u in range(step):
            lanes = [128 * (kept * u + j) for j in range(kept)]
            stacked = jnp.concatenate([result[:, at : at + 128] for at in lanes], axis=0)
            if mine:
                out_ref[step * i + u] = stacked
            else:
                out_ref[step * i + u] = (stacked + before_ref[step * i + u]).astype(BF16)

    last = blocks // step - 1
    products(0, cross0_ref)

    def owners(i, carry):
        products(2 * i + 1, cross1_ref)
        project(2 * i, cross0_ref)
        products(jnp.minimum(2 * i + 2, last), cross0_ref)
        project(2 * i + 1, cross1_ref)
        return carry

    lax.fori_loop(0, blocks // (2 * step), owners, 0)


def lag_kernel(slots, scale, valid_ref, parts_ref, table_ref, out_ref, wide_ref, stage_ref, sem_ref):
    bands = parts_ref.shape[0] // 2
    kept = slots // 2
    deep = parts_ref.shape[1] // kept

    def gather(i, carry):
        for n in range(4):
            b = 4 * i + n
            at = pl.multiple_of(b * deep, 8)
            for half in range(2):
                values = parts_ref[2 * b + half].astype(F32)
                for j in range(kept):
                    lane = 128 * (half * kept + j)
                    wide_ref[pl.ds(at, deep), lane : lane + 128] = values[deep * j : deep * (j + 1)]
        return carry

    lax.fori_loop(0, bands // 4, gather, 0)
    copies = []
    for first in range(0, slots, 2):
        columns = wide_ref[:, 128 * first : 128 * first + 256].astype(BF16)
        for n in range(NLAG // 128):
            result = jnp.dot(table_ref[128 * n : 128 * n + 128, :], columns, preferred_element_type=F32)
            for j in range(2):
                weight = valid_ref[:, first + j : first + j + 1].astype(F32) * scale
                turned = result[:, 128 * j : 128 * j + 128].T * weight
                half = turned.shape[0] // 2
                at = (first + j) * (NLAG // 128) + n
                quarter = half // 2
                for parity in range(2):
                    pieces = (
                        (quarter * parity, HALF, quarter),
                        (half + quarter * parity, half + HALF, quarter - HALF // 2),
                        (half + quarter * (parity + 1) - HALF // 2, 0, HALF // 2),
                    )
                    for row, channel, count in pieces:
                        stage_ref[at, pl.ds(channel + parity, count, stride=2), :] = turned[row : row + count]
                lanes = pl.ds(128 * n, 128)
                copy = pltpu.make_async_copy(stage_ref.at[at], out_ref.at[first + j, :, lanes], sem_ref.at[at])
                copy.start()
                copies.append(copy)
    for copy in copies:
        copy.wait()


def vmem():
    return pl.BlockSpec(memory_space=pltpu.VMEM)


def params():
    return pltpu.CompilerParams(vmem_limit_bytes=VMEM_BYTES)


def near(array):
    return pltpu.with_memory_space_constraint(array, pltpu.VMEM)


def distant(array):
    return pltpu.with_memory_space_constraint(array, pltpu.HBM)


def far():
    return pl.BlockSpec(memory_space=pltpu.HBM)


def body(samples, fan_taps, pair_blocks, pair_valid, coil_offsets):
    width = samples.shape[0]
    length = samples.shape[2]
    bin_count = length // 2
    devices = lax.axis_size("group") * lax.axis_size("shard")
    shards = lax.axis_size("shard")
    bins_device = bin_count // devices
    slots = pair_valid.shape[0]
    inner = length // RADIX
    lanes = bin_count // RADIX
    chunk = 64

    twiddle, table = forward_constants(length)
    basis, lag_table = band_constants(devices // 2, 2 * bins_device, length)
    project = projection_constants(basis, 2)
    deep = project.shape[1]
    bins_k = np.arange(bin_count)
    counts = np.minimum(bins_k + SMOOTH, bin_count - 1) - np.maximum(bins_k - SMOOTH, 0) + 1
    small = np.zeros((3 * RADIX, inner), np.float32)
    small[: 2 * RADIX] = twiddle
    small[2 * RADIX :, :lanes] = (1.0 / counts).reshape(lanes, RADIX).T

    x = samples.reshape(width, length)
    after = lax.ppermute(x[: 2 * HALF], AXES, [((i + 1) % devices, i) for i in range(devices)])

    own, ready, taps, both, small, table = pl.pallas_call(
        own_kernel,
        out_shape=(
            pltpu.VMEM((RADIX, 2, width, lanes), F32),
            pltpu.VMEM((RADIX, 2, width, lanes), F32),
            pltpu.VMEM((RADIX, 2 * HALF + 1, lanes), F32),
            pltpu.VMEM((RADIX, HALF + 1, lanes), F32),
            pltpu.VMEM(small.shape, F32),
            pltpu.VMEM(table.shape, BF16),
        ),
        in_specs=[far()] * 4,
        out_specs=(vmem(),) * 6,
        scratch_shapes=[
            pltpu.VMEM((width, length), BF16),
            pltpu.VMEM(fan_taps.shape, F32),
            pltpu.VMEM((RADIX * chunk, 4 * inner), BF16),
            pltpu.VMEM((RADIX * chunk, 4 * inner), BF16),
            pltpu.VMEM((bin_count + lanes, 128), F32),
            pltpu.VMEM((2, width // 2 + 8, lanes), F32),
            pltpu.VMEM((2, width // 2, lanes), F32),
            pltpu.VMEM((2, width // 2, lanes), F32),
            pltpu.VMEM((2, width // 2, lanes), F32),
            pltpu.SemaphoreType.DMA((width // chunk + 3,)),
        ],
        compiler_params=params(),
        name="own_spectra",
    )(distant(x), distant(fan_taps), distant(jnp.asarray(small)), distant(jnp.asarray(table)))

    rows = pl.pallas_call(
        functools.partial(whiten_kernel, length),
        out_shape=pltpu.VMEM((2 * bin_count, width), BF16),
        in_specs=[vmem()] * 8,
        out_specs=vmem(),
        scratch_shapes=[
            pltpu.VMEM((RADIX * 2 * HALF, 4 * inner), BF16),
            pltpu.VMEM((2, RADIX * 2 * HALF, lanes), F32),
            pltpu.VMEM((2, 4 * HALF, lanes), F32),
            pltpu.VMEM((2, 3 * HALF, lanes), F32),
            pltpu.VMEM((2, 3 * HALF, lanes), F32),
            pltpu.VMEM((2, HALF, lanes), F32),
            pltpu.VMEM((RADIX, 2, 2 * HALF, lanes), F32),
            pltpu.VMEM((RADIX + 1, width, lanes), F32),
            pltpu.VMEM((width, lanes), F32),
            pltpu.VMEM((2 * bin_count + lanes, width), F32),
        ],
        compiler_params=params(),
        name="whiten",
    )(near(coil_offsets.reshape(1, -1)), near(own), near(ready), near(after), near(small), near(table), near(taps), near(both))

    band = lax.all_to_all(
        rows.reshape(devices, 2 * bins_device, width), AXES, split_axis=0, concat_axis=0, tiled=True
    )
    other = lax.ppermute(band, "shard", [(i, i ^ 1) for i in range(shards)])

    pairs = distant(pair_blocks.T)
    project = near(jnp.asarray(project))
    sums = (devices, slots // 2 * deep, width)

    def products(mine, part, before):
        return pl.pallas_call(
            functools.partial(pair_kernel, slots, mine),
            out_shape=pltpu.VMEM(sums, F32 if mine else BF16),
            in_specs=[far()] + [vmem()] * (2 + len(before)),
            out_specs=vmem(),
            scratch_shapes=[
                pltpu.VMEM((devices, 2 * bins_device, width), F32),
                pltpu.VMEM((devices, 2 * bins_device, width), F32),
                pltpu.VMEM((2 * bins_device, 4 * slots * width), BF16),
                pltpu.VMEM((2 * bins_device, 4 * slots * width), BF16),
                pltpu.SMEM(pairs.shape, jnp.int32),
                pltpu.SemaphoreType.DMA((1,)),
            ],
            compiler_params=params(),
            name="pairs_own_part" if mine else "pairs_other_part",
        )(pairs, near(part), project, *before)

    first = products(True, band, ())
    parts = products(False, other, (near(first),))

    owned = lax.all_to_all(parts, AXES, split_axis=0, concat_axis=0, tiled=True)

    return pl.pallas_call(
        functools.partial(lag_kernel, slots, float(1.0 / np.sqrt(bin_count * samples.shape[1]))),
        out_shape=jax.ShapeDtypeStruct((slots, width, NLAG), F32),
        in_specs=[vmem()] * 3,
        out_specs=pl.BlockSpec(memory_space=pl.ANY),
        scratch_shapes=[
            pltpu.VMEM((devices // 2 * deep, slots * width), F32),
            pltpu.VMEM((slots * NLAG // 128, width, 128), F32),
            pltpu.SemaphoreType.DMA((slots * NLAG // 128,)),
        ],
        compiler_params=params(),
        name="lags",
    )(near(pair_valid.reshape(1, -1)), near(owned), near(jnp.asarray(lag_table)))


def solution(mesh):
    return jax.shard_map(
        body,
        mesh=mesh,
        in_specs=(P(AXES, None, None), P(), P(), P(AXES), P()),
        out_specs=P(AXES, None, None),
        check_vma=False,
    )
```

```python
import functools

import jax
import jax.numpy as jnp
import ml_dtypes
import numpy as np
from jax import lax
from jax.experimental import pallas as pl
from jax.experimental.pallas import tpu as pltpu
from jax.sharding import PartitionSpec as P

AXES = ("group", "shard")
HALF = 16
SMOOTH = 64
NLAG = 512
EPSILON = 1e-05
RADIX = 16
VMEM_BYTES = 32 * 1024 * 1024
F32 = jnp.float32
BF16 = jnp.bfloat16


def as_bf16(table):
    return table.astype(ml_dtypes.bfloat16)


def forward_constants(length):
    inner = length // RADIX
    n1 = np.arange(inner)
    turns = (np.arange(RADIX)[:, None] * n1[None, :]) * (2.0 * np.pi / length)
    twiddle = np.concatenate([np.cos(turns), np.sin(turns)]).astype(np.float32)
    angle = np.mod(n1[:, None] * np.arange(inner // 2)[None, :], inner) * (2.0 * np.pi / inner)
    cosine, sine = np.cos(angle), np.sin(angle)
    table = np.concatenate(
        [np.concatenate([cosine, -sine], axis=1), np.concatenate([sine, cosine], axis=1)]
    ) / np.sqrt(length)
    high = as_bf16(table)
    low = as_bf16(table - high.astype(np.float64))
    return twiddle, np.concatenate([high, low])


def band_constants(bands, width, length):
    place = np.arange(width)
    diagonal = ((width - 1 - 2 * place) / 2.0) ** 2 * np.cos(np.pi * NLAG / length)
    beside = place[1:] * (width - place[1:]) / 2.0
    matrix = np.diag(diagonal) + np.diag(beside, 1) + np.diag(beside, -1)
    vectors = np.linalg.eigh(matrix)[1][:, ::-1]
    upper = vectors[(width + 1) // 2 :]
    vectors = vectors * np.sign(upper[np.argmax(np.abs(upper), axis=0), np.arange(width)])[None, :]
    lags = np.arange(NLAG) - NLAG // 2
    waves = np.exp(2j * np.pi * np.outer(place - (width - 1) / 2.0, lags) / length)
    rank = width
    for fewer in range(4, width, 4):
        basis = vectors[:, :fewer]
        error = waves - basis @ (basis.T @ waves)
        if np.sqrt(np.mean(np.abs(error) ** 2)) < 1e-7:
            rank = fewer
            break
    basis = vectors[:, :rank]
    partner = basis.T @ waves
    centres = width * np.arange(bands) + (width - 1) / 2.0
    carrier = np.exp(2j * np.pi * np.outer(centres, lags) / length)
    whole = carrier[:, None, :] * partner[None, :, :]
    table = np.concatenate([whole.real, -whole.imag], axis=1).reshape(bands * 2 * rank, NLAG)
    return basis, as_bf16(np.ascontiguousarray(table.T))


def projection_constants(basis, halves):
    width, rank = basis.shape
    groups = width // halves // RADIX
    rows = np.zeros((halves, 2, rank, groups, 2, RADIX))
    split = basis.T.reshape(rank, halves, groups, RADIX).transpose(1, 0, 2, 3)
    rows[:, 0, :, :, 0, :] = split
    rows[:, 1, :, :, 1, :] = split
    return as_bf16(rows.reshape(halves, 2 * rank, 2 * groups * RADIX))


def real_dft(values):
    count = len(values)
    if count == 1:
        return [(values[0], None)]
    even, odd = real_dft(values[0::2]), real_dft(values[1::2])
    out = [None] * (count // 2 + 1)
    out[0] = (even[0][0] + odd[0][0], None)
    out[count // 2] = (even[0][0] - odd[0][0], None)
    for k in range(1, count // 4 + 1):
        er, ei = even[k]
        orr, oi = odd[k]
        if 4 * k == count:
            out[k] = (er, -orr)
            continue
        c, s = float(np.cos(2 * np.pi * k / count)), float(np.sin(2 * np.pi * k / count))
        tr = orr * c + oi * s
        ti = oi * c - orr * s
        out[k] = (er + tr, ei + ti)
        out[count // 2 - k] = (er - tr, ti - ei)
    return out


def transform_rows(x_ref, first, rows, twiddle_ref, z_ref):
    inner = x_ref.shape[1] // RADIX
    for at in range(0, rows, 16):
        for lane in range(0, inner, 128):
            values = [
                x_ref[first + at : first + at + 16, inner * j + lane : inner * j + lane + 128].astype(F32)
                for j in range(RADIX)
            ]
            bins = real_dft(values)
            for q in range(RADIX):
                yr, yi = bins[q] if q <= RADIX // 2 else bins[RADIX - q]
                if q > RADIX // 2:
                    yi = -yi
                if q == 0:
                    zr, zi = yr, jnp.zeros_like(yr)
                else:
                    c = twiddle_ref[q : q + 1, lane : lane + 128]
                    s = twiddle_ref[RADIX + q : RADIX + q + 1, lane : lane + 128]
                    if yi is None:
                        zr, zi = yr * c, -yr * s
                    else:
                        zr, zi = yr * c + yi * s, yi * c - yr * s
                where = slice(q * rows + at, q * rows + at + 16)
                for part, z in ((0, zr), (1, zi)):
                    high = z.astype(BF16)
                    z_ref[where, part * inner + lane : part * inner + lane + 128] = high
                    low = (z - high.astype(F32)).astype(BF16)
                    start = (2 + part) * inner + lane
                    z_ref[where, start : start + 128] = low


def transform_inner(z, table_ref):
    depth = z.shape[1] // 2
    high, low = table_ref[0:depth, :], table_ref[depth:, :]
    out = jnp.dot(z[:, :depth], high, preferred_element_type=F32)
    out = out + jnp.dot(z[:, depth:], high, preferred_element_type=F32)
    return out + jnp.dot(z[:, :depth], low, preferred_element_type=F32)


def short_filters(taps_ref, both_ref, q, even_ref, odd_ref, pair_ref, part_ref, r, even, odd, rows):
    evens = jnp.zeros((rows + 8, 128), F32)
    odds = jnp.zeros((rows, 128), F32)
    pairs = jnp.zeros((rows, 128), F32)
    for u in range(HALF + 1):
        evens = evens + taps_ref[q, 2 * u : 2 * u + 1, :] * even_ref[r, even + u : even + u + rows + 8, :]
    part_ref[r, 0 : rows + 8, :] = evens
    for u in range(HALF):
        odds = odds + taps_ref[q, 2 * u + 1 : 2 * u + 2, :] * odd_ref[r, odd + u : odd + u + rows, :]
    for u in range(HALF + 1):
        pairs = pairs + both_ref[q, u : u + 1, :] * pair_ref[r, odd + u : odd + u + rows, :]
    return evens[:rows] + odds, pairs - (part_ref[r, 1 : rows + 1, :] + odds)


def head_kernel(x_hbm, taps_hbm, small_hbm, head_ref, taps_ref, small_ref, sem_ref):
    sources = (x_hbm.at[pl.ds(0, head_ref.shape[0])], taps_hbm, small_hbm)
    targets = (head_ref, taps_ref, small_ref)
    copies = [pltpu.make_async_copy(sources[i], targets[i], sem_ref.at[i]) for i in range(3)]
    for copy in copies:
        copy.start()
    for copy in copies:
        copy.wait()


def own_kernel(
    x_hbm, taps_ref, small_ref, table_hbm, out_ref, first_ref, split_ref, both_ref, table_ref,
    x_ref, z0_ref, z1_ref, turned_ref, even_ref, odd_ref, pair_ref, part_ref, sem_ref,
):
    chunk = z0_ref.shape[0] // RADIX
    steps = x_ref.shape[0] // chunk
    slots = (z0_ref, z1_ref)
    copies = []
    for i in range(steps):
        rows = pl.ds(i * chunk, chunk)
        copies.append(pltpu.make_async_copy(x_hbm.at[rows], x_ref.at[rows], sem_ref.at[i]))
    table_copy = pltpu.make_async_copy(table_hbm, table_ref, sem_ref.at[steps])
    for i, copy in enumerate(copies):
        copy.start()
        if i == 0:
            table_copy.start()

    count = taps_ref.shape[0]
    pitch = RADIX + 1
    for at in range(0, taps_ref.shape[1], 128):
        turned = taps_ref[:, at : at + 128].T
        for n in range(128 // RADIX):
            row = (at // RADIX + n) * pitch
            turned_ref[row : row + RADIX, 0:count] = turned[RADIX * n : RADIX * (n + 1)]
    for q in range(RADIX):
        taps = turned_ref[pl.ds(q, 128, stride=pitch), 0:count].T
        split_ref[q, 0:count, :] = taps
        even = split_ref[q, pl.ds(0, HALF, stride=2), :]
        odd = split_ref[q, pl.ds(1, HALF, stride=2), :]
        both_ref[q, 0:HALF, :] = even + odd
        both_ref[q, HALF : HALF + 1, :] = taps[count - 1 :]

    copies[0].wait()
    transform_rows(x_ref, 0, chunk, small_ref, z0_ref)
    table_copy.wait()
    for i in range(steps):
        if i + 1 < steps:
            copies[1 + i].wait()
            transform_rows(x_ref, (i + 1) * chunk, chunk, small_ref, slots[(i + 1) % 2])
        values = transform_inner(slots[i % 2][...], table_ref)
        for q in range(RADIX):
            out_ref[q, 0, i * chunk : (i + 1) * chunk, :] = values[q * chunk : (q + 1) * chunk, :128]
            out_ref[q, 1, i * chunk : (i + 1) * chunk, :] = values[q * chunk : (q + 1) * chunk, 128:]

    half = x_ref.shape[0] // 2
    rows = half - HALF
    quarter = half // 2
    even_ref[:, half:, :] = jnp.zeros((2, 8, 128), F32)

    def filter_step(q, carry):
        for r in range(2):
            even_ref[r, 0:half, :] = out_ref[q, r, pl.ds(0, half, stride=2), :]
            odd_ref[r] = out_ref[q, r, pl.ds(1, half, stride=2), :]
            pair_ref[r] = odd_ref[r] + even_ref[r, 1 : half + 1, :]
            result = short_filters(split_ref, both_ref, q, even_ref, odd_ref, pair_ref, part_ref, r, 0, 0, rows)
            for parity in range(2):
                first_ref[q, r, quarter * parity : quarter * (parity + 1), :] = result[parity][:quarter]
                at = half + quarter * parity
                first_ref[q, r, at : at + rows - quarter, :] = result[parity][quarter:]
        return carry

    lax.fori_loop(0, RADIX, filter_step, 0)


def whiten_kernel(
    length, offset_ref, own_ref, first_ref, next_ref, small_ref, table_ref, taps_ref, both_ref, out_ref,
    z_ref, halo_ref, even_ref, odd_ref, pair_ref, part_ref, late_ref, power_ref, base_ref, rows_ref,
):
    width = own_ref.shape[2]
    device = lax.axis_index(AXES)
    devices = offset_ref.shape[1]
    inside = jnp.where(device == devices - 1, 0.0, 1.0)
    transform_rows(next_ref, 0, 2 * HALF, small_ref, z_ref)
    values = transform_inner(z_ref[...], table_ref)
    halo_ref[0] = values[:, :128]
    halo_ref[1] = values[:, 128:]

    power_ref[0] = jnp.zeros(power_ref.shape[1:], F32)

    half = width // 2
    edge = HALF // 2
    main = half - HALF
    zeros = jnp.zeros((edge, 128), F32)

    def joined(q, r):
        count = half // 2 - HALF
        parts = [first_ref[q, r, 0 : half + count, :], late_ref[q, r, 0:HALF, :]]
        parts += [first_ref[q, r, half + half // 2 : half + half // 2 + count, :], late_ref[q, r, HALF:, :]]
        return jnp.concatenate(parts, axis=0)

    def filter_step(q, n):
        at = pl.multiple_of(q * 2 * HALF, 2 * HALF)
        for r in range(2):
            b = 2 * n + r
            for parity, ref, pitch in ((0, even_ref, 4 * edge), (1, odd_ref, 3 * edge)):
                last = own_ref[q, r, pl.ds(2 * main + parity, 2 * edge, stride=2), :]
                after = halo_ref[r, pl.ds(at + parity, 2 * edge, stride=2), :]
                ref[b, 0 : 2 * edge, :] = last
                ref[b, 2 * edge : 3 * edge, :] = after[:edge] * inside
                ref[b, pitch : pitch + edge, :] = last[edge:] * inside
                ref[b, pitch + edge : pitch + 3 * edge, :] = after
            for line in range(2):
                even, odd = 4 * edge * line, 3 * edge * line
                even_ref[b, even + 3 * edge : even + 4 * edge, :] = zeros
                pair_ref[b, odd : odd + 3 * edge, :] = (
                    odd_ref[b, odd : odd + 3 * edge, :] + even_ref[b, even + 1 : even + 3 * edge + 1, :]
                )
            for line in range(2):
                result = short_filters(
                    taps_ref, both_ref, q, even_ref, odd_ref, pair_ref, part_ref, b, 4 * edge * line, 3 * edge * line, edge
                )
                for parity in range(2):
                    row = HALF * parity + edge * line
                    late_ref[q, r, row : row + edge, :] = result[parity]

    def filter_steps(i, carry):
        for n in range(together):
            filter_step(together * i + n, n)
        for n in range(together):
            q = together * i + n
            real, imaginary = joined(q, 0), joined(q, 1)
            power_ref[q + 1] = power_ref[q] + (real * real + imaginary * imaginary)
        return carry

    together = 4
    lax.fori_loop(0, RADIX // together, filter_steps, 0)

    reach = SMOOTH // RADIX
    lane = lax.broadcasted_iota(jnp.int32, (1, 128), 1)

    def shifted(values, by):
        inside = jnp.where((lane + by >= 0) & (lane + by < 128), 1.0, 0.0)
        return pltpu.roll(values, (-by) % 128, 1) * inside

    whole = power_ref[RADIX]
    base = whole
    for by in range(1, reach):
        base = base + (shifted(whole, by) + shifted(whole, -by))
    base_ref[...] = base

    bins = lax.broadcasted_iota(jnp.int32, (RADIX, 128), 1) * RADIX + lax.broadcasted_iota(
        jnp.int32, (RADIX, 128), 0
    )
    place = lax.broadcasted_iota(jnp.int32, offset_ref.shape, 1)
    turns = []
    for block in (device, lax.rem(device + 1, devices)):
        offset = jnp.sum(jnp.where(place == block, offset_ref[...], 0), axis=1, keepdims=True)
        phases = lax.rem(bins * offset, length).astype(F32) * (2.0 * np.pi / length)
        turns.append((jnp.cos(phases), jnp.sin(phases)))

    def by_row(part, q):
        mine, its = turns[0][part][q : q + 1, :], turns[1][part][q : q + 1, :]
        sizes = (half + half // 2 - edge, edge, half // 2 - edge, edge)
        return jnp.concatenate(
            [jnp.broadcast_to(its if n % 2 else mine, (size, 128)) for n, size in enumerate(sizes)], axis=0
        )

    pitch = 2 * RADIX + 1
    for q in range(RADIX):
        window = (
            base_ref[...]
            + shifted(power_ref[RADIX] - power_ref[q], -reach)
            + shifted(power_ref[q + 1], reach)
        )
        scale = lax.rsqrt(window * small_ref[2 * RADIX + q : 2 * RADIX + q + 1, 0:128] + EPSILON)
        fr, fi = joined(q, 0), joined(q, 1)
        c, s = by_row(0, q), by_row(1, q)
        wr = (fr * c + fi * s) * scale
        wi = (fi * c - fr * s) * scale
        rows_ref[pl.ds(q, 128, stride=pitch), :] = wr.T
        rows_ref[pl.ds(RADIX + q, 128, stride=pitch), :] = wi.T
    for m in range(128):
        rows = rows_ref[m * pitch : m * pitch + 2 * RADIX, :]
        out_ref[2 * RADIX * m : 2 * RADIX * (m + 1), :] = rows.astype(BF16)


def pair_kernel(slots, mine, pairs_hbm, band_ref, basis_ref, *refs):
    if mine:
        before_ref = None
    else:
        before_ref, refs = refs[0], refs[1:]
    out_ref, left_ref, right_ref, cross0_ref, cross1_ref, pairs_ref, sem_ref = refs
    copy = pltpu.make_async_copy(pairs_hbm, pairs_ref, sem_ref.at[0])
    copy.start()
    blocks = band_ref.shape[0]
    groups = band_ref.shape[1] // (2 * RADIX)
    deep = basis_ref.shape[1]
    half = lax.rem(lax.axis_index("shard"), 2)
    part = half if mine else 1 - half
    kept = slots // 2
    step = cross0_ref.shape[1] // (128 * kept)

    lane = lax.broadcasted_iota(jnp.int32, band_ref.shape[1:], 1)
    from_before = (lane >= 64) & (lax.rem(lane, 32) >= 32 - HALF // 2)

    def spread(i, carry):
        before = band_ref[lax.rem(8 * i + blocks - 1, blocks)].astype(F32)
        for n in range(8):
            values = band_ref[8 * i + n].astype(F32)
            whole = jnp.where(from_before, before, values)
            left_ref[8 * i + n] = whole
            right_ref[8 * i + n] = pltpu.roll(whole, 64, 1)
            before = values
        return carry

    lax.fori_loop(0, blocks // 8, spread, 0)
    copy.wait()

    def products(i, cross_ref):
        for n in range(step * kept):
            slot = (step * i + n // kept) * slots + half * kept + n % kept
            a, b = pairs_ref[0, slot], pairs_ref[1, slot]
            for m in range(groups):
                lo, mid, hi = 2 * RADIX * m, 2 * RADIX * m + RADIX, 2 * RADIX * (m + 1)
                lr, li = left_ref[a, lo:mid, :], left_ref[a, mid:hi, :]
                rr, ri = right_ref[b, lo:mid, :], right_ref[b, mid:hi, :]
                cross_ref[lo:mid, 128 * n : 128 * n + 128] = (lr * rr + li * ri).astype(BF16)
                cross_ref[mid:hi, 128 * n : 128 * n + 128] = (li * rr - lr * ri).astype(BF16)

    def project(i, cross_ref):
        result = jnp.dot(basis_ref[part], cross_ref[...], preferred_element_type=F32)
        for u in range(step):
            lanes = [128 * (kept * u + j) for j in range(kept)]
            stacked = jnp.concatenate([result[:, at : at + 128] for at in lanes], axis=0)
            if mine:
                out_ref[step * i + u] = stacked
            else:
                out_ref[step * i + u] = (stacked + before_ref[step * i + u]).astype(BF16)

    last = blocks // step - 1
    products(0, cross0_ref)

    def owners(i, carry):
        products(2 * i + 1, cross1_ref)
        project(2 * i, cross0_ref)
        products(jnp.minimum(2 * i + 2, last), cross0_ref)
        project(2 * i + 1, cross1_ref)
        return carry

    lax.fori_loop(0, blocks // (2 * step), owners, 0)


def lag_kernel(slots, scale, valid_ref, parts_ref, table_ref, out_ref, wide_ref, stage_ref, sem_ref):
    bands = parts_ref.shape[0] // 2
    kept = slots // 2
    deep = parts_ref.shape[1] // kept

    def gather(i, carry):
        for n in range(4):
            b = 4 * i + n
            at = pl.multiple_of(b * deep, 8)
            for half in range(2):
                values = parts_ref[2 * b + half].astype(F32)
                for j in range(kept):
                    lane = 128 * (half * kept + j)
                    wide_ref[pl.ds(at, deep), lane : lane + 128] = values[deep * j : deep * (j + 1)]
        return carry

    lax.fori_loop(0, bands // 4, gather, 0)
    copies = []
    for first in range(0, slots, 2):
        columns = wide_ref[:, 128 * first : 128 * first + 256].astype(BF16)
        for n in range(NLAG // 128):
            result = jnp.dot(table_ref[128 * n : 128 * n + 128, :], columns, preferred_element_type=F32)
            for j in range(2):
                weight = valid_ref[:, first + j : first + j + 1].astype(F32) * scale
                turned = result[:, 128 * j : 128 * j + 128].T * weight
                half = turned.shape[0] // 2
                at = (first + j) * (NLAG // 128) + n
                quarter = half // 2
                for parity in range(2):
                    pieces = (
                        (quarter * parity, HALF, quarter),
                        (half + quarter * parity, half + HALF, quarter - HALF // 2),
                        (half + quarter * (parity + 1) - HALF // 2, 0, HALF // 2),
                    )
                    for row, channel, count in pieces:
                        stage_ref[at, pl.ds(channel + parity, count, stride=2), :] = turned[row : row + count]
                lanes = pl.ds(128 * n, 128)
                copy = pltpu.make_async_copy(stage_ref.at[at], out_ref.at[first + j, :, lanes], sem_ref.at[at])
                copy.start()
                copies.append(copy)
    for copy in copies:
        copy.wait()


def vmem():
    return pl.BlockSpec(memory_space=pltpu.VMEM)


def params():
    return pltpu.CompilerParams(vmem_limit_bytes=VMEM_BYTES)


def near(array):
    return pltpu.with_memory_space_constraint(array, pltpu.VMEM)


def distant(array):
    return pltpu.with_memory_space_constraint(array, pltpu.HBM)


def far():
    return pl.BlockSpec(memory_space=pltpu.HBM)


def body(samples, fan_taps, pair_blocks, pair_valid, coil_offsets):
    width = samples.shape[0]
    length = samples.shape[2]
    bin_count = length // 2
    devices = lax.axis_size("group") * lax.axis_size("shard")
    shards = lax.axis_size("shard")
    bins_device = bin_count // devices
    slots = pair_valid.shape[0]
    inner = length // RADIX
    lanes = bin_count // RADIX
    chunk = 64

    twiddle, table = forward_constants(length)
    basis, lag_table = band_constants(devices // 2, 2 * bins_device, length)
    project = projection_constants(basis, 2)
    deep = project.shape[1]
    bins_k = np.arange(bin_count)
    counts = np.minimum(bins_k + SMOOTH, bin_count - 1) - np.maximum(bins_k - SMOOTH, 0) + 1
    small = np.zeros((3 * RADIX, inner), np.float32)
    small[: 2 * RADIX] = twiddle
    small[2 * RADIX :, :lanes] = (1.0 / counts).reshape(lanes, RADIX).T

    x = samples.reshape(width, length)
    x, fan_taps, small = distant(x), distant(fan_taps), distant(jnp.asarray(small))
    head, fan_taps, small = pl.pallas_call(
        head_kernel,
        out_shape=(
            pltpu.VMEM((2 * HALF, length), BF16),
            pltpu.VMEM(fan_taps.shape, F32),
            pltpu.VMEM(small.shape, F32),
        ),
        in_specs=[far()] * 3,
        out_specs=(vmem(),) * 3,
        scratch_shapes=[pltpu.SemaphoreType.DMA((3,))],
        compiler_params=params(),
        name="head",
    )(x, fan_taps, small)
    after = lax.ppermute(head, AXES, [((i + 1) % devices, i) for i in range(devices)])

    own, ready, taps, both, table = pl.pallas_call(
        own_kernel,
        out_shape=(
            pltpu.VMEM((RADIX, 2, width, lanes), F32),
            pltpu.VMEM((RADIX, 2, width, lanes), F32),
            pltpu.VMEM((RADIX, 2 * HALF + 1, lanes), F32),
            pltpu.VMEM((RADIX, HALF + 1, lanes), F32),
            pltpu.VMEM(table.shape, BF16),
        ),
        in_specs=[far(), vmem(), vmem(), far()],
        out_specs=(vmem(),) * 5,
        scratch_shapes=[
            pltpu.VMEM((width, length), BF16),
            pltpu.VMEM((RADIX * chunk, 4 * inner), BF16),
            pltpu.VMEM((RADIX * chunk, 4 * inner), BF16),
            pltpu.VMEM((bin_count + lanes, 128), F32),
            pltpu.VMEM((2, width // 2 + 8, lanes), F32),
            pltpu.VMEM((2, width // 2, lanes), F32),
            pltpu.VMEM((2, width // 2, lanes), F32),
            pltpu.VMEM((2, width // 2, lanes), F32),
            pltpu.SemaphoreType.DMA((width // chunk + 1,)),
        ],
        compiler_params=params(),
        name="own_spectra",
    )(x, near(fan_taps), near(small), distant(jnp.asarray(table)))

    rows = pl.pallas_call(
        functools.partial(whiten_kernel, length),
        out_shape=pltpu.VMEM((2 * bin_count, width), BF16),
        in_specs=[vmem()] * 8,
        out_specs=vmem(),
        scratch_shapes=[
            pltpu.VMEM((RADIX * 2 * HALF, 4 * inner), BF16),
            pltpu.VMEM((2, RADIX * 2 * HALF, lanes), F32),
            pltpu.VMEM((8, 4 * HALF, lanes), F32),
            pltpu.VMEM((8, 3 * HALF, lanes), F32),
            pltpu.VMEM((8, 3 * HALF, lanes), F32),
            pltpu.VMEM((8, HALF, lanes), F32),
            pltpu.VMEM((RADIX, 2, 2 * HALF, lanes), F32),
            pltpu.VMEM((RADIX + 1, width, lanes), F32),
            pltpu.VMEM((width, lanes), F32),
            pltpu.VMEM((2 * bin_count + lanes, width), F32),
        ],
        compiler_params=params(),
        name="whiten",
    )(near(coil_offsets.reshape(1, -1)), near(own), near(ready), near(after), near(small), near(table), near(taps), near(both))

    band = lax.all_to_all(
        rows.reshape(devices, 2 * bins_device, width), AXES, split_axis=0, concat_axis=0, tiled=True
    )
    other = lax.ppermute(band, "shard", [(i, i ^ 1) for i in range(shards)])

    pairs = distant(pair_blocks.T)
    project = near(jnp.asarray(project))
    sums = (devices, slots // 2 * deep, width)

    def products(mine, part, before):
        return pl.pallas_call(
            functools.partial(pair_kernel, slots, mine),
            out_shape=pltpu.VMEM(sums, F32 if mine else BF16),
            in_specs=[far()] + [vmem()] * (2 + len(before)),
            out_specs=vmem(),
            scratch_shapes=[
                pltpu.VMEM((devices, 2 * bins_device, width), F32),
                pltpu.VMEM((devices, 2 * bins_device, width), F32),
                pltpu.VMEM((2 * bins_device, 4 * slots * width), BF16),
                pltpu.VMEM((2 * bins_device, 4 * slots * width), BF16),
                pltpu.SMEM(pairs.shape, jnp.int32),
                pltpu.SemaphoreType.DMA((1,)),
            ],
            compiler_params=params(),
            name="pairs_own_part" if mine else "pairs_other_part",
        )(pairs, near(part), project, *before)

    first = products(True, band, ())
    parts = products(False, other, (near(first),))

    owned = lax.all_to_all(parts, AXES, split_axis=0, concat_axis=0, tiled=True)

    return pl.pallas_call(
        functools.partial(lag_kernel, slots, float(1.0 / np.sqrt(bin_count * samples.shape[1]))),
        out_shape=jax.ShapeDtypeStruct((slots, width, NLAG), F32),
        in_specs=[vmem()] * 3,
        out_specs=pl.BlockSpec(memory_space=pl.ANY),
        scratch_shapes=[
            pltpu.VMEM((devices // 2 * deep, slots * width), F32),
            pltpu.VMEM((slots * NLAG // 128, width, 128), F32),
            pltpu.SemaphoreType.DMA((slots * NLAG // 128,)),
        ],
        compiler_params=params(),
        name="lags",
    )(near(pair_valid.reshape(1, -1)), near(owned), near(jnp.asarray(lag_table)))


def solution(mesh):
    return jax.shard_map(
        body,
        mesh=mesh,
        in_specs=(P(AXES, None, None), P(), P(), P(AXES), P()),
        out_specs=P(AXES, None, None),
        check_vma=False,
    )
```

```python
import functools

import jax
import jax.numpy as jnp
import ml_dtypes
import numpy as np
from jax import lax
from jax.experimental import pallas as pl
from jax.experimental.pallas import tpu as pltpu
from jax.sharding import PartitionSpec as P

AXES = ("group", "shard")
HALF = 16
SMOOTH = 64
NLAG = 512
EPSILON = 1e-05
RADIX = 16
VMEM_BYTES = 32 * 1024 * 1024
F32 = jnp.float32
BF16 = jnp.bfloat16


def as_bf16(table):
    return table.astype(ml_dtypes.bfloat16)


def forward_constants(length):
    inner = length // RADIX
    n1 = np.arange(inner)
    turns = (np.arange(RADIX)[:, None] * n1[None, :]) * (2.0 * np.pi / length)
    twiddle = np.concatenate([np.cos(turns), np.sin(turns)]).astype(np.float32)
    angle = np.mod(n1[:, None] * np.arange(inner // 2)[None, :], inner) * (2.0 * np.pi / inner)
    cosine, sine = np.cos(angle), np.sin(angle)
    table = np.concatenate(
        [np.concatenate([cosine, -sine], axis=1), np.concatenate([sine, cosine], axis=1)]
    ) / np.sqrt(length)
    high = as_bf16(table)
    low = as_bf16(table - high.astype(np.float64))
    return twiddle, np.concatenate([high, low])


def band_constants(bands, width, length):
    place = np.arange(width)
    diagonal = ((width - 1 - 2 * place) / 2.0) ** 2 * np.cos(np.pi * NLAG / length)
    beside = place[1:] * (width - place[1:]) / 2.0
    matrix = np.diag(diagonal) + np.diag(beside, 1) + np.diag(beside, -1)
    vectors = np.linalg.eigh(matrix)[1][:, ::-1]
    upper = vectors[(width + 1) // 2 :]
    vectors = vectors * np.sign(upper[np.argmax(np.abs(upper), axis=0), np.arange(width)])[None, :]
    lags = np.arange(NLAG) - NLAG // 2
    waves = np.exp(2j * np.pi * np.outer(place - (width - 1) / 2.0, lags) / length)
    rank = width
    for fewer in range(4, width, 4):
        basis = vectors[:, :fewer]
        error = waves - basis @ (basis.T @ waves)
        if np.sqrt(np.mean(np.abs(error) ** 2)) < 1e-7:
            rank = fewer
            break
    basis = vectors[:, :rank]
    partner = basis.T @ waves
    centres = width * np.arange(bands) + (width - 1) / 2.0
    carrier = np.exp(2j * np.pi * np.outer(centres, lags) / length)
    whole = carrier[:, None, :] * partner[None, :, :]
    table = np.concatenate([whole.real, -whole.imag], axis=1).reshape(bands * 2 * rank, NLAG)
    return basis, as_bf16(np.ascontiguousarray(table.T))


def projection_constants(basis, halves):
    width, rank = basis.shape
    groups = width // halves // RADIX
    rows = np.zeros((halves, 2, rank, groups, 2, RADIX))
    split = basis.T.reshape(rank, halves, groups, RADIX).transpose(1, 0, 2, 3)
    rows[:, 0, :, :, 0, :] = split
    rows[:, 1, :, :, 1, :] = split
    return as_bf16(rows.reshape(halves, 2 * rank, 2 * groups * RADIX))


def real_dft(values):
    count = len(values)
    if count == 1:
        return [(values[0], None)]
    even, odd = real_dft(values[0::2]), real_dft(values[1::2])
    out = [None] * (count // 2 + 1)
    out[0] = (even[0][0] + odd[0][0], None)
    out[count // 2] = (even[0][0] - odd[0][0], None)
    for k in range(1, count // 4 + 1):
        er, ei = even[k]
        orr, oi = odd[k]
        if 4 * k == count:
            out[k] = (er, -orr)
            continue
        c, s = float(np.cos(2 * np.pi * k / count)), float(np.sin(2 * np.pi * k / count))
        tr = orr * c + oi * s
        ti = oi * c - orr * s
        out[k] = (er + tr, ei + ti)
        out[count // 2 - k] = (er - tr, ti - ei)
    return out


def transform_rows(x_ref, first, rows, twiddle_ref, z_ref):
    inner = x_ref.shape[1] // RADIX
    for at in range(0, rows, 16):
        for lane in range(0, inner, 128):
            values = [
                x_ref[first + at : first + at + 16, inner * j + lane : inner * j + lane + 128].astype(F32)
                for j in range(RADIX)
            ]
            bins = real_dft(values)
            for q in range(RADIX):
                yr, yi = bins[q] if q <= RADIX // 2 else bins[RADIX - q]
                if q > RADIX // 2:
                    yi = -yi
                if q == 0:
                    zr, zi = yr, jnp.zeros_like(yr)
                else:
                    c = twiddle_ref[q : q + 1, lane : lane + 128]
                    s = twiddle_ref[RADIX + q : RADIX + q + 1, lane : lane + 128]
                    if yi is None:
                        zr, zi = yr * c, -yr * s
                    else:
                        zr, zi = yr * c + yi * s, yi * c - yr * s
                where = slice(q * rows + at, q * rows + at + 16)
                for part, z in ((0, zr), (1, zi)):
                    high = z.astype(BF16)
                    z_ref[where, part * inner + lane : part * inner + lane + 128] = high
                    low = (z - high.astype(F32)).astype(BF16)
                    start = (2 + part) * inner + lane
                    z_ref[where, start : start + 128] = low


def transform_inner(z, table_ref):
    depth = z.shape[1] // 2
    high, low = table_ref[0:depth, :], table_ref[depth:, :]
    out = jnp.dot(z[:, :depth], high, preferred_element_type=F32)
    out = out + jnp.dot(z[:, depth:], high, preferred_element_type=F32)
    return out + jnp.dot(z[:, :depth], low, preferred_element_type=F32)


def short_filters(taps_ref, both_ref, q, even_ref, odd_ref, pair_ref, part_ref, r, even, odd, rows):
    evens = jnp.zeros((rows + 8, 128), F32)
    odds = jnp.zeros((rows, 128), F32)
    pairs = jnp.zeros((rows, 128), F32)
    for u in range(HALF + 1):
        evens = evens + taps_ref[q, 2 * u : 2 * u + 1, :] * even_ref[r, even + u : even + u + rows + 8, :]
    part_ref[r, 0 : rows + 8, :] = evens
    for u in range(HALF):
        odds = odds + taps_ref[q, 2 * u + 1 : 2 * u + 2, :] * odd_ref[r, odd + u : odd + u + rows, :]
    for u in range(HALF + 1):
        pairs = pairs + both_ref[q, u : u + 1, :] * pair_ref[r, odd + u : odd + u + rows, :]
    return evens[:rows] + odds, pairs - (part_ref[r, 1 : rows + 1, :] + odds)


def head_kernel(x_hbm, head_ref, sem_ref):
    copy = pltpu.make_async_copy(x_hbm.at[pl.ds(0, head_ref.shape[0])], head_ref, sem_ref.at[0])
    copy.start()
    copy.wait()


def own_kernel(
    x_hbm, taps_hbm, small_hbm, table_hbm, out_ref, first_ref, split_ref, both_ref, small_ref, table_ref,
    x_ref, taps_ref, z0_ref, z1_ref, turned_ref, even_ref, odd_ref, pair_ref, part_ref, sem_ref,
):
    chunk = z0_ref.shape[0] // RADIX
    steps = x_ref.shape[0] // chunk
    slots = (z0_ref, z1_ref)
    taps_copy = pltpu.make_async_copy(taps_hbm, taps_ref, sem_ref.at[steps + 1])
    small_copy = pltpu.make_async_copy(small_hbm, small_ref, sem_ref.at[steps + 2])
    taps_copy.start()
    small_copy.start()
    copies = []
    for i in range(steps):
        rows = pl.ds(i * chunk, chunk)
        copies.append(pltpu.make_async_copy(x_hbm.at[rows], x_ref.at[rows], sem_ref.at[i]))
    table_copy = pltpu.make_async_copy(table_hbm, table_ref, sem_ref.at[steps])
    for i, copy in enumerate(copies):
        copy.start()
        if i == 0:
            table_copy.start()

    taps_copy.wait()
    count = taps_ref.shape[0]
    pitch = RADIX + 1
    for at in range(0, taps_ref.shape[1], 128):
        turned = taps_ref[:, at : at + 128].T
        for n in range(128 // RADIX):
            row = (at // RADIX + n) * pitch
            turned_ref[row : row + RADIX, 0:count] = turned[RADIX * n : RADIX * (n + 1)]
    for q in range(RADIX):
        taps = turned_ref[pl.ds(q, 128, stride=pitch), 0:count].T
        split_ref[q, 0:count, :] = taps
        even = split_ref[q, pl.ds(0, HALF, stride=2), :]
        odd = split_ref[q, pl.ds(1, HALF, stride=2), :]
        both_ref[q, 0:HALF, :] = even + odd
        both_ref[q, HALF : HALF + 1, :] = taps[count - 1 :]

    small_copy.wait()
    copies[0].wait()
    transform_rows(x_ref, 0, chunk, small_ref, z0_ref)
    table_copy.wait()
    for i in range(steps):
        if i + 1 < steps:
            copies[1 + i].wait()
            transform_rows(x_ref, (i + 1) * chunk, chunk, small_ref, slots[(i + 1) % 2])
        values = transform_inner(slots[i % 2][...], table_ref)
        for q in range(RADIX):
            out_ref[q, 0, i * chunk : (i + 1) * chunk, :] = values[q * chunk : (q + 1) * chunk, :128]
            out_ref[q, 1, i * chunk : (i + 1) * chunk, :] = values[q * chunk : (q + 1) * chunk, 128:]

    half = x_ref.shape[0] // 2
    rows = half - HALF
    quarter = half // 2
    even_ref[:, half:, :] = jnp.zeros((2, 8, 128), F32)

    def filter_step(q, carry):
        for r in range(2):
            even_ref[r, 0:half, :] = out_ref[q, r, pl.ds(0, half, stride=2), :]
            odd_ref[r] = out_ref[q, r, pl.ds(1, half, stride=2), :]
            pair_ref[r] = odd_ref[r] + even_ref[r, 1 : half + 1, :]
            result = short_filters(split_ref, both_ref, q, even_ref, odd_ref, pair_ref, part_ref, r, 0, 0, rows)
            for parity in range(2):
                first_ref[q, r, quarter * parity : quarter * (parity + 1), :] = result[parity][:quarter]
                at = half + quarter * parity
                first_ref[q, r, at : at + rows - quarter, :] = result[parity][quarter:]
        return carry

    lax.fori_loop(0, RADIX, filter_step, 0)


def whiten_kernel(
    length, offset_ref, own_ref, first_ref, next_ref, small_ref, table_ref, taps_ref, both_ref, out_ref,
    z_ref, halo_ref, even_ref, odd_ref, pair_ref, part_ref, late_ref, power_ref, base_ref, rows_ref,
):
    width = own_ref.shape[2]
    device = lax.axis_index(AXES)
    devices = offset_ref.shape[1]
    inside = jnp.where(device == devices - 1, 0.0, 1.0)
    transform_rows(next_ref, 0, 2 * HALF, small_ref, z_ref)
    values = transform_inner(z_ref[...], table_ref)
    halo_ref[0] = values[:, :128]
    halo_ref[1] = values[:, 128:]

    power_ref[0] = jnp.zeros(power_ref.shape[1:], F32)

    half = width // 2
    edge = HALF // 2
    main = half - HALF
    zeros = jnp.zeros((edge, 128), F32)

    def joined(q, r):
        count = half // 2 - HALF
        parts = [first_ref[q, r, 0 : half + count, :], late_ref[q, r, 0:HALF, :]]
        parts += [first_ref[q, r, half + half // 2 : half + half // 2 + count, :], late_ref[q, r, HALF:, :]]
        return jnp.concatenate(parts, axis=0)

    def filter_step(q, n):
        at = pl.multiple_of(q * 2 * HALF, 2 * HALF)
        for r in range(2):
            b = 2 * n + r
            for parity, ref, pitch in ((0, even_ref, 4 * edge), (1, odd_ref, 3 * edge)):
                last = own_ref[q, r, pl.ds(2 * main + parity, 2 * edge, stride=2), :]
                after = halo_ref[r, pl.ds(at + parity, 2 * edge, stride=2), :]
                ref[b, 0 : 2 * edge, :] = last
                ref[b, 2 * edge : 3 * edge, :] = after[:edge] * inside
                ref[b, pitch : pitch + edge, :] = last[edge:] * inside
                ref[b, pitch + edge : pitch + 3 * edge, :] = after
            for line in range(2):
                even, odd = 4 * edge * line, 3 * edge * line
                even_ref[b, even + 3 * edge : even + 4 * edge, :] = zeros
                pair_ref[b, odd : odd + 3 * edge, :] = (
                    odd_ref[b, odd : odd + 3 * edge, :] + even_ref[b, even + 1 : even + 3 * edge + 1, :]
                )
            for line in range(2):
                result = short_filters(
                    taps_ref, both_ref, q, even_ref, odd_ref, pair_ref, part_ref, b, 4 * edge * line, 3 * edge * line, edge
                )
                for parity in range(2):
                    row = HALF * parity + edge * line
                    late_ref[q, r, row : row + edge, :] = result[parity]

    def filter_steps(i, carry):
        for n in range(together):
            filter_step(together * i + n, n)
        for n in range(together):
            q = together * i + n
            real, imaginary = joined(q, 0), joined(q, 1)
            power_ref[q + 1] = power_ref[q] + (real * real + imaginary * imaginary)
        return carry

    together = 4
    lax.fori_loop(0, RADIX // together, filter_steps, 0)

    reach = SMOOTH // RADIX
    lane = lax.broadcasted_iota(jnp.int32, (1, 128), 1)

    def shifted(values, by):
        inside = jnp.where((lane + by >= 0) & (lane + by < 128), 1.0, 0.0)
        return pltpu.roll(values, (-by) % 128, 1) * inside

    whole = power_ref[RADIX]
    base = whole
    for by in range(1, reach):
        base = base + (shifted(whole, by) + shifted(whole, -by))
    base_ref[...] = base

    bins = lax.broadcasted_iota(jnp.int32, (RADIX, 128), 1) * RADIX + lax.broadcasted_iota(
        jnp.int32, (RADIX, 128), 0
    )
    place = lax.broadcasted_iota(jnp.int32, offset_ref.shape, 1)
    turns = []
    for block in (device, lax.rem(device + 1, devices)):
        offset = jnp.sum(jnp.where(place == block, offset_ref[...], 0), axis=1, keepdims=True)
        phases = lax.rem(bins * offset, length).astype(F32) * (2.0 * np.pi / length)
        turns.append((jnp.cos(phases), jnp.sin(phases)))

    def by_row(part, q):
        mine, its = turns[0][part][q : q + 1, :], turns[1][part][q : q + 1, :]
        sizes = (half + half // 2 - edge, edge, half // 2 - edge, edge)
        return jnp.concatenate(
            [jnp.broadcast_to(its if n % 2 else mine, (size, 128)) for n, size in enumerate(sizes)], axis=0
        )

    pitch = 2 * RADIX + 1
    for q in range(RADIX):
        window = (
            base_ref[...]
            + shifted(power_ref[RADIX] - power_ref[q], -reach)
            + shifted(power_ref[q + 1], reach)
        )
        scale = lax.rsqrt(window * small_ref[2 * RADIX + q : 2 * RADIX + q + 1, 0:128] + EPSILON)
        fr, fi = joined(q, 0), joined(q, 1)
        c, s = by_row(0, q), by_row(1, q)
        wr = (fr * c + fi * s) * scale
        wi = (fi * c - fr * s) * scale
        rows_ref[pl.ds(q, 128, stride=pitch), :] = wr.T
        rows_ref[pl.ds(RADIX + q, 128, stride=pitch), :] = wi.T
    for m in range(128):
        rows = rows_ref[m * pitch : m * pitch + 2 * RADIX, :]
        out_ref[2 * RADIX * m : 2 * RADIX * (m + 1), :] = rows.astype(BF16)


def pair_kernel(slots, mine, pairs_hbm, band_ref, basis_ref, *refs):
    if mine:
        before_ref = None
    else:
        before_ref, refs = refs[0], refs[1:]
    out_ref, left_ref, right_ref, cross0_ref, cross1_ref, pairs_ref, sem_ref = refs
    copy = pltpu.make_async_copy(pairs_hbm, pairs_ref, sem_ref.at[0])
    copy.start()
    blocks = band_ref.shape[0]
    groups = band_ref.shape[1] // (2 * RADIX)
    deep = basis_ref.shape[1]
    half = lax.rem(lax.axis_index("shard"), 2)
    part = half if mine else 1 - half
    kept = slots // 2
    step = cross0_ref.shape[1] // (128 * kept)

    lane = lax.broadcasted_iota(jnp.int32, band_ref.shape[1:], 1)
    from_before = (lane >= 64) & (lax.rem(lane, 32) >= 32 - HALF // 2)

    def spread(i, carry):
        before = band_ref[lax.rem(8 * i + blocks - 1, blocks)].astype(F32)
        for n in range(8):
            values = band_ref[8 * i + n].astype(F32)
            whole = jnp.where(from_before, before, values)
            left_ref[8 * i + n] = whole
            right_ref[8 * i + n] = pltpu.roll(whole, 64, 1)
            before = values
        return carry

    lax.fori_loop(0, blocks // 8, spread, 0)
    copy.wait()

    def products(i, cross_ref):
        for n in range(step * kept):
            slot = (step * i + n // kept) * slots + half * kept + n % kept
            a, b = pairs_ref[0, slot], pairs_ref[1, slot]
            for m in range(groups):
                lo, mid, hi = 2 * RADIX * m, 2 * RADIX * m + RADIX, 2 * RADIX * (m + 1)
                lr, li = left_ref[a, lo:mid, :], left_ref[a, mid:hi, :]
                rr, ri = right_ref[b, lo:mid, :], right_ref[b, mid:hi, :]
                cross_ref[lo:mid, 128 * n : 128 * n + 128] = (lr * rr + li * ri).astype(BF16)
                cross_ref[mid:hi, 128 * n : 128 * n + 128] = (li * rr - lr * ri).astype(BF16)

    def project(i, cross_ref):
        result = jnp.dot(basis_ref[part], cross_ref[...], preferred_element_type=F32)
        for u in range(step):
            lanes = [128 * (kept * u + j) for j in range(kept)]
            stacked = jnp.concatenate([result[:, at : at + 128] for at in lanes], axis=0)
            if mine:
                out_ref[step * i + u] = stacked
            else:
                out_ref[step * i + u] = (stacked + before_ref[step * i + u]).astype(BF16)

    last = blocks // step - 1
    products(0, cross0_ref)

    def owners(i, carry):
        products(2 * i + 1, cross1_ref)
        project(2 * i, cross0_ref)
        products(jnp.minimum(2 * i + 2, last), cross0_ref)
        project(2 * i + 1, cross1_ref)
        return carry

    lax.fori_loop(0, blocks // (2 * step), owners, 0)


def lag_kernel(slots, scale, valid_ref, parts_ref, table_ref, out_ref, wide_ref, stage_ref, sem_ref):
    bands = parts_ref.shape[0] // 2
    kept = slots // 2
    deep = parts_ref.shape[1] // kept

    def gather(i, carry):
        for n in range(4):
            b = 4 * i + n
            at = pl.multiple_of(b * deep, 8)
            for half in range(2):
                values = parts_ref[2 * b + half].astype(F32)
                for j in range(kept):
                    lane = 128 * (half * kept + j)
                    wide_ref[pl.ds(at, deep), lane : lane + 128] = values[deep * j : deep * (j + 1)]
        return carry

    lax.fori_loop(0, bands // 4, gather, 0)
    copies = []
    for first in range(0, slots, 2):
        columns = wide_ref[:, 128 * first : 128 * first + 256].astype(BF16)
        for n in range(NLAG // 128):
            result = jnp.dot(table_ref[128 * n : 128 * n + 128, :], columns, preferred_element_type=F32)
            for j in range(2):
                weight = valid_ref[:, first + j : first + j + 1].astype(F32) * scale
                turned = result[:, 128 * j : 128 * j + 128].T * weight
                half = turned.shape[0] // 2
                at = (first + j) * (NLAG // 128) + n
                quarter = half // 2
                for parity in range(2):
                    pieces = (
                        (quarter * parity, HALF, quarter),
                        (half + quarter * parity, half + HALF, quarter - HALF // 2),
                        (half + quarter * (parity + 1) - HALF // 2, 0, HALF // 2),
                    )
                    for row, channel, count in pieces:
                        stage_ref[at, pl.ds(channel + parity, count, stride=2), :] = turned[row : row + count]
                lanes = pl.ds(128 * n, 128)
                copy = pltpu.make_async_copy(stage_ref.at[at], out_ref.at[first + j, :, lanes], sem_ref.at[at])
                copy.start()
                copies.append(copy)
    for copy in copies:
        copy.wait()


def vmem():
    return pl.BlockSpec(memory_space=pltpu.VMEM)


def params():
    return pltpu.CompilerParams(vmem_limit_bytes=VMEM_BYTES)


def near(array):
    return pltpu.with_memory_space_constraint(array, pltpu.VMEM)


def distant(array):
    return pltpu.with_memory_space_constraint(array, pltpu.HBM)


def far():
    return pl.BlockSpec(memory_space=pltpu.HBM)


def body(samples, fan_taps, pair_blocks, pair_valid, coil_offsets):
    width = samples.shape[0]
    length = samples.shape[2]
    bin_count = length // 2
    devices = lax.axis_size("group") * lax.axis_size("shard")
    shards = lax.axis_size("shard")
    bins_device = bin_count // devices
    slots = pair_valid.shape[0]
    inner = length // RADIX
    lanes = bin_count // RADIX
    chunk = 64

    twiddle, table = forward_constants(length)
    basis, lag_table = band_constants(devices // 2, 2 * bins_device, length)
    project = projection_constants(basis, 2)
    deep = project.shape[1]
    bins_k = np.arange(bin_count)
    counts = np.minimum(bins_k + SMOOTH, bin_count - 1) - np.maximum(bins_k - SMOOTH, 0) + 1
    small = np.zeros((3 * RADIX, inner), np.float32)
    small[: 2 * RADIX] = twiddle
    small[2 * RADIX :, :lanes] = (1.0 / counts).reshape(lanes, RADIX).T

    x = samples.reshape(width, length)
    x, fan_taps, small = distant(x), distant(fan_taps), distant(jnp.asarray(small))
    head = pl.pallas_call(
        head_kernel,
        out_shape=pltpu.VMEM((2 * HALF, length), BF16),
        in_specs=[far()],
        out_specs=vmem(),
        scratch_shapes=[pltpu.SemaphoreType.DMA((1,))],
        compiler_params=params(),
        name="head",
    )(x)
    after = lax.ppermute(head, AXES, [((i + 1) % devices, i) for i in range(devices)])

    own, ready, taps, both, small, table = pl.pallas_call(
        own_kernel,
        out_shape=(
            pltpu.VMEM((RADIX, 2, width, lanes), F32),
            pltpu.VMEM((RADIX, 2, width, lanes), F32),
            pltpu.VMEM((RADIX, 2 * HALF + 1, lanes), F32),
            pltpu.VMEM((RADIX, HALF + 1, lanes), F32),
            pltpu.VMEM(small.shape, F32),
            pltpu.VMEM(table.shape, BF16),
        ),
        in_specs=[far()] * 4,
        out_specs=(vmem(),) * 6,
        scratch_shapes=[
            pltpu.VMEM((width, length), BF16),
            pltpu.VMEM(fan_taps.shape, F32),
            pltpu.VMEM((RADIX * chunk, 4 * inner), BF16),
            pltpu.VMEM((RADIX * chunk, 4 * inner), BF16),
            pltpu.VMEM((bin_count + lanes, 128), F32),
            pltpu.VMEM((2, width // 2 + 8, lanes), F32),
            pltpu.VMEM((2, width // 2, lanes), F32),
            pltpu.VMEM((2, width // 2, lanes), F32),
            pltpu.VMEM((2, width // 2, lanes), F32),
            pltpu.SemaphoreType.DMA((width // chunk + 3,)),
        ],
        compiler_params=params(),
        name="own_spectra",
    )(x, fan_taps, small, distant(jnp.asarray(table)))

    rows = pl.pallas_call(
        functools.partial(whiten_kernel, length),
        out_shape=pltpu.VMEM((2 * bin_count, width), BF16),
        in_specs=[vmem()] * 8,
        out_specs=vmem(),
        scratch_shapes=[
            pltpu.VMEM((RADIX * 2 * HALF, 4 * inner), BF16),
            pltpu.VMEM((2, RADIX * 2 * HALF, lanes), F32),
            pltpu.VMEM((8, 4 * HALF, lanes), F32),
            pltpu.VMEM((8, 3 * HALF, lanes), F32),
            pltpu.VMEM((8, 3 * HALF, lanes), F32),
            pltpu.VMEM((8, HALF, lanes), F32),
            pltpu.VMEM((RADIX, 2, 2 * HALF, lanes), F32),
            pltpu.VMEM((RADIX + 1, width, lanes), F32),
            pltpu.VMEM((width, lanes), F32),
            pltpu.VMEM((2 * bin_count + lanes, width), F32),
        ],
        compiler_params=params(),
        name="whiten",
    )(near(coil_offsets.reshape(1, -1)), near(own), near(ready), near(after), near(small), near(table), near(taps), near(both))

    band = lax.all_to_all(
        rows.reshape(devices, 2 * bins_device, width), AXES, split_axis=0, concat_axis=0, tiled=True
    )
    other = lax.ppermute(band, "shard", [(i, i ^ 1) for i in range(shards)])

    pairs = distant(pair_blocks.T)
    project = near(jnp.asarray(project))
    sums = (devices, slots // 2 * deep, width)

    def products(mine, part, before):
        return pl.pallas_call(
            functools.partial(pair_kernel, slots, mine),
            out_shape=pltpu.VMEM(sums, F32 if mine else BF16),
            in_specs=[far()] + [vmem()] * (2 + len(before)),
            out_specs=vmem(),
            scratch_shapes=[
                pltpu.VMEM((devices, 2 * bins_device, width), F32),
                pltpu.VMEM((devices, 2 * bins_device, width), F32),
                pltpu.VMEM((2 * bins_device, 4 * slots * width), BF16),
                pltpu.VMEM((2 * bins_device, 4 * slots * width), BF16),
                pltpu.SMEM(pairs.shape, jnp.int32),
                pltpu.SemaphoreType.DMA((1,)),
            ],
            compiler_params=params(),
            name="pairs_own_part" if mine else "pairs_other_part",
        )(pairs, near(part), project, *before)

    first = products(True, band, ())
    parts = products(False, other, (near(first),))

    owned = lax.all_to_all(parts, AXES, split_axis=0, concat_axis=0, tiled=True)

    return pl.pallas_call(
        functools.partial(lag_kernel, slots, float(1.0 / np.sqrt(bin_count * samples.shape[1]))),
        out_shape=jax.ShapeDtypeStruct((slots, width, NLAG), F32),
        in_specs=[vmem()] * 3,
        out_specs=pl.BlockSpec(memory_space=pl.ANY),
        scratch_shapes=[
            pltpu.VMEM((devices // 2 * deep, slots * width), F32),
            pltpu.VMEM((slots * NLAG // 128, width, 128), F32),
            pltpu.SemaphoreType.DMA((slots * NLAG // 128,)),
        ],
        compiler_params=params(),
        name="lags",
    )(near(pair_valid.reshape(1, -1)), near(owned), near(jnp.asarray(lag_table)))


def solution(mesh):
    return jax.shard_map(
        body,
        mesh=mesh,
        in_specs=(P(AXES, None, None), P(), P(), P(AXES), P()),
        out_specs=P(AXES, None, None),
        check_vma=False,
    )
```
